128 devices in a mesh: section: 2 (over x_lo), tensor: 16 (over x_hi, z, core), dp: 4 (over y).
Axes of the slice: x: 4 (x_hi: 2, x_lo: 2; x = x_hi * 2 + x_lo), y: 4, z: 4, core: 2. Of those that a mesh axis runs over, the one named last changes fastest.
Arguments:
- images: bfloat16 [8, 1024, 1024], P('dp', 'tensor'), may hold values from -6 to 6
- out_grad: bfloat16 [8, 1024, 1024], P('dp', 'tensor'), may hold values from -6 to 6
- live_images: int32 [8], replicated, may hold values from 0 to 1, as said below
- attn_in: bfloat16 [2, 1024, 3, 1024], P('section', None, None, 'tensor'), may hold values from -0.1875 to 0.1875
- qv_bias: float32 [2, 2, 1024], P('section', None, 'tensor'), may hold values from -1.5 to 1.5
- attn_out: bfloat16 [2, 1024, 1024], P('section', 'tensor'), may hold values from -0.75 to 0.75
- mlp_in: bfloat16 [2, 1024, 4096], P('section', None, 'tensor'), may hold values from -0.1875 to 0.1875
- mlp_bias: float32 [2, 4096], P('section', 'tensor'), may hold values from -2.5 to 2.5
- mlp_out: bfloat16 [2, 4096, 1024], P('section', 'tensor'), may hold values from -0.125 to 0.125
- vectors: float32 [2, 8, 1024], P('section'), may hold values from -1.2 to 2
Outputs:
- section_out: bfloat16 [2, 8, 1024, 1024], P('section', 'dp', 'tensor')
- section_in_grad: bfloat16 [2, 8, 1024, 1024], P('section', 'dp', 'tensor')
- attn_in_grad: float32 [2, 1024, 3, 1024], P('section', None, None, 'tensor')
- qv_bias_grad: float32 [2, 2, 1024], P('section', None, 'tensor')
- attn_out_grad: float32 [2, 1024, 1024], P('section', 'tensor')
- mlp_in_grad: float32 [2, 1024, 4096], P('section', None, 'tensor')
- mlp_bias_grad: float32 [2, 4096], P('section', 'tensor')
- mlp_out_grad: float32 [2, 4096, 1024], P('section', 'tensor')
- vectors_grad: float32 [2, 8, 1024], P('section')
The draws below stay inside these ranges and needn't reach their ends.
Inputs may be any that keep to these rules, and one draw needn't show every extreme that they name: `live_images`: the images of a data group in a micro-batch occupy that micro-batch's first slots of the group; in every micro-batch one data group holds 1 image and another none.
All inputs are finite; a program needn't handle non-finite values.
Results may differ from the reference program's by a relative error of at most 0.018.
Values may be sent and summed in bfloat16 or wider, within the bound.
A program may use at most 128 MiB of HBM per device.

```python
import math
import jax
import jax.numpy as jnp
from jax import lax

D = 1024
H = 16
HD = 64
FF = 4096
TOK_IMG = 1024
MICRO = 2
IMG_MB = 1
HHD = 1024
IMAGES = 8
N_DP = 4


def draw_live_images(key, part):
    key = jax.random.fold_in(key, 7)
    base_key, order_key = jax.random.split(key)
    base = jax.random.randint(base_key, (N_DP, MICRO), 0, IMG_MB + 1)
    orders = jax.vmap(lambda one_key: jax.random.permutation(one_key, N_DP))(jax.random.split(order_key, MICRO))
    groups = jnp.arange(N_DP, dtype=jnp.int32)[:, None]
    filled = groups == orders[:, 0][None, :]
    emptied = groups == orders[:, 1][None, :]
    counts = jnp.where(filled, IMG_MB, jnp.where(emptied, 0, base))
    return counts.reshape(N_DP * MICRO).astype(jnp.int32)


def draw_vectors(key, part):
    key = jax.random.fold_in(key, 11)
    gain_key, shift_key, scale_key = jax.random.split(key, 3)
    gains = jax.random.uniform(gain_key, (2, 8, D), jnp.float32, 0.5, 1.5)
    shifts = jnp.clip(0.3 * jax.random.normal(shift_key, (2, 8, D), jnp.float32), -1.2, 1.2)
    scales = jnp.exp(jax.random.uniform(scale_key, (2, 8, D), jnp.float32, math.log(0.5), math.log(2.0)))
    row_ids = jnp.arange(8)[None, :, None]
    is_gain = (row_ids == 0) | (row_ids == 4)
    is_scale = (row_ids == 3) | (row_ids == 7)
    return jnp.where(is_gain, gains, jnp.where(is_scale, scales, shifts)).astype(jnp.float32)


def block_levels(own_key, dims, pieces, smallest, top_value):
    factor_of, own = 1.0, jax.random.fold_in(own_key, 6)
    for dim, shards_of in pieces:
        steps = jnp.exp(jax.random.uniform(jax.random.fold_in(own, dim), (shards_of,), jnp.float32, smallest / len(pieces), top_value / len(pieces)))
        factor_of = factor_of * jnp.repeat(steps, dims[dim] // shards_of).reshape([-1 if axis == dim else 1 for axis in range(len(dims))])
    return factor_of


def bell_draw(key, dims, width, limit, shards=(), kind=jnp.bfloat16):
    result = jax.random.normal(key, dims, jnp.float32) * width
    if len(shards) > 0:
        result = block_levels(key, dims, shards, -0.22, 0.18) * result
    return jnp.clip(result, min=-limit, max=limit).astype(kind)


def setup_inputs(seed: int = 0) -> dict:
    key_list = jax.random.split(jax.random.key(seed), 11)
    images = bell_draw(key_list[0], (IMAGES, TOK_IMG, D), 1.0, 6.0, ((0, 4), (1, 16)))
    out_grad = bell_draw(key_list[1], (IMAGES, TOK_IMG, D), 1.0, 6.0, ((0, 4), (1, 16)))
    live_images = draw_live_images(jax.random.fold_in(key_list[10], 71), 0)
    attn_in = bell_draw(key_list[3], (2, D, 3, HHD), D ** -0.5, 0.1875, ((0, 2), (3, 16)))
    qv_bias = bell_draw(key_list[4], (2, 2, HHD), 0.3, 1.5, ((0, 2), (2, 16)), jnp.float32)
    attn_out = bell_draw(key_list[5], (2, HHD, D), (HHD // 16) ** -0.5, 0.75, ((0, 2), (1, 16)))
    mlp_in = bell_draw(key_list[6], (2, D, FF), D ** -0.5, 0.1875, ((0, 2), (2, 16)))
    mlp_bias = bell_draw(key_list[7], (2, FF), 0.5, 2.5, ((0, 2), (1, 16)), jnp.float32)
    mlp_out = bell_draw(key_list[8], (2, FF, D), (FF // 2) ** -0.5, 0.125, ((0, 2), (1, 16)))
    vectors = draw_vectors(jax.random.fold_in(key_list[10], 71), 0)
    return dict(images=images, out_grad=out_grad, live_images=live_images, attn_in=attn_in, qv_bias=qv_bias, attn_out=attn_out, mlp_in=mlp_in, mlp_bias=mlp_bias, mlp_out=mlp_out, vectors=vectors)


EPSILON = 1e-06
PRECISE = lax.Precision.HIGHEST

@jax.custom_vjp
def low(v):
    return lax.optimization_barrier(v.astype(jnp.bfloat16)).astype(jnp.float32)

@jax.custom_vjp
def low_back(v):
    return v

def low_keep(v):
    return (low(v), None)

def low_pass(kept, grad):
    return (grad,)

def back_keep(v):
    return (v, None)

def back_low(kept, grad):
    return (low(grad),)
low.defvjp(low_keep, low_pass)
low_back.defvjp(back_keep, back_low)

def round_both(value):
    return low_back(low(value))

def normalize(tokens, gain_vec, offset):
    center = tokens - lax.optimization_barrier(jnp.mean(tokens, axis=-1, keepdims=True))
    return center * lax.rsqrt(lax.optimization_barrier(jnp.mean(center * center, axis=-1, keepdims=True)) + EPSILON) * gain_vec + offset

def attention(queries, keys_in, values):
    block_rows = min(512, TOK_IMG)
    query_parts = queries.reshape(TOK_IMG // block_rows, block_rows, H, HD)
    key_heads = keys_in.reshape(TOK_IMG, H, HD)
    value_heads = values.reshape(TOK_IMG, H, HD)

    def score_block(q_block):
        scores = low_back(jnp.einsum('qhe,khe->hqk', q_block, key_heads, precision=PRECISE) * HD ** (-0.5))
        shares = jax.nn.softmax(scores, axis=-1)
        attended = jnp.einsum('hqk,khe->qhe', low(shares), value_heads, precision=PRECISE)
        return attended.reshape(block_rows, H * HD)
    return lax.map(jax.checkpoint(score_block), query_parts).reshape(TOK_IMG, H * HD)

def layer_fwd(tokens, params, section_num):
    w_in, qv_bias, w_out, w_up, b_up, w_down, vectors = [param[section_num] for param in params]
    normed = low(normalize(tokens, vectors[0], vectors[1]))
    mixture = jnp.einsum('td,dcf->tcf', normed, w_in, precision=PRECISE)
    queries = round_both(mixture[:, 0] + qv_bias[0])
    keys_in = round_both(mixture[:, 1])
    values = round_both(mixture[:, 2] + qv_bias[1])
    attended = round_both(attention(queries, keys_in, values))
    branch = low_back(jnp.dot(attended, w_out, precision=PRECISE) + vectors[2])
    hidden = tokens + vectors[3] * branch
    normed_two = low(normalize(hidden, vectors[4], vectors[5]))
    pre_act = low_back(jnp.dot(normed_two, w_up, precision=PRECISE) + b_up)
    activated = low(jax.nn.gelu(pre_act, approximate=False))
    branch_two = low_back(jnp.dot(activated, w_down, precision=PRECISE) + vectors[6])
    return hidden + vectors[7] * branch_two

def reference(images, out_grad, live_images, attn_in, qv_bias, attn_out, mlp_in, mlp_bias, mlp_out, vectors):
    params = (attn_in.astype(jnp.float32), qv_bias, attn_out.astype(jnp.float32), mlp_in.astype(jnp.float32), mlp_bias, mlp_out.astype(jnp.float32), vectors)
    counts = live_images.reshape(N_DP, MICRO)
    totals = lax.optimization_barrier(jnp.sum(counts, axis=0)).astype(jnp.float32)
    within = jnp.arange(IMG_MB, dtype=jnp.int32)
    slot_weight = jnp.where(within[None, None, :] < counts[:, :, None], 1.0 / totals[None, :, None], jnp.float32(0.0)).reshape(IMAGES).astype(jnp.float32)

    def forward(start_rows, params, offset_rows):

        def per_image(image_pair):
            image_rows, added = image_pair
            first_out = layer_fwd(image_rows, params, 0)
            second = layer_fwd(round_both(first_out) + added, params, 1)
            return (first_out, second)
        return lax.map(jax.checkpoint(per_image), (start_rows, offset_rows))
    start_rows = images.astype(jnp.float32)
    zero_rows = jnp.zeros_like(start_rows)
    (first_out, second), pullback = jax.vjp(forward, start_rows, params, zero_rows)
    cotangent = out_grad.astype(jnp.float32) * slot_weight[:, None, None]
    grad_start, grad_params, grad_middle = pullback((jnp.zeros_like(first_out), cotangent))
    section_out = jnp.stack([first_out, second]).astype(jnp.bfloat16)
    section_in_grad = jnp.stack([grad_start, grad_middle]).astype(jnp.bfloat16)
    return (section_out, section_in_grad, grad_params[0], grad_params[1], grad_params[2], grad_params[3], grad_params[4], grad_params[5], grad_params[6])
```

```python
import jax
import jax.numpy as jnp
from jax import lax
from jax.experimental import pallas as pl
from jax.experimental.pallas import tpu as pltpu
from jax.sharding import PartitionSpec as P

MESH = pl.DeviceIdType.MESH
F32 = jnp.float32
BF16 = jnp.bfloat16
EPSILON = 1e-06
D = 1024
MICRO = 2
LANE = 8
ROWS = 64
PAIRS = LANE // 2
DP = 4
BIAS_ROW = 8
GATHERS = 4
SMALL, QKV, OUT, UP, DOWN = range(5)


def dot_nn(a, b):
    return lax.dot_general(a, b, (((1,), (0,)), ((), ())), preferred_element_type=F32)


def dot_nt(a, b):
    return lax.dot_general(a, b, (((1,), (1,)), ((), ())), preferred_element_type=F32)


def dot_tn(a, b):
    return lax.dot_general(a, b, (((0,), (0,)), ((), ())), preferred_element_type=F32)


def normalize(rows):
    center = rows - jnp.mean(rows, axis=-1, keepdims=True)
    inv = lax.rsqrt(jnp.mean(center * center, axis=-1, keepdims=True) + EPSILON)
    return center * inv, inv


def normalize_back(grad, unit, inv, gain):
    scaled = grad * gain
    return inv * (
        scaled
        - jnp.mean(scaled, axis=-1, keepdims=True)
        - unit * jnp.mean(scaled * unit, axis=-1, keepdims=True)
    )


def sum_rows(rows):
    return jnp.sum(rows, axis=0, keepdims=True)


def kernel(
    x_in, cot_in, small_in, qkv_in, out_in, up_in, down_in,
    so_ref, ig_ref, gw_ref, sm_ref,
    small_w, qkv_w, out_w, up_w, down_w,
    gathered, parts, landed,
    xs, units, invs, branches, hidden, cot,
    queries, kv, attended, probs, act, slope, d_pre, d_mix, d_kv, d_kv_in, d_att,
    grad_m, grad_a, core_m, core_a, mine_m, mine_a, recv_m, recv_a, full_m, full_a,
    vec, lane_vec, core_vec, group_vec, outs, outs_in,
    w_local, w_send, w_recv, ag_send, ag_recv, rs_send, rs_recv,
    kv_send, kv_recv, core_send, core_recv, pair_send, pair_recv, dp_send, dp_recv,
    out_send, out_recv, lane_send, lane_recv, cv_send, cv_recv, gv_send, gv_recv,
):
    section = lax.axis_index("section")
    group = lax.axis_index("dp")
    tensor = lax.axis_index("tensor")
    core = lax.rem(tensor, 2)
    lane = tensor // 2
    own_pair = lane // 2
    other = 1 - core
    member = section * DP + group

    def chip(index):
        return {"tensor": index * 2 + core}

    to_core = {"tensor": lane * 2 + other}
    to_section = {"section": 1 - section}

    def ahead(step):
        return lax.rem(lane + step, LANE)

    def remote(src, dst, send_sem, recv_sem, device):
        return pltpu.make_async_remote_copy(
            src_ref=src, dst_ref=dst, send_sem=send_sem, recv_sem=recv_sem,
            device_id=device, device_id_type=MESH,
        )

    barrier = pltpu.get_barrier_semaphore()
    for step in range(1, LANE):
        pl.semaphore_signal(barrier, inc=1, device_id=chip(ahead(step)), device_id_type=MESH)
    pl.semaphore_signal(barrier, inc=1, device_id=to_core, device_id_type=MESH)
    for step in range(1, 2 * DP):
        friend = lax.rem(member + step, 2 * DP)
        pl.semaphore_signal(
            barrier, inc=1, device_id={"section": friend // DP, "dp": lax.rem(friend, DP)},
            device_id_type=MESH,
        )
    pl.semaphore_wait(barrier, LANE - 1 + 1 + 2 * DP - 1)

    def piece(kind, layer, whose):
        return (
            small_w.at[layer, whose], qkv_w.at[layer, :, whose], out_w.at[layer, whose],
            up_w.at[layer, whose], down_w.at[layer, whose],
        )[kind]

    sources = (small_in, qkv_in, out_in, up_in, down_in)

    def local_piece(kind):
        return pltpu.make_async_copy(sources[kind], piece(kind, section, core), w_local.at[kind])

    def core_piece(kind):
        return remote(sources[kind], piece(kind, section, core),
                      w_send.at[0, kind], w_recv.at[0, kind], to_core)

    def section_piece(kind):
        return remote(sources[kind], piece(kind, section, core),
                      w_send.at[1, kind], w_recv.at[1, kind], to_section)

    def relay_piece(kind):
        return remote(piece(kind, 1 - section, core), piece(kind, 1 - section, core),
                      w_send.at[2, kind], w_recv.at[2, kind], to_core)

    def arrived_piece(kind, way, layer, whose):
        there = piece(kind, layer, whose)
        return remote(there, there, w_send.at[way, kind], w_recv.at[way, kind], to_core)

    for kind in range(5):
        local_piece(kind).start()
    for kind in range(5):
        section_piece(kind).start()
        core_piece(kind).start()

    def take_pieces(kinds):
        for kind in kinds:
            arrived_piece(kind, 1, 1 - section, core).wait_recv()
            relay_piece(kind).start()
        for kind in kinds:
            local_piece(kind).wait()
            arrived_piece(kind, 0, section, other).wait_recv()
            arrived_piece(kind, 2, 1 - section, other).wait_recv()

    def gather_copy(layer, which, slot, dest):
        block = gathered.at[layer, which, lane]
        return remote(block, block, ag_send.at[slot], ag_recv.at[which, lane], chip(dest))

    def gather_dests():
        found = [own_pair * 2 + 1 - lax.rem(lane, 2)]
        for step in range(1, PAIRS):
            pair = lax.rem(own_pair + PAIRS - step, PAIRS)
            found += [pair * 2, pair * 2 + 1]
        return found

    def gather_start(layer, which, rows):
        gathered[layer, which, lane] = rows
        for slot, dest in enumerate(gather_dests()):
            gather_copy(layer, which, slot, dest).start()

    def gather_finish(layer, which):
        for slot, dest in enumerate(gather_dests()):
            gather_copy(layer, which, slot, dest).wait_send()

    def gather_take(layer, which, pair):
        for side in range(2):
            source = pair * 2 + side

            @pl.when(source != lane)
            def _():
                block = gathered.at[layer, which, source]
                remote(block, block, ag_send.at[0], ag_recv.at[which, source],
                       to_core).wait_recv()

        return gathered[layer, which, pl.ds(pair * 2, 2)].reshape(2 * ROWS, D)

    def whole(layer, which):
        return gathered[layer, which].reshape(LANE * ROWS, D)

    def part_copy(which, dest):
        return remote(parts.at[which % 2, dest], landed.at[which % 2, lane],
                      rs_send.at[dest], rs_recv.at[which, lane], chip(dest))

    def part_start(which, pair, rows):
        parts[which % 2, pl.ds(pair * 2, 2)] = rows.astype(BF16).reshape(2, ROWS, D)
        for side in range(2):
            dest = pair * 2 + side

            @pl.when(dest != lane)
            def _():
                part_copy(which, dest).start()

    def part_sum(which):
        total = parts[which % 2, lane].astype(F32)
        for step in range(1, LANE):
            source = ahead(step)
            block = landed.at[which % 2, source]
            remote(block, block, rs_send.at[source], rs_recv.at[which, source],
                   to_core).wait_recv()
            total = total + landed[which % 2, source].astype(F32)
        for step in range(1, LANE):
            part_copy(which, ahead(step)).wait_send()
        return total

    def each_pair(work, first=0):
        @pl.loop(0, PAIRS)
        def _(step):
            work(lax.rem(own_pair + first + step, PAIRS))

    def pair_rows(pair):
        return pl.ds(pl.multiple_of(pair * 2 * ROWS, 2 * ROWS), 2 * ROWS)

    first_head = lax.broadcasted_iota(jnp.int32, (2 * ROWS, 128), 1) < 64

    def vector(layer, row):
        return small_w[layer, core, row:row + 1]

    def both_biases(layer, first, length):
        row = slice(BIAS_ROW, BIAS_ROW + 1)
        return jnp.concatenate(
            [small_w[layer, 0, row, first:first + length],
             small_w[layer, 1, row, first:first + length]], axis=-1)

    def keep_inv(layer, which, inv):
        invs[layer, which] = jnp.broadcast_to(inv, (ROWS, 128))

    def get_inv(layer, which):
        return invs[layer, which, :, 0:1]

    xs[0] = x_in[...].astype(F32)
    vec[...] = jnp.zeros_like(vec)
    take_pieces((SMALL,))

    @pl.loop(0, 2)
    def _(layer):
        unit, inv = normalize(xs[layer])
        units[layer, 0] = unit
        keep_inv(layer, 0, inv)
        gather_start(layer, 0, (unit * vector(layer, 0) + vector(layer, 1)).astype(BF16))

        @pl.when(layer == 0)
        def _():
            take_pieces((QKV,))

        q_bias = both_biases(layer, 0, 64)
        v_bias = both_biases(layer, 128, 64)

        def project(pair):
            rows = gather_take(layer, 0, pair)
            mixed = dot_nt(rows, qkv_w[layer].reshape(384, D))
            queries[layer, pair_rows(pair)] = (
                (mixed[:, 0:128] + q_bias).astype(BF16).astype(F32) * 0.125).astype(BF16)
            kv[layer, core, pair_rows(pair), 0:128] = mixed[:, 128:256].astype(BF16)
            kv[layer, core, pair_rows(pair), 128:256] = (mixed[:, 256:384] + v_bias).astype(BF16)

        each_pair(project)
        kv_copy = remote(kv.at[layer, core], kv.at[layer, core],
                         kv_send.at[0, layer], kv_recv.at[0, layer], to_core)
        kv_copy.start()

        @pl.when(layer == 0)
        def _():
            take_pieces((OUT,))

        there = kv.at[layer, other]
        remote(there, there, kv_send.at[0, layer], kv_recv.at[0, layer], to_core).wait_recv()

        def attend(pair):
            rows = queries[layer, pair_rows(pair)]
            keys = kv[layer, :, :, 0:128].reshape(2 * LANE * ROWS, 128)
            values = kv[layer, :, :, 128:256].reshape(2 * LANE * ROWS, 128)
            found = []
            for head in range(2):
                mask = first_head if head == 0 else jnp.logical_not(first_head)
                scores = dot_nt(jnp.where(mask, rows, jnp.zeros_like(rows)), keys)
                grown = jnp.exp(scores - jnp.max(scores, axis=-1, keepdims=True))
                share = (grown / jnp.sum(grown, axis=-1, keepdims=True)).astype(BF16)
                probs[layer, head, pair_rows(pair)] = share
                found.append(dot_nn(share, values))
            result = jnp.where(first_head, found[0], found[1]).astype(BF16)
            attended[layer, pair_rows(pair)] = result
            part_start(0, pair, dot_nn(result, out_w[layer].reshape(128, D)))

        each_pair(attend, 1)
        kv_copy.wait_send()
        gather_finish(layer, 0)
        branch = part_sum(0) + vector(layer, 2)
        branches[layer, 0] = branch
        state = xs[layer] + vector(layer, 3) * branch
        hidden[...] = state

        unit, inv = normalize(state)
        units[layer, 1] = unit
        keep_inv(layer, 1, inv)
        gather_start(layer, 1, (unit * vector(layer, 4) + vector(layer, 5)).astype(BF16))

        @pl.when(layer == 0)
        def _():
            take_pieces((UP, DOWN))

        up_bias = both_biases(layer, 256, 256)

        def feed(pair):
            rows = gather_take(layer, 1, pair)
            pre = dot_nt(rows, up_w[layer].reshape(512, D)) + up_bias
            cdf = 0.5 + 0.5 * lax.erf(pre * 0.7071067811865476)
            bell = jnp.exp(-0.5 * pre * pre) * 0.3989422804014327
            value = (pre * cdf).astype(BF16)
            act[layer, pair_rows(pair)] = value
            slope[layer, pair_rows(pair)] = cdf + pre * bell
            part_start(1, pair, dot_nn(value, down_w[layer].reshape(512, D)))

        each_pair(feed)
        gather_finish(layer, 1)
        branch = part_sum(1) + vector(layer, 6)
        branches[layer, 1] = branch
        rounded = (hidden[...] + vector(layer, 7) * branch).astype(BF16)
        outs[0, layer] = rounded

        @pl.when(layer == 0)
        def _():
            xs[1] = rounded.astype(F32)

    def out_copy(which):
        return remote(outs.at[which, 1 - section], outs_in.at[which],
                      out_send.at[which], out_recv.at[which], to_section)

    out_copy(0).start()

    def core_copy(kind, layer):
        source, dest = ((grad_m, core_m), (grad_a, core_a))[kind]
        return remote(source.at[layer, other], dest.at[layer],
                      core_send.at[kind, layer], core_recv.at[kind, layer], to_core)

    def owner_copy(kind, layer, quarter):
        source, dest, length = ((mine_m, recv_m, 128), (mine_a, recv_a, 64))[kind]
        return remote(source.at[layer, pl.ds(quarter * length, length)], dest.at[member],
                      pair_send.at[kind, layer, quarter], pair_recv.at[kind, member],
                      {"section": layer, "dp": quarter})

    def owned(layer, quarter):
        return jnp.logical_and(layer == section, quarter == group)

    def core_sum_and_send(kind, layer):
        there, mine, own = ((core_m, mine_m, grad_m), (core_a, mine_a, grad_a))[kind]
        core_copy(kind, layer).wait_recv()
        mine[layer] = (own[layer, core].astype(F32) + there[layer].astype(F32)).astype(BF16)
        for quarter in range(DP):
            @pl.when(jnp.logical_not(owned(layer, quarter)))
            def _():
                owner_copy(kind, layer, quarter).start()

    cot[...] = cot_in[...]

    @pl.loop(0, 2)
    def _(turn):
        layer = 1 - turn
        above = cot[...]
        d_branch2 = (above * vector(layer, 7)).astype(BF16)
        gather_start(layer, 2, d_branch2)
        vec[layer, 7:8] = sum_rows(above * branches[layer, 1])
        vec[layer, 6:7] = sum_rows(d_branch2.astype(F32))

        def feed_back(pair):
            rows = gather_take(layer, 2, pair)
            d_act = dot_nt(rows, down_w[layer].reshape(512, D))
            back = (d_act * slope[layer, pair_rows(pair)]).astype(BF16)
            d_pre[pair_rows(pair)] = back
            vec[layer, 8:9, 0:512] += sum_rows(back.astype(F32))
            part_start(2, pair, dot_nn(back, up_w[layer].reshape(512, D)))

        each_pair(feed_back)
        gather_finish(layer, 2)
        for whose in range(2):
            units_of = slice(whose * 256, whose * 256 + 256)
            grad_m[layer, whose, 0:256] = dot_tn(d_pre[:, units_of], whole(layer, 1)).astype(BF16)
            grad_m[layer, whose, 256:512] = dot_tn(
                act[layer, :, units_of], whole(layer, 2)).astype(BF16)
        core_copy(0, layer).start()
        d_normed = part_sum(2)
        unit, inv = units[layer, 1], get_inv(layer, 1)
        vec[layer, 4:5] = sum_rows(d_normed * unit)
        vec[layer, 5:6] = sum_rows(d_normed)
        d_hidden = above + normalize_back(d_normed, unit, inv, vector(layer, 4))
        hidden[...] = d_hidden
        d_branch = (d_hidden * vector(layer, 3)).astype(BF16)
        gather_start(layer, 3, d_branch)
        vec[layer, 3:4] = sum_rows(d_hidden * branches[layer, 0])
        vec[layer, 2:3] = sum_rows(d_branch.astype(F32))
        core_sum_and_send(0, layer)
        d_kv[...] = jnp.zeros_like(d_kv)

        def attend_back(pair):
            rows = gather_take(layer, 3, pair)
            d_out = dot_nt(rows, out_w[layer].reshape(128, D)).astype(BF16)
            keys = kv[layer, :, :, 0:128].reshape(2 * LANE * ROWS, 128)
            values = kv[layer, :, :, 128:256].reshape(2 * LANE * ROWS, 128)
            q_rows = queries[layer, pair_rows(pair)]
            found, score_grads, shares, q_heads, d_heads = [], [], [], [], []
            for head in range(2):
                mask = first_head if head == 0 else jnp.logical_not(first_head)
                d_head = jnp.where(mask, d_out, jnp.zeros_like(d_out))
                share = probs[layer, head, pair_rows(pair)]
                d_share = dot_nt(d_head, values)
                wide = share.astype(F32)
                product = wide * d_share
                d_score = (product - wide * jnp.sum(product, axis=-1, keepdims=True)).astype(BF16)
                found.append(dot_nn(d_score, keys))
                score_grads.append(d_score)
                shares.append(share)
                q_heads.append(jnp.where(mask, q_rows, jnp.zeros_like(q_rows)))
                d_heads.append(d_head)
            d_query = (jnp.where(first_head, found[0], found[1]) * 0.125).astype(BF16)
            d_mix[pair_rows(pair), 0:128] = d_query
            vec[layer, 9:10, 0:128] += sum_rows(d_query.astype(F32))
            d_keys = dot_tn(jnp.concatenate(score_grads, 0), jnp.concatenate(q_heads, 0))
            d_values = dot_tn(jnp.concatenate(shares, 0), jnp.concatenate(d_heads, 0))
            d_kv[:, :, 0:128] += d_keys.reshape(2, LANE * ROWS, 128)
            d_kv[:, :, 128:256] += d_values.reshape(2, LANE * ROWS, 128)

        each_pair(attend_back)
        gather_finish(layer, 3)
        kv_back = remote(d_kv.at[other], d_kv_in.at[layer],
                         kv_send.at[1, layer], kv_recv.at[1, layer], to_core)
        kv_back.start()
        grads = dot_tn(attended[layer], whole(layer, 3)).astype(BF16)
        grad_a[layer, 0, 192:256] = grads[0:64]
        grad_a[layer, 1, 192:256] = grads[64:128]
        kv_back.wait_recv()
        totals = (d_kv[core] + d_kv_in[layer]).astype(BF16)
        d_mix[:, 128:384] = totals
        vec[layer, 9:10, 128:256] = sum_rows(totals[:, 128:256].astype(F32))

        def project_back(pair):
            part_start(3, pair, dot_nn(d_mix[pair_rows(pair)], qkv_w[layer].reshape(384, D)))

        each_pair(project_back, 1)
        for third in range(3):
            grads = dot_tn(d_mix[:, third * 128:third * 128 + 128], whole(layer, 0)).astype(BF16)
            grad_a[layer, 0, third * 64:third * 64 + 64] = grads[0:64]
            grad_a[layer, 1, third * 64:third * 64 + 64] = grads[64:128]
        core_copy(1, layer).start()
        kv_back.wait_send()
        d_normed = part_sum(3)
        unit, inv = units[layer, 0], get_inv(layer, 0)
        vec[layer, 0:1] = sum_rows(d_normed * unit)
        vec[layer, 1:2] = sum_rows(d_normed)
        rounded = (hidden[...] + normalize_back(d_normed, unit, inv, vector(layer, 0))).astype(BF16)
        outs[1, layer] = rounded
        cot[...] = rounded.astype(F32)
        core_sum_and_send(1, layer)

    out_copy(1).start()

    def lane_copy(dest):
        return remote(vec.at[:, pl.ds(0, 8)], lane_vec.at[lane],
                      lane_send.at[dest], lane_recv.at[lane], chip(dest))

    for step in range(1, LANE):
        lane_copy(ahead(step)).start()
    for step in range(1, LANE):
        source = ahead(step)
        remote(vec.at[:, pl.ds(0, 8)], lane_vec.at[source],
               lane_send.at[source], lane_recv.at[source], to_core).wait_recv()
    for step in range(1, LANE):
        lane_copy(ahead(step)).wait_send()
    for step in range(1, LANE):
        vec[:, 0:8] += lane_vec[ahead(step)]
    cv_copy = remote(vec, core_vec, cv_send.at[0], cv_recv.at[0], to_core)
    cv_copy.start()
    cv_copy.wait()
    vec[...] += core_vec[...]

    def group_copy(layer, quarter):
        return remote(vec.at[layer], group_vec.at[member], gv_send.at[layer, quarter],
                      gv_recv.at[member], {"section": layer, "dp": quarter})

    for layer in range(2):
        for quarter in range(DP):
            @pl.when(jnp.logical_not(owned(layer, quarter)))
            def _():
                group_copy(layer, quarter).start()

    def full_copy(kind, dest):
        ref = (full_m, full_a)[kind]
        return remote(ref.at[group], ref.at[group], dp_send.at[kind, dest],
                      dp_recv.at[kind, group], {"dp": dest})

    for kind in range(2):
        mine, recv, full, length = ((mine_m, recv_m, full_m, 128),
                                    (mine_a, recv_a, full_a, 64))[kind]
        for step in range(1, 2 * DP):
            source = lax.rem(member + step, 2 * DP)
            block = recv.at[source]
            remote(block, block, dp_send.at[kind, 0], pair_recv.at[kind, source],
                   to_core).wait_recv()
        total = mine[section, pl.ds(pl.multiple_of(group * length, length), length)].astype(F32)
        for step in range(1, 2 * DP):
            total = total + recv[lax.rem(member + step, 2 * DP)].astype(F32)
        full[group] = total.astype(BF16)
        for step in range(1, DP):
            full_copy(kind, lax.rem(group + step, DP)).start()

    for step in range(1, 2 * DP):
        source = lax.rem(member + step, 2 * DP)
        block = group_vec.at[source]
        remote(block, block, gv_send.at[0, 0], gv_recv.at[source], to_core).wait_recv()
    total = vec[section]
    for step in range(1, 2 * DP):
        total = total + group_vec[lax.rem(member + step, 2 * DP)]
    sm_ref[...] = total

    for which, ref in ((0, so_ref), (1, ig_ref)):
        out_copy(which).wait()
        ref[section] = outs[which, section]
        ref[1 - section] = outs_in[which]

    for kind in range(2):
        full, length, base = ((full_m, 128, 0), (full_a, 64, 512))[kind]
        for step in range(1, DP):
            source = lax.rem(group + step, DP)
            block = full.at[source]
            remote(block, block, dp_send.at[kind, source], dp_recv.at[kind, source],
                   to_core).wait_recv()
        gw_ref[base:base + DP * length] = full[...].reshape(DP * length, D).astype(F32)

    for kind in range(5):
        core_piece(kind).wait_send()
        section_piece(kind).wait_send()
        relay_piece(kind).wait_send()
    for kind in range(2):
        for step in range(1, DP):
            full_copy(kind, lax.rem(group + step, DP)).wait_send()
        for layer in range(2):
            core_copy(kind, layer).wait_send()
            for quarter in range(DP):
                @pl.when(jnp.logical_not(owned(layer, quarter)))
                def _():
                    owner_copy(kind, layer, quarter).wait_send()
    for layer in range(2):
        for quarter in range(DP):
            @pl.when(jnp.logical_not(owned(layer, quarter)))
            def _():
                group_copy(layer, quarter).wait_send()


def run_layers(x_rows, cot_rows, small, qkv, out, up, down):
    vmem = pl.BlockSpec(memory_space=pltpu.VMEM)
    anywhere = pl.BlockSpec(memory_space=pl.ANY)
    dma = pltpu.SemaphoreType.DMA
    tokens = LANE * ROWS
    scratch = [
        pltpu.VMEM((2, 2, 16, D), F32),
        pltpu.VMEM((2, 3, 2, 64, D), BF16),
        pltpu.VMEM((2, 2, 64, D), BF16),
        pltpu.VMEM((2, 2, 256, D), BF16),
        pltpu.VMEM((2, 2, 256, D), BF16),
        pltpu.VMEM((2, GATHERS, LANE, ROWS, D), BF16),
        pltpu.VMEM((2, LANE, ROWS, D), BF16),
        pltpu.VMEM((2, LANE, ROWS, D), BF16),
        pltpu.VMEM((2, ROWS, D), F32),
        pltpu.VMEM((2, 2, ROWS, D), F32),
        pltpu.VMEM((2, 2, ROWS, 128), F32),
        pltpu.VMEM((2, 2, ROWS, D), F32),
        pltpu.VMEM((ROWS, D), F32),
        pltpu.VMEM((ROWS, D), F32),
        pltpu.VMEM((2, tokens, 128), BF16),
        pltpu.VMEM((2, 2, tokens, 256), BF16),
        pltpu.VMEM((2, tokens, 128), BF16),
        pltpu.VMEM((2, 2, tokens, 2 * tokens), BF16),
        pltpu.VMEM((2, tokens, 512), BF16),
        pltpu.VMEM((2, tokens, 512), F32),
        pltpu.VMEM((tokens, 512), BF16),
        pltpu.VMEM((tokens, 384), BF16),
        pltpu.VMEM((2, tokens, 256), F32),
        pltpu.VMEM((2, tokens, 256), F32),
        pltpu.VMEM((16, 128), F32),
        pltpu.VMEM((2, 2, 512, D), BF16),
        pltpu.VMEM((2, 2, 256, D), BF16),
        pltpu.VMEM((2, 512, D), BF16),
        pltpu.VMEM((2, 256, D), BF16),
        pltpu.VMEM((2, 512, D), BF16),
        pltpu.VMEM((2, 256, D), BF16),
        pltpu.VMEM((2 * DP, 128, D), BF16),
        pltpu.VMEM((2 * DP, 64, D), BF16),
        pltpu.VMEM((DP, 128, D), BF16),
        pltpu.VMEM((DP, 64, D), BF16),
        pltpu.VMEM((2, 16, D), F32),
        pltpu.VMEM((LANE, 2, 8, D), F32),
        pltpu.VMEM((2, 16, D), F32),
        pltpu.VMEM((2 * DP, 16, D), F32),
        pltpu.VMEM((2, 2, ROWS, D), BF16),
        pltpu.VMEM((2, ROWS, D), BF16),
        dma((5,)), dma((3, 5)), dma((3, 5)),
        dma((LANE,)), dma((GATHERS, LANE)),
        dma((LANE,)), dma((GATHERS, LANE)),
        dma((2, 2)), dma((2, 2)),
        dma((2, 2)), dma((2, 2)),
        dma((2, 2, DP)), dma((2, 2 * DP)),
        dma((2, DP)), dma((2, DP)),
        dma((2,)), dma((2,)),
        dma((LANE,)), dma((LANE,)),
        dma((1,)), dma((1,)),
        dma((2, DP)), dma((2 * DP,)),
    ]
    return pl.pallas_call(
        kernel,
        out_shape=(
            jax.ShapeDtypeStruct((2, ROWS, D), BF16),
            jax.ShapeDtypeStruct((2, ROWS, D), BF16),
            jax.ShapeDtypeStruct((768, D), F32),
            jax.ShapeDtypeStruct((16, D), F32),
        ),
        in_specs=[vmem, vmem] + [anywhere] * 5,
        out_specs=(vmem,) * 4,
        scratch_shapes=scratch,
        name="two_layers",
        compiler_params=pltpu.CompilerParams(
            collective_id=0, has_side_effects=True, vmem_limit_bytes=63 * 2**20
        ),
    )(x_rows, cot_rows, small, qkv, out, up, down)


def body(
    images, out_grad, live_images, attn_in, qv_bias, attn_out, mlp_in, mlp_bias, mlp_out, vectors
):
    section = lax.axis_index("section")
    core = lax.rem(lax.axis_index("tensor"), 2)
    counts = live_images.reshape(-1, MICRO)
    totals = jnp.sum(counts, axis=0).astype(F32)
    own = lax.dynamic_slice(counts, (lax.axis_index("dp"), section), (1, 1))[0, 0]
    weight = jnp.where(own > 0, 1.0 / totals[section], F32(0.0))
    x_rows = lax.dynamic_index_in_dim(images, section, 0, keepdims=False)
    cot_rows = lax.dynamic_index_in_dim(out_grad, section, 0, keepdims=False).astype(F32) * weight
    gap = jnp.zeros((64,), F32)
    biases = jnp.concatenate(
        [qv_bias[0, 0], gap, qv_bias[0, 1], gap, mlp_bias[0], jnp.zeros((512,), F32)])
    small = jnp.concatenate([vectors[0], biases[None], jnp.zeros((7, D), F32)], axis=0)
    qkv = attn_in[0].transpose(1, 2, 0)
    up = mlp_in[0].T
    section_out, section_in_grad, grads, sums = run_layers(
        x_rows, cot_rows, small, qkv, attn_out[0], up, mlp_out[0])
    g_in = grads[512:704].reshape(3, 64, D).transpose(2, 0, 1)
    g_up_bias = lax.dynamic_slice(sums, (8, core * 256), (1, 256))
    g_query = lax.dynamic_slice(sums, (9, core * 64), (1, 64))
    g_value = lax.dynamic_slice(sums, (9, 128 + core * 64), (1, 64))
    return (
        section_out[None],
        section_in_grad[None],
        g_in[None],
        jnp.concatenate([g_query, g_value], axis=0)[None],
        grads[704:768][None],
        grads[0:256].T[None],
        g_up_bias,
        grads[256:512][None],
        sums[0:8][None],
    )


def solution(mesh):
    placed = (
        P("dp", "tensor", None),
        P("dp", "tensor", None),
        P(),
        P("section", None, None, "tensor"),
        P("section", None, "tensor"),
        P("section", "tensor", None),
        P("section", None, "tensor"),
        P("section", "tensor"),
        P("section", "tensor", None),
        P("section", None, None),
    )
    return jax.shard_map(
        body,
        mesh=mesh,
        in_specs=placed,
        out_specs=(
            P("section", "dp", "tensor", None),
            P("section", "dp", "tensor", None),
            P("section", None, None, "tensor"),
            P("section", None, "tensor"),
            P("section", "tensor", None),
            P("section", None, "tensor"),
            P("section", "tensor"),
            P("section", "tensor", None),
            P("section", None, None),
        ),
        check_vma=False,
    )
```

```python
import jax
import jax.numpy as jnp
from jax import lax
from jax.experimental import pallas as pl
from jax.experimental.pallas import tpu as pltpu
from jax.sharding import PartitionSpec as P

MESH = pl.DeviceIdType.MESH
F32 = jnp.float32
BF16 = jnp.bfloat16
EPSILON = 1e-06
D = 1024
MICRO = 2
LANE = 4
QUAD = 4
ROWS = 64
PAIRS = LANE // 2
TOKENS = LANE * ROWS
DP = 4
BIAS_ROW = 8
GATHERS = 4
SMALL, ATTN, MLP = range(3)


def dot_nn(a, b):
    return lax.dot_general(a, b, (((1,), (0,)), ((), ())), preferred_element_type=F32)


def dot_nt(a, b):
    return lax.dot_general(a, b, (((1,), (1,)), ((), ())), preferred_element_type=F32)


def dot_tn(a, b):
    return lax.dot_general(a, b, (((0,), (0,)), ((), ())), preferred_element_type=F32)


def normalize(rows):
    center = rows - jnp.mean(rows, axis=-1, keepdims=True)
    inv = lax.rsqrt(jnp.mean(center * center, axis=-1, keepdims=True) + EPSILON)
    return center * inv, inv


def normalize_back(grad, unit, inv, gain):
    scaled = grad * gain
    return inv * (
        scaled
        - jnp.mean(scaled, axis=-1, keepdims=True)
        - unit * jnp.mean(scaled * unit, axis=-1, keepdims=True)
    )


def sum_rows(rows):
    return jnp.sum(rows, axis=0, keepdims=True)


def kernel(
    x_in, cot_in, small_in, attn_in, mlp_in,
    so_ref, ig_ref, gm_ref, ga_ref, sm_ref,
    small_w, attn_w, mlp_w,
    gathered, parts, landed,
    xs, units, invs, branches, hidden, cot,
    qkv_out, qkv_got, queries, keys, values, att_out, att_got, attended, probs,
    act, slope, d_pre, d_att_got, d_keys, d_values,
    grad_m, grad_a, core_m, core_a, dp_m, dp_a, part_m, part_a, recv_m, recv_a, full_m, full_a,
    vec, lane_vec, core_vec, x_vec, dp_vec, outs, outs_in,
    w_local, w_x_send, w_x_recv, w_dp_send, w_dp_recv, w_core_send, w_core_recv,
    ag_send, ag_recv, rs_send, rs_recv, quad_send, quad_recv,
    core_send, core_recv, dp_send, dp_recv, x_send, x_recv, full_send, full_recv,
    out_send, out_recv, lane_send, lane_recv, cv_send, cv_recv, xv_send, xv_recv,
    yv_send, yv_recv,
):
    section = lax.axis_index("section")
    group = lax.axis_index("dp")
    tensor = lax.axis_index("tensor")
    core = lax.rem(tensor, 2)
    lane = lax.rem(tensor // 2, LANE)
    high = tensor // (2 * LANE)
    own_pair = lane // 2
    other = 1 - core
    quad = high * 2 + core
    along_x = section * 2 + high

    def place(high_at, lane_at, core_at):
        return (high_at * LANE + lane_at) * 2 + core_at

    def to_lane(index):
        return {"tensor": place(high, index, core)}

    def to_quad(index):
        return {"tensor": place(index // 2, lane, lax.rem(index, 2))}

    def to_x(section_at, high_at):
        return {"section": section_at, "tensor": place(high_at, lane, core)}

    def to_dp(index):
        return {"dp": index}

    to_core = {"tensor": place(high, lane, other)}

    def next_of(own, step, count):
        return lax.rem(own + step, count)

    def remote(src, dst, send_sem, recv_sem, device):
        return pltpu.make_async_remote_copy(
            src_ref=src, dst_ref=dst, send_sem=send_sem, recv_sem=recv_sem,
            device_id=device, device_id_type=MESH,
        )

    def arrival(block, recv_sem):
        return remote(block, block, cv_send.at[0], recv_sem, to_core)

    sources = (small_in, attn_in, mlp_in)
    stores = (small_w, attn_w, mlp_w)

    def local_piece(kind):
        return pltpu.make_async_copy(
            sources[kind], stores[kind].at[section, quad], w_local.at[kind])

    for kind in range(3):
        local_piece(kind).start()

    barrier = pltpu.get_barrier_semaphore()
    friends = [to_lane(next_of(lane, step, LANE)) for step in range(1, LANE)]
    friends += [to_quad(next_of(quad, step, QUAD)) for step in range(1, QUAD)]
    friends += [to_x(1 - section, high), to_x(1 - section, 1 - high)]
    friends += [to_dp(next_of(group, step, DP)) for step in range(1, DP)]
    for friend in friends:
        pl.semaphore_signal(barrier, inc=1, device_id=friend, device_id_type=MESH)
    pl.semaphore_wait(barrier, len(friends))

    def is_own(layer, source):
        return jnp.logical_and(layer == section, source == high)

    def quarter(index):
        return pl.ds(pl.multiple_of(index * 128, 128), 128)

    def x_piece(kind, step):
        peer = next_of(along_x, step, 4)
        origin, there = sources[kind], stores[kind].at[section, quad]
        if kind == MLP:
            origin, there = origin.at[quarter(group)], there.at[quarter(group)]
        return remote(origin, there, w_x_send.at[kind, step], w_x_recv.at[kind, along_x],
                      to_x(peer // 2, lax.rem(peer, 2)))

    def dp_piece(layer, source, step):
        block = mlp_w.at[layer, source * 2 + core, quarter(group)]
        return remote(block, block, w_dp_send.at[layer * 2 + source, step],
                      w_dp_recv.at[layer * 2 + source, group], to_dp(next_of(group, step, DP)))

    def core_piece(kind, layer, source):
        block = stores[kind].at[layer, source * 2 + core]
        return remote(block, block, w_core_send.at[kind, layer * 2 + source],
                      w_core_recv.at[kind, layer * 2 + source], to_core)

    def send_pieces(kind):
        for step in range(1, 4):
            x_piece(kind, step).start()

    def spread_pieces(layer):
        for source in range(2):
            @pl.when(jnp.logical_not(is_own(layer, source)))
            def _():
                arrival(mlp_w.at[layer, source * 2 + core, quarter(group)],
                        w_x_recv.at[MLP, layer * 2 + source]).wait_recv()
                for step in range(1, DP):
                    dp_piece(layer, source, step).start()

    def relay_pieces(kind, layer):
        for source in range(2):
            @pl.when(is_own(layer, source))
            def _():
                local_piece(kind).wait()

            @pl.when(jnp.logical_not(is_own(layer, source)))
            def _():
                if kind == MLP:
                    for step in range(1, DP):
                        sender = next_of(group, step, DP)
                        arrival(mlp_w.at[layer, source * 2 + core, quarter(sender)],
                                w_dp_recv.at[layer * 2 + source, sender]).wait_recv()
                else:
                    arrival(stores[kind].at[layer, source * 2 + core],
                            w_x_recv.at[kind, layer * 2 + source]).wait_recv()

            core_piece(kind, layer, source).start()

    def take_pieces(kind, layer):
        for source in range(2):
            arrival(stores[kind].at[layer, source * 2 + other],
                    w_core_recv.at[kind, layer * 2 + source]).wait_recv()

    def gather_copy(layer, which, step):
        block = gathered.at[layer, which, lane]
        dest = jnp.bitwise_xor(lane, step)
        return remote(block, block, ag_send.at[step], ag_recv.at[which, lane], to_lane(dest))

    def gather_start(layer, which, rows):
        gathered[layer, which, lane] = rows
        for step in (2, 3, 1):
            gather_copy(layer, which, step).start()

    def gather_finish(layer, which):
        for step in (2, 3, 1):
            gather_copy(layer, which, step).wait_send()

    def gather_take(layer, which, pair):
        for side in range(2):
            source = pair * 2 + side

            @pl.when(source != lane)
            def _():
                arrival(gathered.at[layer, which, source], ag_recv.at[which, source]).wait_recv()

        return gathered[layer, which, pl.ds(pair * 2, 2)].reshape(2 * ROWS, D)

    def whole(layer, which):
        return gathered[layer, which].reshape(TOKENS, D)

    def part_copy(which, dest):
        return remote(parts.at[which % 2, dest], landed.at[which % 2, lane],
                      rs_send.at[dest], rs_recv.at[which, lane], to_lane(dest))

    def part_start(which, pair, rows):
        parts[which % 2, pl.ds(pair * 2, 2)] = rows.astype(BF16).reshape(2, ROWS, D)
        for side in range(2):
            dest = pair * 2 + side

            @pl.when(dest != lane)
            def _():
                part_copy(which, dest).start()

    def part_sum(which):
        total = parts[which % 2, lane].astype(F32)
        for step in range(1, LANE):
            source = next_of(lane, step, LANE)
            arrival(landed.at[which % 2, source], rs_recv.at[which, source]).wait_recv()
            total = total + landed[which % 2, source].astype(F32)
        for step in range(1, LANE):
            part_copy(which, next_of(lane, step, LANE)).wait_send()
        return total

    def each_pair(work, first=0):
        @pl.loop(0, PAIRS)
        def _(step):
            work(lax.rem(own_pair + first + step, PAIRS))

    def pair_rows(pair):
        return pl.ds(pl.multiple_of(pair * 2 * ROWS, 2 * ROWS), 2 * ROWS)

    d_att_out, d_mix_out, d_mix_got = att_out, qkv_out, qkv_got
    exchanges = ((qkv_out, qkv_got), (att_out, att_got), (d_att_out, d_att_got),
                 (d_mix_out, d_mix_got))

    def quad_copy(which, dest):
        origin, there = exchanges[which]
        return remote(origin.at[dest], there.at[quad], quad_send.at[which, dest],
                      quad_recv.at[which, quad], to_quad(dest))

    def quad_start(which):
        origin, there = exchanges[which]
        for step in (2, 3, 1):
            quad_copy(which, jnp.bitwise_xor(quad, step)).start()
        there[quad] = origin[quad]

    def quad_take(which):
        there = exchanges[which][1]
        for step in (1, 2, 3):
            source = jnp.bitwise_xor(quad, step)
            arrival(there.at[source], quad_recv.at[which, source]).wait_recv()

    def quad_finish(which):
        for step in (1, 2, 3):
            quad_copy(which, jnp.bitwise_xor(quad, step)).wait_send()

    def token_rows(source, half=0, length=TOKENS):
        return pl.ds(pl.multiple_of(source * TOKENS + half * length, length), length)

    def vector(layer, row):
        return small_w[layer, quad, row:row + 1]

    def all_biases(layer, first):
        row = slice(BIAS_ROW, BIAS_ROW + 1)
        return jnp.concatenate(
            [small_w[layer, member, row, first:first + 256] for member in range(QUAD)], axis=-1)

    def keep_inv(layer, which, inv):
        invs[layer, which] = jnp.broadcast_to(inv, (ROWS, 128))

    def get_inv(layer, which):
        return invs[layer, which, :, 0:1]

    def attn_weights(layer):
        return attn_w[layer].reshape(QUAD * 256, D)

    def out_weights(layer):
        return attn_w[layer, :, 192:256].reshape(QUAD * 64, D)

    def up_weights(layer):
        return mlp_w[layer, :, 0:256].reshape(QUAD * 256, D)

    def down_weights(layer):
        return mlp_w[layer, :, 256:512].reshape(QUAD * 256, D)

    send_pieces(SMALL)

    @pl.when(section == 0)
    def _():
        send_pieces(ATTN)
        send_pieces(MLP)

    xs[0] = x_in[...].astype(F32)
    vec[...] = jnp.zeros_like(vec)
    for layer in range(2):
        relay_pieces(SMALL, layer)

    @pl.loop(0, 2)
    def _(layer):
        unit, inv = normalize(xs[layer])
        units[layer, 0] = unit
        keep_inv(layer, 0, inv)
        gather_start(layer, 0, (unit * vector(layer, 0) + vector(layer, 1)).astype(BF16))

        @pl.when(layer == 0)
        def _():
            relay_pieces(ATTN, 0)
            for either in range(2):
                take_pieces(SMALL, either)

        take_pieces(ATTN, layer)
        qkv_bias = all_biases(layer, 0)

        def project(pair):
            rows = gather_take(layer, 0, pair)
            mixed = (dot_nt(rows, attn_weights(layer)) + qkv_bias).astype(BF16)
            for member in range(QUAD):
                qkv_out[member, pair_rows(pair)] = mixed[:, member * 256:member * 256 + 256]

        each_pair(project)
        quad_start(0)

        @pl.when(layer == 0)
        def _():
            @pl.when(section == 1)
            def _():
                send_pieces(ATTN)
                send_pieces(MLP)

            spread_pieces(0)

        @pl.when(layer == 1)
        def _():
            relay_pieces(MLP, 1)

        quad_take(0)
        for source in range(QUAD):
            block = qkv_got[source]
            queries[layer, token_rows(source)] = (block[:, 0:64].astype(F32) * 0.125).astype(BF16)
            keys[layer, token_rows(source)] = block[:, 64:128]
            values[layer, token_rows(source)] = block[:, 128:192]

        @pl.loop(0, QUAD)
        def _(step):
            source = lax.rem(quad + 1 + step, QUAD)
            for half in range(2):
                rows = token_rows(source, half, 128)
                scores = dot_nt(queries[layer, rows], keys[layer])
                grown = jnp.exp(scores - jnp.max(scores, axis=-1, keepdims=True))
                share = (grown / jnp.sum(grown, axis=-1, keepdims=True)).astype(BF16)
                probs[layer, rows] = share
                att_out[source, half * 128:half * 128 + 128] = dot_nn(
                    share, values[layer]).astype(BF16)

            @pl.when(source != quad)
            def _():
                quad_copy(1, source).start()

        att_got[quad] = att_out[quad]
        quad_take(1)
        attended[layer] = jnp.concatenate([att_got[member] for member in range(QUAD)], axis=-1)

        def project_out(pair):
            part_start(0, pair, dot_nn(attended[layer, pair_rows(pair)], out_weights(layer)))

        each_pair(project_out, 1)
        quad_finish(0)
        quad_finish(1)
        gather_finish(layer, 0)
        branch = part_sum(0) + vector(layer, 2)
        branches[layer, 0] = branch
        state = xs[layer] + vector(layer, 3) * branch
        hidden[...] = state

        unit, inv = normalize(state)
        units[layer, 1] = unit
        keep_inv(layer, 1, inv)
        gather_start(layer, 1, (unit * vector(layer, 4) + vector(layer, 5)).astype(BF16))

        @pl.when(layer == 0)
        def _():
            relay_pieces(MLP, 0)
            spread_pieces(1)

        take_pieces(MLP, layer)
        up_bias = all_biases(layer, 256)

        def feed(pair):
            rows = gather_take(layer, 1, pair)
            pre = dot_nt(rows, up_weights(layer)) + up_bias
            cdf = 0.5 + 0.5 * lax.erf(pre * 0.7071067811865476)
            bell = jnp.exp(-0.5 * pre * pre) * 0.3989422804014327
            value = (pre * cdf).astype(BF16)
            act[layer, pair_rows(pair)] = value
            slope[layer, pair_rows(pair)] = (cdf + pre * bell).astype(BF16)
            part_start(1, pair, dot_nn(value, down_weights(layer)))

        each_pair(feed)

        @pl.when(layer == 0)
        def _():
            relay_pieces(ATTN, 1)

        gather_finish(layer, 1)
        branch = part_sum(1) + vector(layer, 6)
        branches[layer, 1] = branch
        rounded = (hidden[...] + vector(layer, 7) * branch).astype(BF16)
        outs[0, layer] = rounded

        @pl.when(layer == 0)
        def _():
            xs[1] = rounded.astype(F32)

    def out_copy(which):
        return remote(outs.at[which, 1 - section], outs_in.at[which],
                      out_send.at[which], out_recv.at[which], to_x(1 - section, high))

    out_copy(0).start()

    grads = (grad_m, grad_a)
    from_core = (core_m, core_a)
    from_dp = (dp_m, dp_a)
    quarters = (part_m, part_a)
    from_x = (recv_m, recv_a)
    fulls = (full_m, full_a)
    lengths = (128, 64)

    def core_copy(kind):
        return remote(grads[kind].at[:, other], from_core[kind],
                      core_send.at[kind], core_recv.at[kind], to_core)

    def dp_rows(kind, index):
        length = lengths[kind]
        return pl.ds(pl.multiple_of(index * length, length), length)

    def dp_copy(kind, layer, step):
        dest = next_of(group, step, DP)
        return remote(grads[kind].at[:, core, dp_rows(kind, dest)],
                      from_dp[kind].at[layer, step - 1],
                      dp_send.at[kind, step], dp_recv.at[kind, layer, step], to_dp(dest))

    def x_copy(kind, layer, source):
        return remote(quarters[kind].at[layer, source], from_x[kind].at[along_x],
                      x_send.at[kind, layer * 2 + source], x_recv.at[kind, along_x],
                      to_x(layer, source))

    def core_done(kind, layer):
        core_copy(kind).wait()
        for source in range(2):
            grads[kind][source, core] = (
                grads[kind][source, core].astype(F32) + from_core[kind][source].astype(F32)
            ).astype(BF16)
        for step in range(1, DP):
            dp_copy(kind, layer, step).start()

    def dp_done(kind, layer):
        total = grads[kind][:, core, dp_rows(kind, group)].astype(F32)
        for step in range(1, DP):
            arrival(from_dp[kind].at[layer, step - 1],
                    dp_recv.at[kind, layer, step]).wait_recv()
            total = total + from_dp[kind][layer, step - 1].astype(F32)
        quarters[kind][layer] = total.astype(BF16)
        for source in range(2):
            @pl.when(jnp.logical_not(is_own(layer, source)))
            def _():
                x_copy(kind, layer, source).start()
        for step in range(1, DP):
            dp_copy(kind, layer, step).wait_send()

    def full_copy(kind, step):
        ref = fulls[kind]
        return remote(ref.at[group], ref.at[group], full_send.at[kind, step],
                      full_recv.at[kind, group], to_dp(next_of(group, step, DP)))

    def x_done(kind):
        total = quarters[kind][section, high].astype(F32)
        for step in range(1, 4):
            source = next_of(along_x, step, 4)
            arrival(from_x[kind].at[source], x_recv.at[kind, source]).wait_recv()
            total = total + from_x[kind][source].astype(F32)
        fulls[kind][group] = total.astype(BF16)
        for step in range(1, DP):
            full_copy(kind, step).start()

    cot[...] = cot_in[...]

    @pl.loop(0, 2)
    def _(turn):
        layer = 1 - turn
        above = cot[...]
        d_branch2 = (above * vector(layer, 7)).astype(BF16)
        gather_start(layer, 2, d_branch2)
        vec[layer, 7:8] = sum_rows(above * branches[layer, 1])
        vec[layer, 6:7] = sum_rows(d_branch2.astype(F32))

        @pl.when(turn == 1)
        def _():
            core_done(1, 1)

        def feed_back(pair):
            rows = gather_take(layer, 2, pair)
            d_act = dot_nt(rows, down_weights(layer))
            back = (d_act * slope[layer, pair_rows(pair)].astype(F32)).astype(BF16)
            d_pre[pair_rows(pair)] = back
            vec[layer, 8:9] += sum_rows(back.astype(F32))
            part_start(2, pair, dot_nn(back, up_weights(layer)))

        each_pair(feed_back)
        gather_finish(layer, 2)
        for member in range(QUAD):
            units_of = slice(member * 256, member * 256 + 256)
            at = (member // 2, member % 2)
            grad_m[at[0], at[1], 0:256] = dot_tn(d_pre[:, units_of], whole(layer, 1)).astype(BF16)
            grad_m[at[0], at[1], 256:512] = dot_tn(
                act[layer, :, units_of], whole(layer, 2)).astype(BF16)
        core_copy(0).start()
        d_normed = part_sum(2)
        unit, inv = units[layer, 1], get_inv(layer, 1)
        vec[layer, 4:5] = sum_rows(d_normed * unit)
        vec[layer, 5:6] = sum_rows(d_normed)
        d_hidden = above + normalize_back(d_normed, unit, inv, vector(layer, 4))
        hidden[...] = d_hidden
        d_branch = (d_hidden * vector(layer, 3)).astype(BF16)
        gather_start(layer, 3, d_branch)
        vec[layer, 3:4] = sum_rows(d_hidden * branches[layer, 0])
        vec[layer, 2:3] = sum_rows(d_branch.astype(F32))
        core_done(0, layer)

        def out_back(pair):
            rows = gather_take(layer, 3, pair)
            d_out = dot_nt(rows, out_weights(layer)).astype(BF16)
            for member in range(QUAD):
                d_att_out[member, pair_rows(pair)] = d_out[:, member * 64:member * 64 + 64]

        each_pair(out_back)
        quad_start(2)
        gather_finish(layer, 3)

        @pl.when(turn == 1)
        def _():
            dp_done(1, 1)

        out_grads = dot_tn(attended[layer], whole(layer, 3)).astype(BF16)
        d_keys[...] = jnp.zeros_like(d_keys)
        d_values[...] = jnp.zeros_like(d_values)
        quad_take(2)

        @pl.loop(0, QUAD)
        def _(source):
            score_grads = []
            for half in range(2):
                rows = token_rows(source, half, 128)
                d_share = dot_nt(d_att_got[source, half * 128:half * 128 + 128], values[layer])
                wide = probs[layer, rows].astype(F32)
                product = wide * d_share
                d_score = (product - wide * jnp.sum(product, axis=-1, keepdims=True)).astype(BF16)
                score_grads.append(d_score)
                d_mix_out[source, half * 128:half * 128 + 128, 0:64] = (
                    dot_nn(d_score, keys[layer]) * 0.125).astype(BF16)
            d_keys[...] += dot_tn(jnp.concatenate(score_grads, 0),
                                  queries[layer, token_rows(source)])
            d_values[...] += dot_tn(probs[layer, token_rows(source)], d_att_got[source])

        for source in range(QUAD):
            d_mix_out[source, :, 64:128] = d_keys[token_rows(source)].astype(BF16)
            d_mix_out[source, :, 128:192] = d_values[token_rows(source)].astype(BF16)
            d_mix_out[source, :, 192:256] = jnp.zeros((TOKENS, 64), BF16)
        quad_start(3)
        for member in range(QUAD):
            grad_a[member // 2, member % 2, 192:256] = out_grads[member * 64:member * 64 + 64]
        quad_take(3)

        def project_back(pair):
            rows = jnp.concatenate(
                [d_mix_got[member, pair_rows(pair)] for member in range(QUAD)], axis=-1)
            vec[layer, 9:10] += sum_rows(rows.astype(F32))
            part_start(3, pair, dot_nn(rows, attn_weights(layer)))

        each_pair(project_back, 1)
        for member in range(QUAD):
            grad_a[member // 2, member % 2, 0:192] = dot_tn(
                d_mix_got[member], whole(layer, 0))[0:192].astype(BF16)
        core_copy(1).start()
        quad_finish(2)
        quad_finish(3)
        dp_done(0, layer)
        d_normed = part_sum(3)
        unit, inv = units[layer, 0], get_inv(layer, 0)
        vec[layer, 0:1] = sum_rows(d_normed * unit)
        vec[layer, 1:2] = sum_rows(d_normed)
        rounded = (hidden[...] + normalize_back(d_normed, unit, inv, vector(layer, 0))).astype(BF16)
        outs[1, layer] = rounded
        cot[...] = rounded.astype(F32)

    core_done(1, 0)
    out_copy(1).start()
    x_done(0)

    def lane_copy(dest):
        return remote(vec.at[:, pl.ds(0, 8)], lane_vec.at[lane],
                      lane_send.at[dest], lane_recv.at[lane], to_lane(dest))

    for step in range(1, LANE):
        lane_copy(next_of(lane, step, LANE)).start()
    for step in range(1, LANE):
        source = next_of(lane, step, LANE)
        arrival(lane_vec.at[source], lane_recv.at[source]).wait_recv()
    for step in range(1, LANE):
        lane_copy(next_of(lane, step, LANE)).wait_send()
    for step in range(1, LANE):
        vec[:, 0:8] += lane_vec[next_of(lane, step, LANE)]
    cv_copy = remote(vec, core_vec, cv_send.at[0], cv_recv.at[0], to_core)
    cv_copy.start()
    cv_copy.wait()
    vec[...] += core_vec[...]

    def xv_copy(layer, source):
        return remote(vec.at[layer], x_vec.at[along_x], xv_send.at[layer * 2 + source],
                      xv_recv.at[along_x], to_x(layer, source))

    for layer in range(2):
        for source in range(2):
            @pl.when(jnp.logical_not(is_own(layer, source)))
            def _():
                xv_copy(layer, source).start()

    dp_done(1, 0)

    total = vec[section]
    for step in range(1, 4):
        source = next_of(along_x, step, 4)
        arrival(x_vec.at[source], xv_recv.at[source]).wait_recv()
        total = total + x_vec[source]
    dp_vec[group] = total

    def yv_copy(step):
        return remote(dp_vec.at[group], dp_vec.at[group], yv_send.at[step],
                      yv_recv.at[group], to_dp(next_of(group, step, DP)))

    for step in range(1, DP):
        yv_copy(step).start()
    x_done(1)

    for which, ref in ((0, so_ref), (1, ig_ref)):
        out_copy(which).wait()
        ref[section] = outs[which, section]
        ref[1 - section] = outs_in[which]

    for step in range(1, DP):
        source = next_of(group, step, DP)
        arrival(dp_vec.at[source], yv_recv.at[source]).wait_recv()
        total = total + dp_vec[source]
    sm_ref[...] = total

    for kind, ref in ((0, gm_ref), (1, ga_ref)):
        for step in range(1, DP):
            source = next_of(group, step, DP)
            arrival(fulls[kind].at[source], full_recv.at[kind, source]).wait_recv()
        ref[...] = fulls[kind][...].reshape(DP * lengths[kind], D)

    for kind in range(3):
        for step in range(1, 4):
            x_piece(kind, step).wait_send()
        for layer in range(2):
            for source in range(2):
                core_piece(kind, layer, source).wait_send()
    for layer in range(2):
        for source in range(2):
            @pl.when(jnp.logical_not(is_own(layer, source)))
            def _():
                for step in range(1, DP):
                    dp_piece(layer, source, step).wait_send()
                for kind in range(2):
                    x_copy(kind, layer, source).wait_send()
                xv_copy(layer, source).wait_send()
    for step in range(1, DP):
        yv_copy(step).wait_send()
        for kind in range(2):
            full_copy(kind, step).wait_send()


def run_layers(x_rows, cot_rows, small, attn, mlp):
    vmem = pl.BlockSpec(memory_space=pltpu.VMEM)
    anywhere = pl.BlockSpec(memory_space=pl.ANY)
    dma = pltpu.SemaphoreType.DMA
    every = QUAD * TOKENS
    scratch = [
        pltpu.VMEM((2, QUAD, 16, D), F32),
        pltpu.VMEM((2, QUAD, 256, D), BF16),
        pltpu.VMEM((2, QUAD, 512, D), BF16),
        pltpu.VMEM((2, GATHERS, LANE, ROWS, D), BF16),
        pltpu.VMEM((2, LANE, ROWS, D), BF16),
        pltpu.VMEM((2, LANE, ROWS, D), BF16),
        pltpu.VMEM((2, ROWS, D), F32),
        pltpu.VMEM((2, 2, ROWS, D), F32),
        pltpu.VMEM((2, 2, ROWS, 128), F32),
        pltpu.VMEM((2, 2, ROWS, D), F32),
        pltpu.VMEM((ROWS, D), F32),
        pltpu.VMEM((ROWS, D), F32),
        pltpu.VMEM((QUAD, TOKENS, 256), BF16),
        pltpu.VMEM((QUAD, TOKENS, 256), BF16),
        pltpu.VMEM((2, every, 64), BF16),
        pltpu.VMEM((2, every, 64), BF16),
        pltpu.VMEM((2, every, 64), BF16),
        pltpu.VMEM((QUAD, TOKENS, 64), BF16),
        pltpu.VMEM((QUAD, TOKENS, 64), BF16),
        pltpu.VMEM((2, TOKENS, 256), BF16),
        pltpu.VMEM((2, every, every), BF16),
        pltpu.VMEM((2, TOKENS, 1024), BF16),
        pltpu.VMEM((2, TOKENS, 1024), BF16),
        pltpu.VMEM((TOKENS, 1024), BF16),
        pltpu.VMEM((QUAD, TOKENS, 64), BF16),
        pltpu.VMEM((every, 64), F32),
        pltpu.VMEM((every, 64), F32),
        pltpu.VMEM((2, 2, 512, D), BF16),
        pltpu.VMEM((2, 2, 256, D), BF16),
        pltpu.VMEM((2, 512, D), BF16),
        pltpu.VMEM((2, 256, D), BF16),
        pltpu.VMEM((2, DP - 1, 2, 128, D), BF16),
        pltpu.VMEM((2, DP - 1, 2, 64, D), BF16),
        pltpu.VMEM((2, 2, 128, D), BF16),
        pltpu.VMEM((2, 2, 64, D), BF16),
        pltpu.VMEM((4, 128, D), BF16),
        pltpu.VMEM((4, 64, D), BF16),
        pltpu.VMEM((DP, 128, D), BF16),
        pltpu.VMEM((DP, 64, D), BF16),
        pltpu.VMEM((2, 16, D), F32),
        pltpu.VMEM((LANE, 2, 8, D), F32),
        pltpu.VMEM((2, 16, D), F32),
        pltpu.VMEM((4, 16, D), F32),
        pltpu.VMEM((DP, 16, D), F32),
        pltpu.VMEM((2, 2, ROWS, D), BF16),
        pltpu.VMEM((2, ROWS, D), BF16),
        dma((3,)), dma((3, 4)), dma((3, 4)),
        dma((4, DP)), dma((4, DP)), dma((3, 4)), dma((3, 4)),
        dma((LANE,)), dma((GATHERS, LANE)),
        dma((LANE,)), dma((GATHERS, LANE)),
        dma((4, QUAD)), dma((4, QUAD)),
        dma((2,)), dma((2,)),
        dma((2, DP)), dma((2, 2, DP)),
        dma((2, 4)), dma((2, 4)),
        dma((2, DP)), dma((2, DP)),
        dma((2,)), dma((2,)),
        dma((LANE,)), dma((LANE,)),
        dma((1,)), dma((1,)),
        dma((4,)), dma((4,)),
        dma((DP,)), dma((DP,)),
    ]
    return pl.pallas_call(
        kernel,
        out_shape=(
            jax.ShapeDtypeStruct((2, ROWS, D), BF16),
            jax.ShapeDtypeStruct((2, ROWS, D), BF16),
            jax.ShapeDtypeStruct((512, D), BF16),
            jax.ShapeDtypeStruct((256, D), BF16),
            jax.ShapeDtypeStruct((16, D), F32),
        ),
        in_specs=[vmem, vmem] + [anywhere] * 3,
        out_specs=(vmem,) * 5,
        scratch_shapes=scratch,
        name="two_layers",
        compiler_params=pltpu.CompilerParams(
            collective_id=0, has_side_effects=True, vmem_limit_bytes=63 * 2**20
        ),
    )(x_rows, cot_rows, small, attn, mlp)


def body(
    images, out_grad, live_images, attn_in, qv_bias, attn_out, mlp_in, mlp_bias, mlp_out, vectors
):
    section = lax.axis_index("section")
    tensor = lax.axis_index("tensor")
    quad = tensor // (2 * LANE) * 2 + lax.rem(tensor, 2)
    counts = live_images.reshape(-1, MICRO)
    totals = jnp.sum(counts, axis=0).astype(F32)
    own = lax.dynamic_slice(counts, (lax.axis_index("dp"), section), (1, 1))[0, 0]
    weight = jnp.where(own > 0, 1.0 / totals[section], F32(0.0))
    x_rows = lax.dynamic_index_in_dim(images, section, 0, keepdims=False)
    cot_rows = lax.dynamic_index_in_dim(out_grad, section, 0, keepdims=False).astype(F32) * weight
    gap = jnp.zeros((64,), F32)
    biases = jnp.concatenate(
        [qv_bias[0, 0], gap, qv_bias[0, 1], gap, mlp_bias[0], jnp.zeros((512,), F32)])
    small = jnp.concatenate([vectors[0], biases[None], jnp.zeros((7, D), F32)], axis=0)
    attn = jnp.concatenate([attn_in[0].transpose(1, 2, 0).reshape(192, D), attn_out[0]], axis=0)
    mlp = jnp.concatenate([mlp_in[0].T, mlp_out[0]], axis=0)
    section_out, section_in_grad, g_mlp, g_attn, sums = run_layers(
        x_rows, cot_rows, small, attn, mlp)
    g_mlp, g_attn = g_mlp.astype(F32), g_attn.astype(F32)
    g_up_bias = lax.dynamic_slice(sums, (8, quad * 256), (1, 256))
    g_qkv_bias = lax.dynamic_slice(sums, (9, quad * 256), (1, 256))
    return (
        section_out[None],
        section_in_grad[None],
        g_attn[0:192].reshape(3, 64, D).transpose(2, 0, 1)[None],
        jnp.concatenate([g_qkv_bias[:, 0:64], g_qkv_bias[:, 128:192]], axis=0)[None],
        g_attn[192:256][None],
        g_mlp[0:256].T[None],
        g_up_bias,
        g_mlp[256:512][None],
        sums[0:8][None],
    )


def solution(mesh):
    placed = (
        P("dp", "tensor", None),
        P("dp", "tensor", None),
        P(),
        P("section", None, None, "tensor"),
        P("section", None, "tensor"),
        P("section", "tensor", None),
        P("section", None, "tensor"),
        P("section", "tensor"),
        P("section", "tensor", None),
        P("section", None, None),
    )
    return jax.shard_map(
        body,
        mesh=mesh,
        in_specs=placed,
        out_specs=(
            P("section", "dp", "tensor", None),
            P("section", "dp", "tensor", None),
            P("section", None, None, "tensor"),
            P("section", None, "tensor"),
            P("section", "tensor", None),
            P("section", None, "tensor"),
            P("section", "tensor"),
            P("section", "tensor", None),
            P("section", None, None),
        ),
        check_vma=False,
    )
```

```python
import jax
import jax.numpy as jnp
from jax import lax
from jax.experimental import pallas as pl
from jax.experimental.pallas import tpu as pltpu
from jax.sharding import PartitionSpec as P

MESH = pl.DeviceIdType.MESH
F32 = jnp.float32
BF16 = jnp.bfloat16
EPSILON = 1e-06
D = 1024
MICRO = 2
LANE = 4
QUAD = 4
ROWS = 64
PAIRS = LANE // 2
TOKENS = LANE * ROWS
DP = 4
BIAS_ROW = 8
XORS = (1, 3, 2, 0)
OWN = 3
GATHERS = 4
SMALL, HEAD, REST, MLP = range(4)


def dot_nn(a, b):
    return lax.dot_general(a, b, (((1,), (0,)), ((), ())), preferred_element_type=F32)


def dot_nt(a, b):
    return lax.dot_general(a, b, (((1,), (1,)), ((), ())), preferred_element_type=F32)


def dot_tn(a, b):
    return lax.dot_general(a, b, (((0,), (0,)), ((), ())), preferred_element_type=F32)


def normalize(rows):
    center = rows - jnp.mean(rows, axis=-1, keepdims=True)
    inv = lax.rsqrt(jnp.mean(center * center, axis=-1, keepdims=True) + EPSILON)
    return center * inv, inv


def normalize_back(grad, unit, inv, gain):
    scaled = grad * gain
    return inv * (
        scaled
        - jnp.mean(scaled, axis=-1, keepdims=True)
        - unit * jnp.mean(scaled * unit, axis=-1, keepdims=True)
    )


def sum_rows(rows):
    return jnp.sum(rows, axis=0, keepdims=True)


def kernel(
    images, out_grad, live, qkv_in, out_in, up_in, down_in, qv_bias, up_bias_in, vectors_in,
    so_ref, ig_ref, g_in_ref, g_out_ref, g_up_ref, g_down_ref, g_qv_ref, g_bias_ref, g_vec_ref,
    small_w, attn_w, mlp_w,
    gathered, parts, landed,
    xs, units, invs, branches, hidden, cot,
    qkv_out, qkv_got, queries, keys, values, att_out, att_got, attended, probs,
    act, slope, d_pre, d_att_got, d_keys, d_values,
    grad_m, grad_a, core_m, core_a, dp_m, dp_a, part_m, part_a, recv_m, recv_a, full_m, full_a,
    vec, lane_vec, core_vec, x_vec, dp_vec, outs, outs_in,
    w_local, w_x_send, w_x_recv, w_dp_send, w_dp_recv, w_core_send, w_core_recv,
    ag_send, ag_recv, rs_send, rs_recv, quad_send, quad_recv,
    core_send, core_recv, dp_send, dp_recv, x_send, x_recv, full_send, full_recv,
    out_send, out_recv, lane_send, lane_recv, cv_send, cv_recv, xv_send, xv_recv,
    yv_send, yv_recv,
):
    section = lax.axis_index("section")
    group = lax.axis_index("dp")
    tensor = lax.axis_index("tensor")
    core = lax.rem(tensor, 2)
    lane = lax.rem(tensor // 2, LANE)
    high = tensor // (2 * LANE)
    other = 1 - core
    quad = high * 2 + core
    along_x = section * 2 + high

    def place(high_at, lane_at, core_at):
        return (high_at * LANE + lane_at) * 2 + core_at

    def to_lane(index):
        return {"tensor": place(high, index, core)}

    def to_quad(index):
        return {"tensor": place(index // 2, lane, lax.rem(index, 2))}

    def to_x(section_at, high_at):
        return {"section": section_at, "tensor": place(high_at, lane, core)}

    def to_dp(index):
        return {"dp": index}

    to_core = {"tensor": place(high, lane, other)}

    def next_of(own, step, count):
        return lax.rem(own + step, count)

    def remote(src, dst, send_sem, recv_sem, device):
        return pltpu.make_async_remote_copy(
            src_ref=src, dst_ref=dst, send_sem=send_sem, recv_sem=recv_sem,
            device_id=device, device_id_type=MESH,
        )

    def arrival(block, recv_sem):
        return remote(block, block, cv_send.at[0], recv_sem, to_core)

    own_attn = attn_w.at[section, quad]
    own_mlp = mlp_w.at[section, quad]
    landing = probs.at[1, :, pl.ds(0, 256)]
    loads = [
        pltpu.make_async_copy(origin, there, w_local.at[at]) for at, (origin, there) in enumerate((
            (qkv_in, own_attn.at[pl.ds(0, 192)]),
            (out_in, own_attn.at[pl.ds(192, 64)]),
            (up_in, landing),
            (down_in, own_mlp.at[pl.ds(256, 256)]),
        ))
    ]
    for load in loads:
        load.start()
    small_w[section, quad, 0:8] = vectors_in[...]
    gap = jnp.zeros((1, 64), F32)
    small_w[section, quad, 8:9] = jnp.concatenate(
        [qv_bias[0:1], gap, qv_bias[1:2], gap, up_bias_in[...], jnp.zeros((1, 512), F32)], axis=1)

    barrier = pltpu.get_barrier_semaphore()
    friends = [to_lane(next_of(lane, step, LANE)) for step in range(1, LANE)]
    friends += [to_quad(next_of(quad, step, QUAD)) for step in range(1, QUAD)]
    friends += [to_x(1 - section, high), to_x(1 - section, 1 - high)]
    friends += [to_dp(next_of(group, step, DP)) for step in range(1, DP)]
    for friend in friends:
        pl.semaphore_signal(barrier, inc=1, device_id=friend, device_id_type=MESH)
    pl.semaphore_wait(barrier, len(friends))

    def is_own(layer, source):
        return jnp.logical_and(layer == section, source == high)

    def piece(kind, layer, member):
        if kind == SMALL:
            return small_w.at[layer, member]
        if kind == MLP:
            return mlp_w.at[layer, member]
        return attn_w.at[layer, member, pl.ds((kind - HEAD) * 128, 128)]

    def by_quarters(kind, layer):
        return kind == MLP or (kind != SMALL and (layer == 1 or kind == HEAD))

    def quarter(kind, layer, member, index):
        if kind == MLP:
            return mlp_w.at[layer, member, pl.ds(pl.multiple_of(index * 128, 128), 128)]
        first = pl.multiple_of((kind - HEAD) * 128 + index * 32, 32)
        return attn_w.at[layer, member, pl.ds(first, 32)]

    def x_block(kind, layer, member):
        if by_quarters(kind, layer):
            return quarter(kind, layer, member, group)
        return piece(kind, layer, member)

    def x_piece(kind, layer, step):
        peer = next_of(along_x, step, 4)
        block = x_block(kind, layer, quad)
        return remote(block, block, w_x_send.at[kind, step], w_x_recv.at[kind, along_x],
                      to_x(peer // 2, lax.rem(peer, 2)))

    def dp_piece(kind, layer, source, step):
        block = quarter(kind, layer, source * 2 + core, group)
        return remote(block, block, w_dp_send.at[kind, layer * 2 + source, step],
                      w_dp_recv.at[kind, layer * 2 + source, group],
                      to_dp(next_of(group, step, DP)))

    def core_piece(kind, layer, source):
        block = piece(kind, layer, source * 2 + core)
        return remote(block, block, w_core_send.at[kind, layer * 2 + source],
                      w_core_recv.at[kind, layer * 2 + source], to_core)

    def send_pieces(kind, layer):
        @pl.when(section == layer)
        def _():
            for step in range(1, 4):
                x_piece(kind, layer, step).start()

    def spread_pieces(kind, layer):
        for source in range(2):
            @pl.when(jnp.logical_not(is_own(layer, source)))
            def _():
                arrival(x_block(kind, layer, source * 2 + core),
                        w_x_recv.at[kind, layer * 2 + source]).wait_recv()
                for step in range(1, DP):
                    dp_piece(kind, layer, source, step).start()

    def relay_pieces(kind, layer):
        for source in range(2):
            @pl.when(jnp.logical_not(is_own(layer, source)))
            def _():
                if by_quarters(kind, layer):
                    for step in range(1, DP):
                        sender = next_of(group, step, DP)
                        arrival(quarter(kind, layer, source * 2 + core, sender),
                                w_dp_recv.at[kind, layer * 2 + source, sender]).wait_recv()
                else:
                    arrival(x_block(kind, layer, source * 2 + core),
                            w_x_recv.at[kind, layer * 2 + source]).wait_recv()

            core_piece(kind, layer, source).start()

    def take_pieces(kind, layer):
        for source in range(2):
            arrival(piece(kind, layer, source * 2 + other),
                    w_core_recv.at[kind, layer * 2 + source]).wait_recv()

    def lane_of(slot):
        return jnp.bitwise_xor(lane, XORS[slot])

    def gather_copy(layer, which, slot):
        return remote(gathered.at[layer, which, OWN], gathered.at[layer, which, slot],
                      ag_send.at[slot], ag_recv.at[which, slot], to_lane(lane_of(slot)))

    def gather_start(layer, which, rows):
        gathered[layer, which, OWN] = rows
        for slot in range(OWN):
            gather_copy(layer, which, slot).start()

    def gather_finish(layer, which):
        for slot in range(OWN):
            gather_copy(layer, which, slot).wait_send()

    def gather_take(layer, which, step):
        for slot in (2 * step, 2 * step + 1):
            if slot != OWN:
                arrival(gathered.at[layer, which, slot], ag_recv.at[which, slot]).wait_recv()
        return gathered[layer, which, 2 * step:2 * step + 2].reshape(2 * ROWS, D)

    def whole(layer, which):
        return gathered[layer, which].reshape(TOKENS, D)

    def part_copy(which, slot):
        return remote(parts.at[which % 2, slot], landed.at[which % 2, slot],
                      rs_send.at[slot], rs_recv.at[which, slot], to_lane(lane_of(slot)))

    def part_start(which, step, rows):
        parts[which % 2, 2 * step:2 * step + 2] = rows.astype(BF16).reshape(2, ROWS, D)
        for slot in (2 * step, 2 * step + 1):
            if slot != OWN:
                part_copy(which, slot).start()

    def part_sum(which):
        total = parts[which % 2, OWN].astype(F32)
        for slot in range(OWN):
            arrival(landed.at[which % 2, slot], rs_recv.at[which, slot]).wait_recv()
            total = total + landed[which % 2, slot].astype(F32)
        for slot in range(OWN):
            part_copy(which, slot).wait_send()
        return total

    def each_pair(work):
        for step in range(PAIRS):
            work(step)

    def pair_rows(step):
        return slice(step * 2 * ROWS, (step + 1) * 2 * ROWS)

    d_att_out, d_mix_out, d_mix_got = att_out, qkv_out, qkv_got
    exchanges = ((qkv_out, qkv_got), (att_out, att_got), (d_att_out, d_att_got),
                 (d_mix_out, d_mix_got))

    def quad_copy(which, dest):
        origin, there = exchanges[which]
        return remote(origin.at[dest], there.at[quad], quad_send.at[which, dest],
                      quad_recv.at[which, quad], to_quad(dest))

    def half_copy(half, dest):
        return remote(qkv_out.at[dest, pair_rows(half)], qkv_got.at[quad, pair_rows(half)],
                      quad_send.at[4 * half, dest], quad_recv.at[4 * half, quad], to_quad(dest))

    def quad_start(which):
        origin, there = exchanges[which]
        for step in (2, 3, 1):
            quad_copy(which, jnp.bitwise_xor(quad, step)).start()
        there[quad] = origin[quad]

    def quad_take(which):
        there = exchanges[which][1]
        for step in (1, 2, 3):
            source = jnp.bitwise_xor(quad, step)
            arrival(there.at[source], quad_recv.at[which, source]).wait_recv()

    def quad_finish(which):
        for step in (1, 2, 3):
            quad_copy(which, jnp.bitwise_xor(quad, step)).wait_send()

    def token_rows(source, half=0, length=TOKENS):
        return pl.ds(pl.multiple_of(source * TOKENS + half * length, length), length)

    def vector(layer, row):
        return small_w[layer, quad, row:row + 1]

    def all_biases(layer, first):
        row = slice(BIAS_ROW, BIAS_ROW + 1)
        return jnp.concatenate(
            [small_w[layer, member, row, first:first + 256] for member in range(QUAD)], axis=-1)

    def keep_inv(layer, which, inv):
        invs[layer, which] = jnp.broadcast_to(inv, (ROWS, 128))

    def get_inv(layer, which):
        return invs[layer, which, :, 0:1]

    def attn_weights(layer):
        return attn_w[layer].reshape(QUAD * 256, D)

    def out_weights(layer):
        return attn_w[layer, :, 192:256].reshape(QUAD * 64, D)

    def up_weights(layer):
        return mlp_w[layer, :, 0:256].reshape(QUAD * 256, D)

    def down_weights(layer):
        return mlp_w[layer, :, 256:512].reshape(QUAD * 256, D)

    for layer in range(2):
        send_pieces(SMALL, layer)
    loads[0].wait()
    loads[1].wait()
    send_pieces(HEAD, 0)
    send_pieces(REST, 0)
    loads[2].wait()
    for part in range(4):
        mlp_w[section, quad, 0:256, part * 256:part * 256 + 256] = (
            probs[1, part * 256:part * 256 + 256, 0:256].astype(F32).T.astype(BF16))
    loads[3].wait()
    send_pieces(MLP, 0)
    xs[0] = images[section].astype(F32)
    vec[...] = jnp.zeros_like(vec)
    for layer in range(2):
        relay_pieces(SMALL, layer)

    @pl.loop(0, 2)
    def _(layer):
        unit, inv = normalize(xs[layer])
        units[layer, 0] = unit
        keep_inv(layer, 0, inv)
        gather_start(layer, 0, (unit * vector(layer, 0) + vector(layer, 1)).astype(BF16))

        @pl.when(layer == 0)
        def _():
            spread_pieces(HEAD, 0)
            relay_pieces(REST, 0)
            relay_pieces(HEAD, 0)
            for either in range(2):
                take_pieces(SMALL, either)

        take_pieces(REST, layer)
        take_pieces(HEAD, layer)
        qkv_bias = all_biases(layer, 0)

        def project(pair):
            rows = gather_take(layer, 0, pair)
            mixed = (dot_nt(rows, attn_weights(layer)) + qkv_bias).astype(BF16)
            for member in range(QUAD):
                qkv_out[member, pair_rows(pair)] = mixed[:, member * 256:member * 256 + 256]
            for step in (2, 3, 1):
                half_copy(pair, jnp.bitwise_xor(quad, step)).start()

        each_pair(project)
        qkv_got[quad] = qkv_out[quad]

        @pl.when(layer == 0)
        def _():
            for kind in (HEAD, REST, MLP):
                send_pieces(kind, 1)
            spread_pieces(MLP, 0)

        @pl.when(layer == 1)
        def _():
            relay_pieces(MLP, 1)

        for half in range(PAIRS):
            for step in (1, 2, 3):
                source = jnp.bitwise_xor(quad, step)
                arrival(qkv_got.at[source, pair_rows(half)],
                        quad_recv.at[4 * half, source]).wait_recv()
        for source in range(QUAD):
            block = qkv_got[source]
            queries[layer, token_rows(source)] = (block[:, 0:64].astype(F32) * 0.125).astype(BF16)
            keys[layer, token_rows(source)] = block[:, 64:128]
            values[layer, token_rows(source)] = block[:, 128:192]

        @pl.loop(0, QUAD)
        def _(step):
            source = lax.rem(quad + 1 + step, QUAD)
            for half in range(2):
                rows = token_rows(source, half, 128)
                scores = dot_nt(queries[layer, rows], keys[layer])
                grown = jnp.exp(scores - jnp.max(scores, axis=-1, keepdims=True))
                share = (grown / jnp.sum(grown, axis=-1, keepdims=True)).astype(BF16)
                probs[layer, rows] = share
                att_out[source, half * 128:half * 128 + 128] = dot_nn(
                    share, values[layer]).astype(BF16)

            @pl.when(source != quad)
            def _():
                quad_copy(1, source).start()

        att_got[quad] = att_out[quad]
        quad_take(1)
        attended[layer] = jnp.concatenate([att_got[member] for member in range(QUAD)], axis=-1)

        def project_out(pair):
            part_start(0, pair, dot_nn(attended[layer, pair_rows(pair)], out_weights(layer)))

        each_pair(project_out)
        for half in range(PAIRS):
            for step in (1, 2, 3):
                half_copy(half, jnp.bitwise_xor(quad, step)).wait_send()
        quad_finish(1)
        gather_finish(layer, 0)
        branch = part_sum(0) + vector(layer, 2)
        branches[layer, 0] = branch
        state = xs[layer] + vector(layer, 3) * branch
        hidden[...] = state

        unit, inv = normalize(state)
        units[layer, 1] = unit
        keep_inv(layer, 1, inv)
        gather_start(layer, 1, (unit * vector(layer, 4) + vector(layer, 5)).astype(BF16))

        @pl.when(layer == 0)
        def _():
            relay_pieces(MLP, 0)
            for kind in (HEAD, REST, MLP):
                spread_pieces(kind, 1)

        take_pieces(MLP, layer)
        up_bias = all_biases(layer, 256)

        def feed(pair):
            rows = gather_take(layer, 1, pair)
            pre = dot_nt(rows, up_weights(layer)) + up_bias
            cdf = 0.5 + 0.5 * lax.erf(pre * 0.7071067811865476)
            bell = jnp.exp(-0.5 * pre * pre) * 0.3989422804014327
            value = (pre * cdf).astype(BF16)
            act[layer, pair_rows(pair)] = value
            slope[layer, pair_rows(pair)] = (cdf + pre * bell).astype(BF16)
            part_start(1, pair, dot_nn(value, down_weights(layer)))

        each_pair(feed)

        @pl.when(layer == 0)
        def _():
            relay_pieces(HEAD, 1)
            relay_pieces(REST, 1)

        gather_finish(layer, 1)
        branch = part_sum(1) + vector(layer, 6)
        branches[layer, 1] = branch
        rounded = (hidden[...] + vector(layer, 7) * branch).astype(BF16)
        outs[0, layer] = rounded

        @pl.when(layer == 0)
        def _():
            xs[1] = rounded.astype(F32)

    def out_copy(which):
        return remote(outs.at[which, 1 - section], outs_in.at[which],
                      out_send.at[which], out_recv.at[which], to_x(1 - section, high))

    out_copy(0).start()

    grads = (grad_m, grad_a)
    from_core = (core_m, core_a)
    from_dp = (dp_m, dp_a)
    quarters = (part_m, part_a)
    from_x = (recv_m, recv_a)
    fulls = (full_m, full_a)
    lengths = (128, 64)

    def core_copy(kind):
        return remote(grads[kind].at[:, other], from_core[kind],
                      core_send.at[kind], core_recv.at[kind], to_core)

    def dp_rows(kind, index):
        length = lengths[kind]
        return pl.ds(pl.multiple_of(index * length, length), length)

    def dp_copy(kind, layer, step):
        dest = next_of(group, step, DP)
        return remote(grads[kind].at[:, core, dp_rows(kind, dest)],
                      from_dp[kind].at[layer, step - 1],
                      dp_send.at[kind, step], dp_recv.at[kind, layer, step], to_dp(dest))

    def x_copy(kind, layer, source):
        return remote(quarters[kind].at[layer, source], from_x[kind].at[along_x],
                      x_send.at[kind, layer * 2 + source], x_recv.at[kind, along_x],
                      to_x(layer, source))

    def core_done(kind, layer):
        core_copy(kind).wait()
        for source in range(2):
            grads[kind][source, core] = (
                grads[kind][source, core].astype(F32) + from_core[kind][source].astype(F32)
            ).astype(BF16)
        for step in range(1, DP):
            dp_copy(kind, layer, step).start()

    def dp_done(kind, layer):
        total = grads[kind][:, core, dp_rows(kind, group)].astype(F32)
        for step in range(1, DP):
            arrival(from_dp[kind].at[layer, step - 1],
                    dp_recv.at[kind, layer, step]).wait_recv()
            total = total + from_dp[kind][layer, step - 1].astype(F32)
        quarters[kind][layer] = total.astype(BF16)
        for source in range(2):
            @pl.when(jnp.logical_not(is_own(layer, source)))
            def _():
                x_copy(kind, layer, source).start()
        for step in range(1, DP):
            dp_copy(kind, layer, step).wait_send()

    def full_copy(kind, step):
        ref = fulls[kind]
        return remote(ref.at[group], ref.at[group], full_send.at[kind, step],
                      full_recv.at[kind, group], to_dp(next_of(group, step, DP)))

    def x_done(kind):
        total = quarters[kind][section, high].astype(F32)
        for step in range(1, 4):
            source = next_of(along_x, step, 4)
            arrival(from_x[kind].at[source], x_recv.at[kind, source]).wait_recv()
            total = total + from_x[kind][source].astype(F32)
        fulls[kind][group] = total.astype(BF16)
        for step in range(1, DP):
            full_copy(kind, step).start()

    mine = live[group * MICRO + section]
    everyone = live[section]
    for step in range(1, DP):
        everyone = everyone + live[step * MICRO + section]
    weight = jnp.where(mine > 0, 1.0 / jnp.full((1, D), everyone, jnp.int32).astype(F32), 0.0)
    cot[...] = out_grad[section].astype(F32) * weight

    @pl.loop(0, 2)
    def _(turn):
        layer = 1 - turn
        above = cot[...]
        d_branch2 = (above * vector(layer, 7)).astype(BF16)
        gather_start(layer, 2, d_branch2)
        vec[layer, 7:8] = sum_rows(above * branches[layer, 1])
        vec[layer, 6:7] = sum_rows(d_branch2.astype(F32))

        @pl.when(turn == 1)
        def _():
            core_done(1, 1)

        def feed_back(pair):
            rows = gather_take(layer, 2, pair)
            d_act = dot_nt(rows, down_weights(layer))
            back = (d_act * slope[layer, pair_rows(pair)].astype(F32)).astype(BF16)
            d_pre[pair_rows(pair)] = back
            vec[layer, 8:9] += sum_rows(back.astype(F32))
            part_start(2, pair, dot_nn(back, up_weights(layer)))

        each_pair(feed_back)
        gather_finish(layer, 2)
        for member in range(QUAD):
            units_of = slice(member * 256, member * 256 + 256)
            at = (member // 2, member % 2)
            grad_m[at[0], at[1], 0:256] = dot_tn(d_pre[:, units_of], whole(layer, 1)).astype(BF16)
            grad_m[at[0], at[1], 256:512] = dot_tn(
                act[layer, :, units_of], whole(layer, 2)).astype(BF16)
        core_copy(0).start()
        d_normed = part_sum(2)
        unit, inv = units[layer, 1], get_inv(layer, 1)
        vec[layer, 4:5] = sum_rows(d_normed * unit)
        vec[layer, 5:6] = sum_rows(d_normed)
        d_hidden = above + normalize_back(d_normed, unit, inv, vector(layer, 4))
        hidden[...] = d_hidden
        d_branch = (d_hidden * vector(layer, 3)).astype(BF16)
        gather_start(layer, 3, d_branch)
        vec[layer, 3:4] = sum_rows(d_hidden * branches[layer, 0])
        vec[layer, 2:3] = sum_rows(d_branch.astype(F32))
        core_done(0, layer)

        def out_back(pair):
            rows = gather_take(layer, 3, pair)
            d_out = dot_nt(rows, out_weights(layer)).astype(BF16)
            for member in range(QUAD):
                d_att_out[member, pair_rows(pair)] = d_out[:, member * 64:member * 64 + 64]

        each_pair(out_back)
        quad_start(2)
        gather_finish(layer, 3)

        @pl.when(turn == 1)
        def _():
            dp_done(1, 1)

        out_grads = dot_tn(attended[layer], whole(layer, 3)).astype(BF16)
        d_keys[...] = jnp.zeros_like(d_keys)
        d_values[...] = jnp.zeros_like(d_values)
        quad_take(2)

        @pl.loop(0, QUAD)
        def _(source):
            score_grads = []
            for half in range(2):
                rows = token_rows(source, half, 128)
                d_share = dot_nt(d_att_got[source, half * 128:half * 128 + 128], values[layer])
                wide = probs[layer, rows].astype(F32)
                product = wide * d_share
                d_score = (product - wide * jnp.sum(product, axis=-1, keepdims=True)).astype(BF16)
                score_grads.append(d_score)
                d_mix_out[source, half * 128:half * 128 + 128, 0:64] = (
                    dot_nn(d_score, keys[layer]) * 0.125).astype(BF16)
            d_keys[...] += dot_tn(jnp.concatenate(score_grads, 0),
                                  queries[layer, token_rows(source)])
            d_values[...] += dot_tn(probs[layer, token_rows(source)], d_att_got[source])

        for source in range(QUAD):
            d_mix_out[source, :, 64:128] = d_keys[token_rows(source)].astype(BF16)
            d_mix_out[source, :, 128:192] = d_values[token_rows(source)].astype(BF16)
            d_mix_out[source, :, 192:256] = jnp.zeros((TOKENS, 64), BF16)
        quad_start(3)
        for member in range(QUAD):
            grad_a[member // 2, member % 2, 192:256] = out_grads[member * 64:member * 64 + 64]
        quad_take(3)

        def project_back(pair):
            rows = jnp.concatenate(
                [d_mix_got[member, pair_rows(pair)] for member in range(QUAD)], axis=-1)
            vec[layer, 9:10] += sum_rows(rows.astype(F32))
            part_start(3, pair, dot_nn(rows, attn_weights(layer)))

        each_pair(project_back)
        for member in range(QUAD):
            grad_a[member // 2, member % 2, 0:192] = dot_tn(
                d_mix_got[member], whole(layer, 0))[0:192].astype(BF16)
        core_copy(1).start()
        quad_finish(2)
        quad_finish(3)
        dp_done(0, layer)
        d_normed = part_sum(3)
        unit, inv = units[layer, 0], get_inv(layer, 0)
        vec[layer, 0:1] = sum_rows(d_normed * unit)
        vec[layer, 1:2] = sum_rows(d_normed)
        rounded = (hidden[...] + normalize_back(d_normed, unit, inv, vector(layer, 0))).astype(BF16)
        outs[1, layer] = rounded
        cot[...] = rounded.astype(F32)

    core_done(1, 0)
    out_copy(1).start()
    x_done(0)

    def lane_copy(dest):
        return remote(vec.at[:, pl.ds(0, 8)], lane_vec.at[lane],
                      lane_send.at[dest], lane_recv.at[lane], to_lane(dest))

    for step in range(1, LANE):
        lane_copy(next_of(lane, step, LANE)).start()
    for step in range(1, LANE):
        source = next_of(lane, step, LANE)
        arrival(lane_vec.at[source], lane_recv.at[source]).wait_recv()
    for step in range(1, LANE):
        lane_copy(next_of(lane, step, LANE)).wait_send()
    for step in range(1, LANE):
        vec[:, 0:8] += lane_vec[next_of(lane, step, LANE)]
    cv_copy = remote(vec, core_vec, cv_send.at[0], cv_recv.at[0], to_core)
    cv_copy.start()
    cv_copy.wait()
    vec[...] += core_vec[...]

    def xv_copy(layer, source):
        return remote(vec.at[layer], x_vec.at[along_x], xv_send.at[layer * 2 + source],
                      xv_recv.at[along_x], to_x(layer, source))

    for layer in range(2):
        for source in range(2):
            @pl.when(jnp.logical_not(is_own(layer, source)))
            def _():
                xv_copy(layer, source).start()

    dp_done(1, 0)

    total = vec[section]
    for step in range(1, 4):
        source = next_of(along_x, step, 4)
        arrival(x_vec.at[source], xv_recv.at[source]).wait_recv()
        total = total + x_vec[source]
    dp_vec[group] = total

    def yv_copy(step):
        return remote(dp_vec.at[group], dp_vec.at[group], yv_send.at[step],
                      yv_recv.at[group], to_dp(next_of(group, step, DP)))

    for step in range(1, DP):
        yv_copy(step).start()
    x_done(1)

    for which, ref in ((0, so_ref), (1, ig_ref)):
        out_copy(which).wait()
        ref[section] = outs[which, section]
        ref[1 - section] = outs_in[which]

    for step in range(1, DP):
        source = next_of(group, step, DP)
        arrival(dp_vec.at[source], yv_recv.at[source]).wait_recv()
        total = total + dp_vec[source]
    for step in range(1, DP):
        yv_copy(step).wait_send()
    g_vec_ref[...] = total[0:8]
    dp_vec[group] = total
    bias_of = dp_vec[group, :, pl.ds(pl.multiple_of(quad * 256, 256), 256)]
    g_bias_ref[...] = bias_of[8:9]
    g_qv_ref[...] = jnp.concatenate([bias_of[9:10, 0:64], bias_of[9:10, 128:192]], axis=0)

    for kind in range(2):
        for step in range(1, DP):
            source = next_of(group, step, DP)
            arrival(fulls[kind].at[source], full_recv.at[kind, source]).wait_recv()
        if kind == 0:
            for part in range(4):
                g_up_ref[part * 256:part * 256 + 256] = full_m[
                    0:2, :, part * 256:part * 256 + 256].reshape(256, 256).astype(F32).T.astype(BF16)
            g_down_ref[...] = full_m[2:4].reshape(256, D)
        else:
            g_in_ref[...] = full_a[0:3].reshape(192, D)
            g_out_ref[...] = full_a[3]

    for layer in range(2):
        @pl.when(section == layer)
        def _():
            for kind in range(4):
                for step in range(1, 4):
                    x_piece(kind, layer, step).wait_send()

        for source in range(2):
            for kind in range(4):
                core_piece(kind, layer, source).wait_send()

            @pl.when(jnp.logical_not(is_own(layer, source)))
            def _():
                for kind in (HEAD, REST, MLP):
                    if by_quarters(kind, layer):
                        for step in range(1, DP):
                            dp_piece(kind, layer, source, step).wait_send()
                for kind in range(2):
                    x_copy(kind, layer, source).wait_send()
                xv_copy(layer, source).wait_send()
    for step in range(1, DP):
        for kind in range(2):
            full_copy(kind, step).wait_send()


def run_layers(*operands):
    vmem = pl.BlockSpec(memory_space=pltpu.VMEM)
    anywhere = pl.BlockSpec(memory_space=pl.ANY)
    dma = pltpu.SemaphoreType.DMA
    every = QUAD * TOKENS
    scratch = [
        pltpu.VMEM((2, QUAD, 16, D), F32),
        pltpu.VMEM((2, QUAD, 256, D), BF16),
        pltpu.VMEM((2, QUAD, 512, D), BF16),
        pltpu.VMEM((2, GATHERS, LANE, ROWS, D), BF16),
        pltpu.VMEM((2, LANE, ROWS, D), BF16),
        pltpu.VMEM((2, LANE, ROWS, D), BF16),
        pltpu.VMEM((2, ROWS, D), F32),
        pltpu.VMEM((2, 2, ROWS, D), F32),
        pltpu.VMEM((2, 2, ROWS, 128), F32),
        pltpu.VMEM((2, 2, ROWS, D), F32),
        pltpu.VMEM((ROWS, D), F32),
        pltpu.VMEM((ROWS, D), F32),
        pltpu.VMEM((QUAD, TOKENS, 256), BF16),
        pltpu.VMEM((QUAD, TOKENS, 256), BF16),
        pltpu.VMEM((2, every, 64), BF16),
        pltpu.VMEM((2, every, 64), BF16),
        pltpu.VMEM((2, every, 64), BF16),
        pltpu.VMEM((QUAD, TOKENS, 64), BF16),
        pltpu.VMEM((QUAD, TOKENS, 64), BF16),
        pltpu.VMEM((2, TOKENS, 256), BF16),
        pltpu.VMEM((2, every, every), BF16),
        pltpu.VMEM((2, TOKENS, 1024), BF16),
        pltpu.VMEM((2, TOKENS, 1024), BF16),
        pltpu.VMEM((TOKENS, 1024), BF16),
        pltpu.VMEM((QUAD, TOKENS, 64), BF16),
        pltpu.VMEM((every, 64), F32),
        pltpu.VMEM((every, 64), F32),
        pltpu.VMEM((2, 2, 512, D), BF16),
        pltpu.VMEM((2, 2, 256, D), BF16),
        pltpu.VMEM((2, 512, D), BF16),
        pltpu.VMEM((2, 256, D), BF16),
        pltpu.VMEM((2, DP - 1, 2, 128, D), BF16),
        pltpu.VMEM((2, DP - 1, 2, 64, D), BF16),
        pltpu.VMEM((2, 2, 128, D), BF16),
        pltpu.VMEM((2, 2, 64, D), BF16),
        pltpu.VMEM((4, 128, D), BF16),
        pltpu.VMEM((4, 64, D), BF16),
        pltpu.VMEM((DP, 128, D), BF16),
        pltpu.VMEM((DP, 64, D), BF16),
        pltpu.VMEM((2, 16, D), F32),
        pltpu.VMEM((LANE, 2, 8, D), F32),
        pltpu.VMEM((2, 16, D), F32),
        pltpu.VMEM((4, 16, D), F32),
        pltpu.VMEM((DP, 16, D), F32),
        pltpu.VMEM((2, 2, ROWS, D), BF16),
        pltpu.VMEM((2, ROWS, D), BF16),
        dma((4,)), dma((4, 4)), dma((4, 4)),
        dma((4, 4, DP)), dma((4, 4, DP)), dma((4, 4)), dma((4, 4)),
        dma((LANE,)), dma((GATHERS, LANE)),
        dma((LANE,)), dma((GATHERS, LANE)),
        dma((5, QUAD)), dma((5, QUAD)),
        dma((2,)), dma((2,)),
        dma((2, DP)), dma((2, 2, DP)),
        dma((2, 4)), dma((2, 4)),
        dma((2, DP)), dma((2, DP)),
        dma((2,)), dma((2,)),
        dma((LANE,)), dma((LANE,)),
        dma((1,)), dma((1,)),
        dma((4,)), dma((4,)),
        dma((DP,)), dma((DP,)),
    ]
    return pl.pallas_call(
        kernel,
        out_shape=(
            jax.ShapeDtypeStruct((2, ROWS, D), BF16),
            jax.ShapeDtypeStruct((2, ROWS, D), BF16),
            jax.ShapeDtypeStruct((192, D), BF16),
            jax.ShapeDtypeStruct((64, D), BF16),
            jax.ShapeDtypeStruct((D, 256), BF16),
            jax.ShapeDtypeStruct((256, D), BF16),
            jax.ShapeDtypeStruct((2, 64), F32),
            jax.ShapeDtypeStruct((1, 256), F32),
            jax.ShapeDtypeStruct((8, D), F32),
        ),
        in_specs=[vmem, vmem, pl.BlockSpec(memory_space=pltpu.SMEM)] + [anywhere] * 4 + [vmem] * 3,
        out_specs=(vmem,) * 9,
        scratch_shapes=scratch,
        name="two_layers",
        compiler_params=pltpu.CompilerParams(
            collective_id=0, has_side_effects=True, vmem_limit_bytes=63 * 2**20
        ),
    )(*operands)


def body(
    images, out_grad, live_images, attn_in, qv_bias, attn_out, mlp_in, mlp_bias, mlp_out, vectors
):
    section_out, section_in_grad, g_in, g_out, g_up, g_down, g_qv, g_bias, g_vec = run_layers(
        images, out_grad, live_images, attn_in[0].transpose(1, 2, 0).reshape(192, D),
        attn_out[0], mlp_in[0], mlp_out[0], qv_bias[0], mlp_bias, vectors[0])
    return (
        section_out[None],
        section_in_grad[None],
        g_in.astype(F32).reshape(3, 64, D).transpose(2, 0, 1)[None],
        g_qv[None],
        g_out.astype(F32)[None],
        g_up.astype(F32)[None],
        g_bias,
        g_down.astype(F32)[None],
        g_vec[None],
    )


def solution(mesh):
    placed = (
        P("dp", "tensor", None),
        P("dp", "tensor", None),
        P(),
        P("section", None, None, "tensor"),
        P("section", None, "tensor"),
        P("section", "tensor", None),
        P("section", None, "tensor"),
        P("section", "tensor"),
        P("section", "tensor", None),
        P("section", None, None),
    )
    return jax.shard_map(
        body,
        mesh=mesh,
        in_specs=placed,
        out_specs=(
            P("section", "dp", "tensor", None),
            P("section", "dp", "tensor", None),
            P("section", None, None, "tensor"),
            P("section", None, "tensor"),
            P("section", "tensor", None),
            P("section", None, "tensor"),
            P("section", "tensor"),
            P("section", "tensor", None),
            P("section", None, None),
        ),
        check_vma=False,
    )
```

```python
import jax
import jax.numpy as jnp
from jax import lax
from jax.experimental import pallas as pl
from jax.experimental.pallas import tpu as pltpu
from jax.sharding import PartitionSpec as P

MESH = pl.DeviceIdType.MESH
F32 = jnp.float32
BF16 = jnp.bfloat16
EPSILON = 1e-06
D = 1024
MICRO = 2
LANE = 4
QUAD = 4
ROWS = 64
PAIRS = LANE // 2
TOKENS = LANE * ROWS
DP = 4
BIAS_ROW = 8
XORS = (1, 3, 2, 0)
OWN = 3
GATHERS = 4
SMALL, HEAD, REST, MLP = range(4)


def dot_nn(a, b):
    return lax.dot_general(a, b, (((1,), (0,)), ((), ())), preferred_element_type=F32)


def dot_nt(a, b):
    return lax.dot_general(a, b, (((1,), (1,)), ((), ())), preferred_element_type=F32)


def dot_tn(a, b):
    return lax.dot_general(a, b, (((0,), (0,)), ((), ())), preferred_element_type=F32)


def normalize(rows):
    center = rows - jnp.mean(rows, axis=-1, keepdims=True)
    inv = lax.rsqrt(jnp.mean(center * center, axis=-1, keepdims=True) + EPSILON)
    return center * inv, inv


def normalize_back(grad, unit, inv, gain):
    scaled = grad * gain
    return inv * (
        scaled
        - jnp.mean(scaled, axis=-1, keepdims=True)
        - unit * jnp.mean(scaled * unit, axis=-1, keepdims=True)
    )


def sum_rows(rows):
    return jnp.sum(rows, axis=0, keepdims=True)


def kernel(
    images, out_grad, live, qkv_in, out_in, up_in, down_in, qv_bias, up_bias_in, vectors_in,
    so_ref, ig_ref, g_in_ref, g_out_ref, g_up_ref, g_down_ref, g_qv_ref, g_bias_ref, g_vec_ref,
    small_w, attn_w, mlp_w,
    gathered, parts, landed,
    xs, units, invs, branches, hidden, cot,
    qkv_out, qkv_got, queries, keys, values, att_out, att_got, attended, probs,
    act, slope, d_pre, d_mixed, d_att_got, d_keys, d_values,
    grad_m, grad_a, core_m, core_a, dp_m, dp_a, part_m, part_a, recv_m, recv_a, full_m, full_a,
    vec, lane_vec, core_vec, x_vec, dp_vec, outs, outs_in,
    w_local, w_x_send, w_x_recv, w_dp_send, w_dp_recv, w_core_send, w_core_recv,
    ag_send, ag_recv, rs_send, rs_recv, quad_send, quad_recv,
    core_send, core_recv, dp_send, dp_recv, x_send, x_recv, full_send, full_recv,
    out_send, out_recv, lane_send, lane_recv, cv_send, cv_recv, xv_send, xv_recv,
    yv_send, yv_recv,
):
    section = lax.axis_index("section")
    group = lax.axis_index("dp")
    tensor = lax.axis_index("tensor")
    core = lax.rem(tensor, 2)
    lane = lax.rem(tensor // 2, LANE)
    high = tensor // (2 * LANE)
    other = 1 - core
    quad = high * 2 + core
    along_x = section * 2 + high

    def place(high_at, lane_at, core_at):
        return (high_at * LANE + lane_at) * 2 + core_at

    def to_lane(index):
        return {"tensor": place(high, index, core)}

    def to_quad(index):
        return {"tensor": place(index // 2, lane, lax.rem(index, 2))}

    def to_x(section_at, high_at):
        return {"section": section_at, "tensor": place(high_at, lane, core)}

    def to_dp(index):
        return {"dp": index}

    to_core = {"tensor": place(high, lane, other)}

    def next_of(own, step, count):
        return lax.rem(own + step, count)

    def remote(src, dst, send_sem, recv_sem, device):
        return pltpu.make_async_remote_copy(
            src_ref=src, dst_ref=dst, send_sem=send_sem, recv_sem=recv_sem,
            device_id=device, device_id_type=MESH,
        )

    def arrival(block, recv_sem):
        return remote(block, block, cv_send.at[0], recv_sem, to_core)

    own_attn = attn_w.at[section, quad]
    own_mlp = mlp_w.at[section, quad]
    landing = probs.at[1, :, pl.ds(0, 256)]
    loads = [
        pltpu.make_async_copy(origin, there, w_local.at[at]) for at, (origin, there) in enumerate((
            (qkv_in, own_attn.at[pl.ds(0, 192)]),
            (out_in, own_attn.at[pl.ds(192, 64)]),
            (up_in, landing),
            (down_in, own_mlp.at[pl.ds(256, 256)]),
        ))
    ]
    for load in loads:
        load.start()
    small_w[section, quad, 0:8] = vectors_in[...]
    gap = jnp.zeros((1, 64), F32)
    small_w[section, quad, 8:9] = jnp.concatenate(
        [qv_bias[0:1], gap, qv_bias[1:2], gap, up_bias_in[...], jnp.zeros((1, 512), F32)], axis=1)

    barrier = pltpu.get_barrier_semaphore()
    friends = [to_lane(next_of(lane, step, LANE)) for step in range(1, LANE)]
    friends += [to_quad(next_of(quad, step, QUAD)) for step in range(1, QUAD)]
    friends += [to_x(1 - section, high), to_x(1 - section, 1 - high)]
    friends += [to_dp(next_of(group, step, DP)) for step in range(1, DP)]
    for friend in friends:
        pl.semaphore_signal(barrier, inc=1, device_id=friend, device_id_type=MESH)
    pl.semaphore_wait(barrier, len(friends))

    def is_own(layer, source):
        return jnp.logical_and(layer == section, source == high)

    def piece(kind, layer, member):
        if kind == SMALL:
            return small_w.at[layer, member]
        if kind == MLP:
            return mlp_w.at[layer, member]
        return attn_w.at[layer, member, pl.ds((kind - HEAD) * 128, 128)]

    def by_quarters(kind, layer):
        return kind == MLP or (kind != SMALL and (layer == 1 or kind == HEAD))

    def quarter(kind, layer, member, index):
        if kind == MLP:
            return mlp_w.at[layer, member, pl.ds(pl.multiple_of(index * 128, 128), 128)]
        first = pl.multiple_of((kind - HEAD) * 128 + index * 32, 32)
        return attn_w.at[layer, member, pl.ds(first, 32)]

    def x_block(kind, layer, member):
        if by_quarters(kind, layer):
            return quarter(kind, layer, member, group)
        return piece(kind, layer, member)

    def x_piece(kind, layer, step):
        peer = next_of(along_x, step, 4)
        block = x_block(kind, layer, quad)
        return remote(block, block, w_x_send.at[kind, step], w_x_recv.at[kind, along_x],
                      to_x(peer // 2, lax.rem(peer, 2)))

    def dp_piece(kind, layer, source, step):
        block = quarter(kind, layer, source * 2 + core, group)
        return remote(block, block, w_dp_send.at[kind, layer * 2 + source, step],
                      w_dp_recv.at[kind, layer * 2 + source, group],
                      to_dp(next_of(group, step, DP)))

    def core_piece(kind, layer, source):
        block = piece(kind, layer, source * 2 + core)
        return remote(block, block, w_core_send.at[kind, layer * 2 + source],
                      w_core_recv.at[kind, layer * 2 + source], to_core)

    def send_pieces(kind, layer):
        @pl.when(section == layer)
        def _():
            for step in range(1, 4):
                x_piece(kind, layer, step).start()

    def spread_pieces(kind, layer):
        for source in range(2):
            @pl.when(jnp.logical_not(is_own(layer, source)))
            def _():
                arrival(x_block(kind, layer, source * 2 + core),
                        w_x_recv.at[kind, layer * 2 + source]).wait_recv()
                for step in range(1, DP):
                    dp_piece(kind, layer, source, step).start()

    def relay_pieces(kind, layer):
        for source in range(2):
            @pl.when(jnp.logical_not(is_own(layer, source)))
            def _():
                if by_quarters(kind, layer):
                    for step in range(1, DP):
                        sender = next_of(group, step, DP)
                        arrival(quarter(kind, layer, source * 2 + core, sender),
                                w_dp_recv.at[kind, layer * 2 + source, sender]).wait_recv()
                else:
                    arrival(x_block(kind, layer, source * 2 + core),
                            w_x_recv.at[kind, layer * 2 + source]).wait_recv()

            core_piece(kind, layer, source).start()

    def take_pieces(kind, layer):
        for source in range(2):
            arrival(piece(kind, layer, source * 2 + other),
                    w_core_recv.at[kind, layer * 2 + source]).wait_recv()

    def lane_of(slot):
        return jnp.bitwise_xor(lane, XORS[slot])

    def gather_copy(layer, which, slot):
        return remote(gathered.at[layer, which, OWN], gathered.at[layer, which, slot],
                      ag_send.at[slot], ag_recv.at[which, slot], to_lane(lane_of(slot)))

    def gather_start(layer, which, rows):
        gathered[layer, which, OWN] = rows
        for slot in range(OWN):
            gather_copy(layer, which, slot).start()

    def gather_finish(layer, which):
        for slot in range(OWN):
            gather_copy(layer, which, slot).wait_send()

    def gather_take(layer, which, step):
        for slot in (2 * step, 2 * step + 1):
            if slot != OWN:
                arrival(gathered.at[layer, which, slot], ag_recv.at[which, slot]).wait_recv()
        return gathered[layer, which, 2 * step:2 * step + 2].reshape(2 * ROWS, D)

    def whole(layer, which):
        return gathered[layer, which].reshape(TOKENS, D)

    def part_copy(which, slot):
        return remote(parts.at[which % 2, slot], landed.at[which % 2, slot],
                      rs_send.at[slot], rs_recv.at[which, slot], to_lane(lane_of(slot)))

    def part_start(which, step, rows):
        parts[which % 2, 2 * step:2 * step + 2] = rows.astype(BF16).reshape(2, ROWS, D)
        for slot in (2 * step, 2 * step + 1):
            if slot != OWN:
                part_copy(which, slot).start()

    def part_sum(which):
        total = parts[which % 2, OWN].astype(F32)
        for slot in range(OWN):
            arrival(landed.at[which % 2, slot], rs_recv.at[which, slot]).wait_recv()
            total = total + landed[which % 2, slot].astype(F32)
        for slot in range(OWN):
            part_copy(which, slot).wait_send()
        return total

    def each_pair(work):
        for step in range(PAIRS):
            work(step)

    def pair_rows(step):
        return slice(step * 2 * ROWS, (step + 1) * 2 * ROWS)

    d_att_out, d_mix_out, d_mix_got = att_out, qkv_out, qkv_got
    exchanges = ((qkv_out, qkv_got), (att_out, att_got), (d_att_out, d_att_got),
                 (d_mix_out, d_mix_got))

    def quad_copy(which, dest):
        origin, there = exchanges[which]
        return remote(origin.at[dest], there.at[quad], quad_send.at[which, dest],
                      quad_recv.at[which, quad], to_quad(dest))

    def pack_rows(member, half, query_key, value):
        qkv_out[member, half, 0:128] = query_key
        qkv_out[member, half, 128:192] = jnp.concatenate([value[0:64], value[64:128]], axis=-1)

    def unpack_values(source, half):
        block = qkv_got[source, half, 128:192]
        return jnp.concatenate([block[:, 0:64], block[:, 64:128]], axis=0)

    def unpack_halves(block):
        return jnp.concatenate([block[:, 0:64], block[:, 64:128]], axis=0)

    def half_copy(half, dest):
        return remote(qkv_out.at[dest, half], qkv_got.at[quad, half],
                      quad_send.at[4 * half, dest], quad_recv.at[4 * half, quad], to_quad(dest))

    def quad_start(which):
        origin, there = exchanges[which]
        for step in (2, 3, 1):
            quad_copy(which, jnp.bitwise_xor(quad, step)).start()
        there[quad] = origin[quad]

    def quad_take(which):
        there = exchanges[which][1]
        for step in (1, 2, 3):
            source = jnp.bitwise_xor(quad, step)
            arrival(there.at[source], quad_recv.at[which, source]).wait_recv()

    def quad_finish(which):
        for step in (1, 2, 3):
            quad_copy(which, jnp.bitwise_xor(quad, step)).wait_send()

    def token_rows(source, half=0, length=TOKENS):
        return pl.ds(pl.multiple_of(source * TOKENS + half * length, length), length)

    def vector(layer, row):
        return small_w[layer, quad, row:row + 1]

    def all_biases(layer, first):
        row = slice(BIAS_ROW, BIAS_ROW + 1)
        return jnp.concatenate(
            [small_w[layer, member, row, first:first + 256] for member in range(QUAD)], axis=-1)

    def keep_inv(layer, which, inv):
        invs[layer, which] = jnp.broadcast_to(inv, (ROWS, 128))

    def get_inv(layer, which):
        return invs[layer, which, :, 0:1]

    def attn_weights(layer):
        return attn_w[layer].reshape(QUAD * 256, D)

    def out_weights(layer):
        return attn_w[layer, :, 192:256].reshape(QUAD * 64, D)

    def up_weights(layer):
        return mlp_w[layer, :, 0:256].reshape(QUAD * 256, D)

    def down_weights(layer):
        return mlp_w[layer, :, 256:512].reshape(QUAD * 256, D)

    for layer in range(2):
        send_pieces(SMALL, layer)
    loads[0].wait()
    loads[1].wait()
    send_pieces(HEAD, 0)
    send_pieces(REST, 0)
    loads[2].wait()
    for part in range(4):
        mlp_w[section, quad, 0:256, part * 256:part * 256 + 256] = (
            probs[1, part * 256:part * 256 + 256, 0:256].astype(F32).T.astype(BF16))
    loads[3].wait()
    send_pieces(MLP, 0)
    xs[0] = images[section].astype(F32)
    vec[...] = jnp.zeros_like(vec)
    for layer in range(2):
        relay_pieces(SMALL, layer)

    @pl.loop(0, 2)
    def _(layer):
        unit, inv = normalize(xs[layer])
        units[layer, 0] = unit
        keep_inv(layer, 0, inv)
        gather_start(layer, 0, (unit * vector(layer, 0) + vector(layer, 1)).astype(BF16))

        @pl.when(layer == 0)
        def _():
            spread_pieces(HEAD, 0)
            relay_pieces(REST, 0)
            relay_pieces(HEAD, 0)
            for either in range(2):
                take_pieces(SMALL, either)

        take_pieces(REST, layer)
        take_pieces(HEAD, layer)
        qkv_bias = all_biases(layer, 0)

        def project(pair):
            rows = gather_take(layer, 0, pair)
            mixed = (dot_nt(rows, attn_weights(layer)) + qkv_bias).astype(BF16)
            for member in range(QUAD):
                first = member * 256
                pack_rows(member, pair, mixed[:, first:first + 128],
                          mixed[:, first + 128:first + 192])
            for step in (2, 3, 1):
                half_copy(pair, jnp.bitwise_xor(quad, step)).start()

        each_pair(project)
        qkv_got[quad] = qkv_out[quad]

        @pl.when(layer == 0)
        def _():
            for kind in (HEAD, REST, MLP):
                send_pieces(kind, 1)
            spread_pieces(MLP, 0)

        @pl.when(layer == 1)
        def _():
            relay_pieces(MLP, 1)

        for half in range(PAIRS):
            for step in (1, 2, 3):
                source = jnp.bitwise_xor(quad, step)
                arrival(qkv_got.at[source, half],
                        quad_recv.at[4 * half, source]).wait_recv()
        for source in range(QUAD):
            for half in range(PAIRS):
                rows = token_rows(source, half, 128)
                block = qkv_got[source, half, 0:128]
                queries[layer, rows] = (block[:, 0:64].astype(F32) * 0.125).astype(BF16)
                keys[layer, rows] = block[:, 64:128]
                values[layer, rows] = unpack_values(source, half)

        @pl.loop(0, QUAD)
        def _(step):
            source = lax.rem(quad + 1 + step, QUAD)
            found = []
            for half in range(2):
                rows = token_rows(source, half, 128)
                scores = dot_nt(queries[layer, rows], keys[layer])
                grown = jnp.exp(scores - jnp.max(scores, axis=-1, keepdims=True))
                share = (grown / jnp.sum(grown, axis=-1, keepdims=True)).astype(BF16)
                probs[layer, rows] = share
                found.append(dot_nn(share, values[layer]).astype(BF16))
            att_out[source] = jnp.concatenate(found, axis=-1)

            @pl.when(source != quad)
            def _():
                quad_copy(1, source).start()

        att_got[quad] = att_out[quad]
        quad_take(1)
        attended[layer] = jnp.concatenate(
            [unpack_halves(att_got[member]) for member in range(QUAD)], axis=-1)

        def project_out(pair):
            part_start(0, pair, dot_nn(attended[layer, pair_rows(pair)], out_weights(layer)))

        each_pair(project_out)
        for half in range(PAIRS):
            for step in (1, 2, 3):
                half_copy(half, jnp.bitwise_xor(quad, step)).wait_send()
        quad_finish(1)
        gather_finish(layer, 0)
        branch = part_sum(0) + vector(layer, 2)
        branches[layer, 0] = branch
        state = xs[layer] + vector(layer, 3) * branch
        hidden[...] = state

        unit, inv = normalize(state)
        units[layer, 1] = unit
        keep_inv(layer, 1, inv)
        gather_start(layer, 1, (unit * vector(layer, 4) + vector(layer, 5)).astype(BF16))

        @pl.when(layer == 0)
        def _():
            relay_pieces(MLP, 0)
            for kind in (HEAD, REST, MLP):
                spread_pieces(kind, 1)

        take_pieces(MLP, layer)
        up_bias = all_biases(layer, 256)

        def feed(pair):
            rows = gather_take(layer, 1, pair)
            pre = dot_nt(rows, up_weights(layer)) + up_bias
            cdf = 0.5 + 0.5 * lax.erf(pre * 0.7071067811865476)
            bell = jnp.exp(-0.5 * pre * pre) * 0.3989422804014327
            value = (pre * cdf).astype(BF16)
            act[layer, pair_rows(pair)] = value
            slope[layer, pair_rows(pair)] = (cdf + pre * bell).astype(BF16)
            part_start(1, pair, dot_nn(value, down_weights(layer)))

        each_pair(feed)

        @pl.when(layer == 0)
        def _():
            relay_pieces(HEAD, 1)
            relay_pieces(REST, 1)

        gather_finish(layer, 1)
        branch = part_sum(1) + vector(layer, 6)
        branches[layer, 1] = branch
        rounded = (hidden[...] + vector(layer, 7) * branch).astype(BF16)
        outs[0, layer] = rounded

        @pl.when(layer == 0)
        def _():
            xs[1] = rounded.astype(F32)

    def out_copy(which):
        return remote(outs.at[which, 1 - section], outs_in.at[which],
                      out_send.at[which], out_recv.at[which], to_x(1 - section, high))

    out_copy(0).start()

    grads = (grad_m, grad_a)
    from_core = (core_m, core_a)
    from_dp = (dp_m, dp_a)
    quarters = (part_m, part_a)
    from_x = (recv_m, recv_a)
    fulls = (full_m, full_a)
    lengths = (128, 64)

    def core_copy(kind):
        return remote(grads[kind].at[:, other], from_core[kind],
                      core_send.at[kind], core_recv.at[kind], to_core)

    def dp_rows(kind, index):
        length = lengths[kind]
        return pl.ds(pl.multiple_of(index * length, length), length)

    def dp_copy(kind, layer, step):
        dest = next_of(group, step, DP)
        return remote(grads[kind].at[:, core, dp_rows(kind, dest)],
                      from_dp[kind].at[layer, step - 1],
                      dp_send.at[kind, step], dp_recv.at[kind, layer, step], to_dp(dest))

    def x_copy(kind, layer, source):
        return remote(quarters[kind].at[layer, source], from_x[kind].at[along_x],
                      x_send.at[kind, layer * 2 + source], x_recv.at[kind, along_x],
                      to_x(layer, source))

    def core_done(kind, layer):
        core_copy(kind).wait()
        for source in range(2):
            grads[kind][source, core] = (
                grads[kind][source, core].astype(F32) + from_core[kind][source].astype(F32)
            ).astype(BF16)
        for step in range(1, DP):
            dp_copy(kind, layer, step).start()

    def dp_done(kind, layer):
        total = grads[kind][:, core, dp_rows(kind, group)].astype(F32)
        for step in range(1, DP):
            arrival(from_dp[kind].at[layer, step - 1],
                    dp_recv.at[kind, layer, step]).wait_recv()
            total = total + from_dp[kind][layer, step - 1].astype(F32)
        quarters[kind][layer] = total.astype(BF16)
        for source in range(2):
            @pl.when(jnp.logical_not(is_own(layer, source)))
            def _():
                x_copy(kind, layer, source).start()
        for step in range(1, DP):
            dp_copy(kind, layer, step).wait_send()

    def full_copy(kind, step):
        ref = fulls[kind]
        return remote(ref.at[group], ref.at[group], full_send.at[kind, step],
                      full_recv.at[kind, group], to_dp(next_of(group, step, DP)))

    def x_done(kind):
        total = quarters[kind][section, high].astype(F32)
        for step in range(1, 4):
            source = next_of(along_x, step, 4)
            arrival(from_x[kind].at[source], x_recv.at[kind, source]).wait_recv()
            total = total + from_x[kind][source].astype(F32)
        fulls[kind][group] = total.astype(BF16)
        for step in range(1, DP):
            full_copy(kind, step).start()

    mine = live[group * MICRO + section]
    everyone = live[section]
    for step in range(1, DP):
        everyone = everyone + live[step * MICRO + section]
    weight = jnp.where(mine > 0, 1.0 / jnp.full((1, D), everyone, jnp.int32).astype(F32), 0.0)
    cot[...] = out_grad[section].astype(F32) * weight

    @pl.loop(0, 2)
    def _(turn):
        layer = 1 - turn
        above = cot[...]
        d_branch2 = (above * vector(layer, 7)).astype(BF16)
        gather_start(layer, 2, d_branch2)
        vec[layer, 7:8] = sum_rows(above * branches[layer, 1])
        vec[layer, 6:7] = sum_rows(d_branch2.astype(F32))

        def feed_back(pair):
            rows = gather_take(layer, 2, pair)
            d_act = dot_nt(rows, down_weights(layer))
            back = (d_act * slope[layer, pair_rows(pair)].astype(F32)).astype(BF16)
            d_pre[pair_rows(pair)] = back
            vec[layer, 8:9] += sum_rows(back.astype(F32))
            part_start(2, pair, dot_nn(back, up_weights(layer)))

        each_pair(feed_back)
        gather_finish(layer, 2)
        for member in range(QUAD):
            units_of = slice(member * 256, member * 256 + 256)
            at = (member // 2, member % 2)
            grad_m[at[0], at[1], 0:256] = dot_tn(d_pre[:, units_of], whole(layer, 1)).astype(BF16)
            grad_m[at[0], at[1], 256:512] = dot_tn(
                act[layer, :, units_of], whole(layer, 2)).astype(BF16)
        core_copy(0).start()
        d_normed = part_sum(2)
        unit, inv = units[layer, 1], get_inv(layer, 1)
        vec[layer, 4:5] = sum_rows(d_normed * unit)
        vec[layer, 5:6] = sum_rows(d_normed)
        d_hidden = above + normalize_back(d_normed, unit, inv, vector(layer, 4))
        hidden[...] = d_hidden
        d_branch = (d_hidden * vector(layer, 3)).astype(BF16)
        gather_start(layer, 3, d_branch)
        vec[layer, 3:4] = sum_rows(d_hidden * branches[layer, 0])
        vec[layer, 2:3] = sum_rows(d_branch.astype(F32))
        core_done(0, layer)

        d_outs = []

        def out_back(pair):
            rows = gather_take(layer, 3, pair)
            d_outs.append(dot_nt(rows, out_weights(layer)).astype(BF16))

        each_pair(out_back)
        for member in range(QUAD):
            d_att_out[member] = jnp.concatenate(
                [half[:, member * 64:member * 64 + 64] for half in d_outs], axis=-1)
        quad_start(2)
        gather_finish(layer, 3)

        @pl.when(turn == 1)
        def _():
            dp_done(1, 1)

        out_grads = dot_tn(attended[layer], whole(layer, 3)).astype(BF16)
        d_keys[...] = jnp.zeros_like(d_keys)
        d_values[...] = jnp.zeros_like(d_values)
        quad_take(2)

        @pl.loop(0, QUAD)
        def _(source):
            d_rows = unpack_halves(d_att_got[source])
            score_grads = []
            for half in range(2):
                rows = token_rows(source, half, 128)
                d_share = dot_nt(d_rows[half * 128:half * 128 + 128], values[layer])
                wide = probs[layer, rows].astype(F32)
                product = wide * d_share
                d_score = (product - wide * jnp.sum(product, axis=-1, keepdims=True)).astype(BF16)
                score_grads.append(d_score)
                d_mix_out[source, half, 0:128, 0:64] = (
                    dot_nn(d_score, keys[layer]) * 0.125).astype(BF16)
            d_keys[...] += dot_tn(jnp.concatenate(score_grads, 0),
                                  queries[layer, token_rows(source)])
            d_values[...] += dot_tn(probs[layer, token_rows(source)], d_rows)

        for source in range(QUAD):
            for half in range(PAIRS):
                rows = token_rows(source, half, 128)
                d_mix_out[source, half, 0:128, 64:128] = d_keys[rows].astype(BF16)
                value = d_values[rows].astype(BF16)
                d_mix_out[source, half, 128:192] = jnp.concatenate(
                    [value[0:64], value[64:128]], axis=-1)
        quad_start(3)
        for member in range(QUAD):
            grad_a[member // 2, member % 2, 192:256] = out_grads[member * 64:member * 64 + 64]
        quad_take(3)

        none = jnp.zeros((2 * ROWS, 64), BF16)

        def project_back(pair):
            for member in range(QUAD):
                first = member * 256
                d_mixed[pair_rows(pair), first:first + 128] = d_mix_got[member, pair, 0:128]
                d_mixed[pair_rows(pair), first + 128:first + 256] = jnp.concatenate(
                    [unpack_values(member, pair), none], axis=-1)
            rows = d_mixed[pair_rows(pair)]
            vec[layer, 9:10] += sum_rows(rows.astype(F32))
            part_start(3, pair, dot_nn(rows, attn_weights(layer)))

        each_pair(project_back)
        for member in range(QUAD):
            grad_a[member // 2, member % 2, 0:192] = dot_tn(
                d_mixed[:, member * 256:member * 256 + 256], whole(layer, 0))[0:192].astype(BF16)
        core_copy(1).start()
        quad_finish(2)
        quad_finish(3)
        dp_done(0, layer)
        core_done(1, layer)
        d_normed = part_sum(3)
        unit, inv = units[layer, 0], get_inv(layer, 0)
        vec[layer, 0:1] = sum_rows(d_normed * unit)
        vec[layer, 1:2] = sum_rows(d_normed)
        rounded = (hidden[...] + normalize_back(d_normed, unit, inv, vector(layer, 0))).astype(BF16)
        outs[1, layer] = rounded
        cot[...] = rounded.astype(F32)

    out_copy(1).start()
    x_done(0)

    def lane_copy(dest):
        return remote(vec.at[:, pl.ds(0, 8)], lane_vec.at[lane],
                      lane_send.at[dest], lane_recv.at[lane], to_lane(dest))

    for step in range(1, LANE):
        lane_copy(next_of(lane, step, LANE)).start()
    for step in range(1, LANE):
        source = next_of(lane, step, LANE)
        arrival(lane_vec.at[source], lane_recv.at[source]).wait_recv()
    for step in range(1, LANE):
        lane_copy(next_of(lane, step, LANE)).wait_send()
    for step in range(1, LANE):
        vec[:, 0:8] += lane_vec[next_of(lane, step, LANE)]
    cv_copy = remote(vec, core_vec, cv_send.at[0], cv_recv.at[0], to_core)
    cv_copy.start()
    cv_copy.wait()
    vec[...] += core_vec[...]

    def xv_copy(layer, source):
        return remote(vec.at[layer], x_vec.at[along_x], xv_send.at[layer * 2 + source],
                      xv_recv.at[along_x], to_x(layer, source))

    for layer in range(2):
        for source in range(2):
            @pl.when(jnp.logical_not(is_own(layer, source)))
            def _():
                xv_copy(layer, source).start()

    dp_done(1, 0)

    total = vec[section]
    for step in range(1, 4):
        source = next_of(along_x, step, 4)
        arrival(x_vec.at[source], xv_recv.at[source]).wait_recv()
        total = total + x_vec[source]
    dp_vec[group] = total

    def yv_copy(step):
        return remote(dp_vec.at[group], dp_vec.at[group], yv_send.at[step],
                      yv_recv.at[group], to_dp(next_of(group, step, DP)))

    for step in range(1, DP):
        yv_copy(step).start()
    x_done(1)

    for which, ref in ((0, so_ref), (1, ig_ref)):
        out_copy(which).wait()
        ref[section] = outs[which, section]
        ref[1 - section] = outs_in[which]

    for step in range(1, DP):
        source = next_of(group, step, DP)
        arrival(dp_vec.at[source], yv_recv.at[source]).wait_recv()
        total = total + dp_vec[source]
    for step in range(1, DP):
        yv_copy(step).wait_send()
    g_vec_ref[...] = total[0:8]
    dp_vec[group] = total
    bias_of = dp_vec[group, :, pl.ds(pl.multiple_of(quad * 256, 256), 256)]
    g_bias_ref[...] = bias_of[8:9]
    g_qv_ref[...] = jnp.concatenate([bias_of[9:10, 0:64], bias_of[9:10, 128:192]], axis=0)

    for kind in range(2):
        for step in range(1, DP):
            source = next_of(group, step, DP)
            arrival(fulls[kind].at[source], full_recv.at[kind, source]).wait_recv()
        if kind == 0:
            for part in range(4):
                g_up_ref[part * 256:part * 256 + 256] = full_m[
                    0:2, :, part * 256:part * 256 + 256].reshape(256, 256).astype(F32).T.astype(BF16)
            g_down_ref[...] = full_m[2:4].reshape(256, D)
        else:
            g_in_ref[...] = full_a[0:3].reshape(192, D)
            g_out_ref[...] = full_a[3]

    for layer in range(2):
        @pl.when(section == layer)
        def _():
            for kind in range(4):
                for step in range(1, 4):
                    x_piece(kind, layer, step).wait_send()

        for source in range(2):
            for kind in range(4):
                core_piece(kind, layer, source).wait_send()

            @pl.when(jnp.logical_not(is_own(layer, source)))
            def _():
                for kind in (HEAD, REST, MLP):
                    if by_quarters(kind, layer):
                        for step in range(1, DP):
                            dp_piece(kind, layer, source, step).wait_send()
                for kind in range(2):
                    x_copy(kind, layer, source).wait_send()
                xv_copy(layer, source).wait_send()
    for step in range(1, DP):
        for kind in range(2):
            full_copy(kind, step).wait_send()


def run_layers(*operands):
    vmem = pl.BlockSpec(memory_space=pltpu.VMEM)
    anywhere = pl.BlockSpec(memory_space=pl.ANY)
    dma = pltpu.SemaphoreType.DMA
    every = QUAD * TOKENS
    scratch = [
        pltpu.VMEM((2, QUAD, 16, D), F32),
        pltpu.VMEM((2, QUAD, 256, D), BF16),
        pltpu.VMEM((2, QUAD, 512, D), BF16),
        pltpu.VMEM((2, GATHERS, LANE, ROWS, D), BF16),
        pltpu.VMEM((2, LANE, ROWS, D), BF16),
        pltpu.VMEM((2, LANE, ROWS, D), BF16),
        pltpu.VMEM((2, ROWS, D), F32),
        pltpu.VMEM((2, 2, ROWS, D), F32),
        pltpu.VMEM((2, 2, ROWS, 128), F32),
        pltpu.VMEM((2, 2, ROWS, D), F32),
        pltpu.VMEM((ROWS, D), F32),
        pltpu.VMEM((ROWS, D), F32),
        pltpu.VMEM((QUAD, PAIRS, 192, 128), BF16),
        pltpu.VMEM((QUAD, PAIRS, 192, 128), BF16),
        pltpu.VMEM((2, every, 64), BF16),
        pltpu.VMEM((2, every, 64), BF16),
        pltpu.VMEM((2, every, 64), BF16),
        pltpu.VMEM((QUAD, 128, 128), BF16),
        pltpu.VMEM((QUAD, 128, 128), BF16),
        pltpu.VMEM((2, TOKENS, 256), BF16),
        pltpu.VMEM((2, every, every), BF16),
        pltpu.VMEM((2, TOKENS, 1024), BF16),
        pltpu.VMEM((2, TOKENS, 1024), BF16),
        pltpu.VMEM((TOKENS, 1024), BF16),
        pltpu.VMEM((TOKENS, 1024), BF16),
        pltpu.VMEM((QUAD, 128, 128), BF16),
        pltpu.VMEM((every, 64), F32),
        pltpu.VMEM((every, 64), F32),
        pltpu.VMEM((2, 2, 512, D), BF16),
        pltpu.VMEM((2, 2, 256, D), BF16),
        pltpu.VMEM((2, 512, D), BF16),
        pltpu.VMEM((2, 256, D), BF16),
        pltpu.VMEM((2, DP - 1, 2, 128, D), BF16),
        pltpu.VMEM((2, DP - 1, 2, 64, D), BF16),
        pltpu.VMEM((2, 2, 128, D), BF16),
        pltpu.VMEM((2, 2, 64, D), BF16),
        pltpu.VMEM((4, 128, D), BF16),
        pltpu.VMEM((4, 64, D), BF16),
        pltpu.VMEM((DP, 128, D), BF16),
        pltpu.VMEM((DP, 64, D), BF16),
        pltpu.VMEM((2, 16, D), F32),
        pltpu.VMEM((LANE, 2, 8, D), F32),
        pltpu.VMEM((2, 16, D), F32),
        pltpu.VMEM((4, 16, D), F32),
        pltpu.VMEM((DP, 16, D), F32),
        pltpu.VMEM((2, 2, ROWS, D), BF16),
        pltpu.VMEM((2, ROWS, D), BF16),
        dma((4,)), dma((4, 4)), dma((4, 4)),
        dma((4, 4, DP)), dma((4, 4, DP)), dma((4, 4)), dma((4, 4)),
        dma((LANE,)), dma((GATHERS, LANE)),
        dma((LANE,)), dma((GATHERS, LANE)),
        dma((5, QUAD)), dma((5, QUAD)),
        dma((2,)), dma((2,)),
        dma((2, DP)), dma((2, 2, DP)),
        dma((2, 4)), dma((2, 4)),
        dma((2, DP)), dma((2, DP)),
        dma((2,)), dma((2,)),
        dma((LANE,)), dma((LANE,)),
        dma((1,)), dma((1,)),
        dma((4,)), dma((4,)),
        dma((DP,)), dma((DP,)),
    ]
    return pl.pallas_call(
        kernel,
        out_shape=(
            jax.ShapeDtypeStruct((2, ROWS, D), BF16),
            jax.ShapeDtypeStruct((2, ROWS, D), BF16),
            jax.ShapeDtypeStruct((192, D), BF16),
            jax.ShapeDtypeStruct((64, D), BF16),
            jax.ShapeDtypeStruct((D, 256), BF16),
            jax.ShapeDtypeStruct((256, D), BF16),
            jax.ShapeDtypeStruct((2, 64), F32),
            jax.ShapeDtypeStruct((1, 256), F32),
            jax.ShapeDtypeStruct((8, D), F32),
        ),
        in_specs=[vmem, vmem, pl.BlockSpec(memory_space=pltpu.SMEM)] + [anywhere] * 4 + [vmem] * 3,
        out_specs=(vmem,) * 9,
        scratch_shapes=scratch,
        name="two_layers",
        compiler_params=pltpu.CompilerParams(
            collective_id=0, has_side_effects=True, vmem_limit_bytes=63 * 2**20
        ),
    )(*operands)


def body(
    images, out_grad, live_images, attn_in, qv_bias, attn_out, mlp_in, mlp_bias, mlp_out, vectors
):
    section_out, section_in_grad, g_in, g_out, g_up, g_down, g_qv, g_bias, g_vec = run_layers(
        images, out_grad, live_images, attn_in[0].transpose(1, 2, 0).reshape(192, D),
        attn_out[0], mlp_in[0], mlp_out[0], qv_bias[0], mlp_bias, vectors[0])
    return (
        section_out[None],
        section_in_grad[None],
        g_in.astype(F32).reshape(3, 64, D).transpose(2, 0, 1)[None],
        g_qv[None],
        g_out.astype(F32)[None],
        g_up.astype(F32)[None],
        g_bias,
        g_down.astype(F32)[None],
        g_vec[None],
    )


def solution(mesh):
    placed = (
        P("dp", "tensor", None),
        P("dp", "tensor", None),
        P(),
        P("section", None, None, "tensor"),
        P("section", None, "tensor"),
        P("section", "tensor", None),
        P("section", None, "tensor"),
        P("section", "tensor"),
        P("section", "tensor", None),
        P("section", None, None),
    )
    return jax.shard_map(
        body,
        mesh=mesh,
        in_specs=placed,
        out_specs=(
            P("section", "dp", "tensor", None),
            P("section", "dp", "tensor", None),
            P("section", None, None, "tensor"),
            P("section", None, "tensor"),
            P("section", "tensor", None),
            P("section", None, "tensor"),
            P("section", "tensor"),
            P("section", "tensor", None),
            P("section", None, None),
        ),
        check_vma=False,
    )
```

```python
import jax
import jax.numpy as jnp
from jax import lax
from jax.experimental import pallas as pl
from jax.experimental.pallas import tpu as pltpu
from jax.sharding import PartitionSpec as P

MESH = pl.DeviceIdType.MESH
F32 = jnp.float32
BF16 = jnp.bfloat16
EPSILON = 1e-06
D = 1024
MICRO = 2
LANE = 4
QUAD = 4
ROWS = 64
HALVES = 2
HALF = ROWS // HALVES
TOKENS = LANE * ROWS
DP = 4
BIAS_ROW = 8
XORS = (1, 3, 2, 0)
OWN = 3
GATHERS = 4
SMALL, HEAD, REST, MLP = range(4)


def dot_nn(a, b):
    return lax.dot_general(a, b, (((1,), (0,)), ((), ())), preferred_element_type=F32)


def dot_nt(a, b):
    return lax.dot_general(a, b, (((1,), (1,)), ((), ())), preferred_element_type=F32)


def dot_tn(a, b):
    return lax.dot_general(a, b, (((0,), (0,)), ((), ())), preferred_element_type=F32)


def normalize(rows):
    center = rows - jnp.mean(rows, axis=-1, keepdims=True)
    inv = lax.rsqrt(jnp.mean(center * center, axis=-1, keepdims=True) + EPSILON)
    return center * inv, inv


def normalize_back(grad, unit, inv, gain):
    scaled = grad * gain
    return inv * (
        scaled
        - jnp.mean(scaled, axis=-1, keepdims=True)
        - unit * jnp.mean(scaled * unit, axis=-1, keepdims=True)
    )


def sum_rows(rows):
    return jnp.sum(rows, axis=0, keepdims=True)


def kernel(
    images, out_grad, live, qkv_in, out_in, up_in, down_in, qv_bias, up_bias_in, vectors_in,
    so_ref, ig_ref, g_in_ref, g_out_ref, g_up_ref, g_down_ref, g_qv_ref, g_bias_ref, g_vec_ref,
    small_w, attn_w, mlp_w,
    gathered, parts, landed,
    xs, units, invs, branches, hidden, cot,
    qkv_out, qkv_got, queries, keys, values, att_out, att_got, attended, probs,
    act, slope, d_pre, d_mixed, d_att_got, d_keys, d_values,
    grad_m, grad_a, core_m, core_a, dp_m, dp_a, part_m, part_a, recv_m, recv_a, full_m, full_a,
    vec, lane_vec, core_vec, x_vec, dp_vec, outs, outs_in,
    w_local, w_x_send, w_x_recv, w_dp_send, w_dp_recv, w_core_send, w_core_recv,
    ag_send, ag_recv, rs_send, rs_recv, quad_send, quad_recv,
    core_send, core_recv, dp_send, dp_recv, x_send, x_recv, full_send, full_recv,
    out_send, out_recv, lane_send, lane_recv, cv_send, cv_recv, xv_send, xv_recv,
    yv_send, yv_recv,
):
    section = lax.axis_index("section")
    group = lax.axis_index("dp")
    tensor = lax.axis_index("tensor")
    core = lax.rem(tensor, 2)
    lane = lax.rem(tensor // 2, LANE)
    high = tensor // (2 * LANE)
    other = 1 - core
    quad = high * 2 + core
    along_x = section * 2 + high

    def place(high_at, lane_at, core_at):
        return (high_at * LANE + lane_at) * 2 + core_at

    def to_lane(index):
        return {"tensor": place(high, index, core)}

    def to_quad(index):
        return {"tensor": place(index // 2, lane, lax.rem(index, 2))}

    def to_x(section_at, high_at):
        return {"section": section_at, "tensor": place(high_at, lane, core)}

    def to_dp(index):
        return {"dp": index}

    to_core = {"tensor": place(high, lane, other)}

    def next_of(own, step, count):
        return lax.rem(own + step, count)

    def remote(src, dst, send_sem, recv_sem, device):
        return pltpu.make_async_remote_copy(
            src_ref=src, dst_ref=dst, send_sem=send_sem, recv_sem=recv_sem,
            device_id=device, device_id_type=MESH,
        )

    def arrival(block, recv_sem):
        return remote(block, block, cv_send.at[0], recv_sem, to_core)

    own_attn = attn_w.at[section, quad]
    own_mlp = mlp_w.at[section, quad]
    landing = probs.at[1, :, pl.ds(0, 256)]
    loads = [
        pltpu.make_async_copy(origin, there, w_local.at[at]) for at, (origin, there) in enumerate((
            (qkv_in, own_attn.at[pl.ds(0, 192)]),
            (out_in, own_attn.at[pl.ds(192, 64)]),
            (up_in, landing),
            (down_in, own_mlp.at[pl.ds(256, 256)]),
        ))
    ]
    for load in loads:
        load.start()
    small_w[section, quad, 0:8] = vectors_in[...]
    gap = jnp.zeros((1, 64), F32)
    small_w[section, quad, 8:9] = jnp.concatenate(
        [qv_bias[0:1], gap, qv_bias[1:2], gap, up_bias_in[...], jnp.zeros((1, 512), F32)], axis=1)

    barrier = pltpu.get_barrier_semaphore()
    friends = [to_lane(next_of(lane, step, LANE)) for step in range(1, LANE)]
    friends += [to_quad(next_of(quad, step, QUAD)) for step in range(1, QUAD)]
    friends += [to_x(1 - section, high), to_x(1 - section, 1 - high)]
    friends += [to_dp(next_of(group, step, DP)) for step in range(1, DP)]
    for friend in friends:
        pl.semaphore_signal(barrier, inc=1, device_id=friend, device_id_type=MESH)
    pl.semaphore_wait(barrier, len(friends))

    def is_own(layer, source):
        return jnp.logical_and(layer == section, source == high)

    def piece(kind, layer, member):
        if kind == SMALL:
            return small_w.at[layer, member]
        if kind == MLP:
            return mlp_w.at[layer, member]
        return attn_w.at[layer, member, pl.ds((kind - HEAD) * 128, 128)]

    def by_quarters(kind, layer):
        return kind == MLP or (kind != SMALL and (layer == 1 or kind == HEAD))

    def quarter(kind, layer, member, index):
        if kind == MLP:
            return mlp_w.at[layer, member, pl.ds(pl.multiple_of(index * 128, 128), 128)]
        first = pl.multiple_of((kind - HEAD) * 128 + index * 32, 32)
        return attn_w.at[layer, member, pl.ds(first, 32)]

    def x_block(kind, layer, member):
        if by_quarters(kind, layer):
            return quarter(kind, layer, member, group)
        return piece(kind, layer, member)

    def x_piece(kind, layer, step):
        peer = next_of(along_x, step, 4)
        block = x_block(kind, layer, quad)
        return remote(block, block, w_x_send.at[kind, step], w_x_recv.at[kind, along_x],
                      to_x(peer // 2, lax.rem(peer, 2)))

    def dp_piece(kind, layer, source, step):
        block = quarter(kind, layer, source * 2 + core, group)
        return remote(block, block, w_dp_send.at[kind, layer * 2 + source, step],
                      w_dp_recv.at[kind, layer * 2 + source, group],
                      to_dp(next_of(group, step, DP)))

    def core_piece(kind, layer, source):
        block = piece(kind, layer, source * 2 + core)
        return remote(block, block, w_core_send.at[kind, layer * 2 + source],
                      w_core_recv.at[kind, layer * 2 + source], to_core)

    def send_pieces(kind, layer):
        @pl.when(section == layer)
        def _():
            for step in range(1, 4):
                x_piece(kind, layer, step).start()

    def spread_pieces(kind, layer):
        for source in range(2):
            @pl.when(jnp.logical_not(is_own(layer, source)))
            def _():
                arrival(x_block(kind, layer, source * 2 + core),
                        w_x_recv.at[kind, layer * 2 + source]).wait_recv()
                for step in range(1, DP):
                    dp_piece(kind, layer, source, step).start()

    def relay_pieces(kind, layer):
        for source in range(2):
            @pl.when(jnp.logical_not(is_own(layer, source)))
            def _():
                if by_quarters(kind, layer):
                    for step in range(1, DP):
                        sender = next_of(group, step, DP)
                        arrival(quarter(kind, layer, source * 2 + core, sender),
                                w_dp_recv.at[kind, layer * 2 + source, sender]).wait_recv()
                else:
                    arrival(x_block(kind, layer, source * 2 + core),
                            w_x_recv.at[kind, layer * 2 + source]).wait_recv()

            core_piece(kind, layer, source).start()

    def take_pieces(kind, layer):
        for source in range(2):
            arrival(piece(kind, layer, source * 2 + other),
                    w_core_recv.at[kind, layer * 2 + source]).wait_recv()

    def lane_of(slot):
        return jnp.bitwise_xor(lane, XORS[slot])

    def gather_copy(layer, which, half, slot):
        at = half * LANE + slot
        return remote(gathered.at[layer, which, half, OWN], gathered.at[layer, which, half, slot],
                      ag_send.at[which, at], ag_recv.at[which, at], to_lane(lane_of(slot)))

    def gather_start(layer, which, half, rows):
        gathered[layer, which, half, OWN] = rows
        for slot in range(OWN):
            gather_copy(layer, which, half, slot).start()

    def gather_finish(layer, which):
        for half in range(HALVES):
            for slot in range(OWN):
                gather_copy(layer, which, half, slot).wait_send()

    def gather_take(layer, which, half):
        for slot in range(OWN):
            arrival(gathered.at[layer, which, half, slot],
                    ag_recv.at[which, half * LANE + slot]).wait_recv()
        return gathered[layer, which, half].reshape(LANE * HALF, D)

    def whole(layer, which):
        return gathered[layer, which].reshape(TOKENS, D)

    def part_copy(which, half, slot):
        at = half * LANE + slot
        return remote(parts.at[which % 2, half, slot], landed.at[which % 2, half, slot],
                      rs_send.at[at], rs_recv.at[which, at], to_lane(lane_of(slot)))

    def part_start(which, half, rows):
        parts[which % 2, half] = rows.astype(BF16).reshape(LANE, HALF, D)
        for slot in range(OWN):
            part_copy(which, half, slot).start()

    def part_sum(which, half):
        total = parts[which % 2, half, OWN].astype(F32)
        for slot in range(OWN):
            arrival(landed.at[which % 2, half, slot],
                    rs_recv.at[which, half * LANE + slot]).wait_recv()
            total = total + landed[which % 2, half, slot].astype(F32)
        for slot in range(OWN):
            part_copy(which, half, slot).wait_send()
        return total

    def own_rows(half):
        return slice(half * HALF, (half + 1) * HALF)

    def each_half(work):
        for half in range(HALVES):
            work(half)

    def half_rows(half):
        return slice(half * LANE * HALF, (half + 1) * LANE * HALF)

    d_att_out, d_mix_out, d_mix_got = att_out, qkv_out, qkv_got
    exchanges = ((qkv_out, qkv_got), (att_out, att_got), (d_att_out, d_att_got),
                 (d_mix_out, d_mix_got))

    def quad_copy(which, dest):
        origin, there = exchanges[which]
        return remote(origin.at[dest], there.at[quad], quad_send.at[which, dest],
                      quad_recv.at[which, quad], to_quad(dest))

    def pack_rows(member, half, query_key, value):
        qkv_out[member, half, 0:128] = query_key
        qkv_out[member, half, 128:192] = jnp.concatenate([value[0:64], value[64:128]], axis=-1)

    def unpack_values(source, half):
        block = qkv_got[source, half, 128:192]
        return jnp.concatenate([block[:, 0:64], block[:, 64:128]], axis=0)

    def unpack_halves(block):
        return jnp.concatenate([block[:, 0:64], block[:, 64:128]], axis=0)

    def half_copy(half, dest):
        return remote(qkv_out.at[dest, half], qkv_got.at[quad, half],
                      quad_send.at[4 * half, dest], quad_recv.at[4 * half, quad], to_quad(dest))

    def quad_start(which):
        origin, there = exchanges[which]
        for step in (2, 3, 1):
            quad_copy(which, jnp.bitwise_xor(quad, step)).start()
        there[quad] = origin[quad]

    def quad_take(which):
        there = exchanges[which][1]
        for step in (1, 2, 3):
            source = jnp.bitwise_xor(quad, step)
            arrival(there.at[source], quad_recv.at[which, source]).wait_recv()

    def quad_finish(which):
        for step in (1, 2, 3):
            quad_copy(which, jnp.bitwise_xor(quad, step)).wait_send()

    def token_rows(source, half=0, length=TOKENS):
        return pl.ds(pl.multiple_of(source * TOKENS + half * length, length), length)

    def vector(layer, row):
        return small_w[layer, quad, row:row + 1]

    def all_biases(layer, first):
        row = slice(BIAS_ROW, BIAS_ROW + 1)
        return jnp.concatenate(
            [small_w[layer, member, row, first:first + 256] for member in range(QUAD)], axis=-1)

    def keep_inv(layer, which, half, inv):
        invs[layer, which, own_rows(half)] = jnp.broadcast_to(inv, (HALF, 128))

    def get_inv(layer, which, half):
        return invs[layer, which, own_rows(half), 0:1]

    def norm_start(layer, which, half, rows):
        unit, inv = normalize(rows)
        units[layer, which, own_rows(half)] = unit
        keep_inv(layer, which, half, inv)
        gain, offset = vector(layer, which * 4), vector(layer, which * 4 + 1)
        gather_start(layer, which, half, (unit * gain + offset).astype(BF16))

    def attn_weights(layer):
        return attn_w[layer].reshape(QUAD * 256, D)

    def out_weights(layer):
        return attn_w[layer, :, 192:256].reshape(QUAD * 64, D)

    def up_weights(layer):
        return mlp_w[layer, :, 0:256].reshape(QUAD * 256, D)

    def down_weights(layer):
        return mlp_w[layer, :, 256:512].reshape(QUAD * 256, D)

    for layer in range(2):
        send_pieces(SMALL, layer)
    loads[0].wait()
    loads[1].wait()
    send_pieces(HEAD, 0)
    send_pieces(REST, 0)
    loads[2].wait()
    for part in range(4):
        mlp_w[section, quad, 0:256, part * 256:part * 256 + 256] = (
            probs[1, part * 256:part * 256 + 256, 0:256].astype(F32).T.astype(BF16))
    loads[3].wait()
    send_pieces(MLP, 0)
    xs[0] = images[section].astype(F32)
    vec[...] = jnp.zeros_like(vec)
    for layer in range(2):
        relay_pieces(SMALL, layer)

    for half in range(HALVES):
        norm_start(0, 0, half, xs[0, own_rows(half)])

    @pl.loop(0, 2)
    def _(layer):
        @pl.when(layer == 0)
        def _():
            spread_pieces(HEAD, 0)
            relay_pieces(REST, 0)
            relay_pieces(HEAD, 0)
            for either in range(2):
                take_pieces(SMALL, either)

        take_pieces(REST, layer)
        take_pieces(HEAD, layer)
        qkv_bias = all_biases(layer, 0)

        def project(pair):
            rows = gather_take(layer, 0, pair)
            mixed = (dot_nt(rows, attn_weights(layer)) + qkv_bias).astype(BF16)
            for member in range(QUAD):
                first = member * 256
                pack_rows(member, pair, mixed[:, first:first + 128],
                          mixed[:, first + 128:first + 192])
            for step in (2, 3, 1):
                half_copy(pair, jnp.bitwise_xor(quad, step)).start()

        each_half(project)
        qkv_got[quad] = qkv_out[quad]

        @pl.when(layer == 0)
        def _():
            for kind in (HEAD, REST, MLP):
                send_pieces(kind, 1)
            spread_pieces(MLP, 0)

        @pl.when(layer == 1)
        def _():
            relay_pieces(MLP, 1)

        for half in range(HALVES):
            for step in (1, 2, 3):
                source = jnp.bitwise_xor(quad, step)
                arrival(qkv_got.at[source, half],
                        quad_recv.at[4 * half, source]).wait_recv()
        for source in range(QUAD):
            for half in range(HALVES):
                rows = token_rows(source, half, 128)
                block = qkv_got[source, half, 0:128]
                queries[layer, rows] = (block[:, 0:64].astype(F32) * 0.125).astype(BF16)
                keys[layer, rows] = block[:, 64:128]
                values[layer, rows] = unpack_values(source, half)

        @pl.loop(0, QUAD)
        def _(step):
            source = lax.rem(quad + 1 + step, QUAD)
            found = []
            for half in range(2):
                rows = token_rows(source, half, 128)
                scores = dot_nt(queries[layer, rows], keys[layer])
                grown = jnp.exp(scores - jnp.max(scores, axis=-1, keepdims=True))
                share = (grown / jnp.sum(grown, axis=-1, keepdims=True)).astype(BF16)
                probs[layer, rows] = share
                found.append(dot_nn(share, values[layer]).astype(BF16))
            att_out[source] = jnp.concatenate(found, axis=-1)

            @pl.when(source != quad)
            def _():
                quad_copy(1, source).start()

        att_got[quad] = att_out[quad]
        quad_take(1)
        attended[layer] = jnp.concatenate(
            [unpack_halves(att_got[member]) for member in range(QUAD)], axis=-1)

        def project_out(pair):
            part_start(0, pair, dot_nn(attended[layer, half_rows(pair)], out_weights(layer)))

        each_half(project_out)
        for half in range(HALVES):
            for step in (1, 2, 3):
                half_copy(half, jnp.bitwise_xor(quad, step)).wait_send()
        quad_finish(1)
        gather_finish(layer, 0)
        for half in range(HALVES):
            branch = part_sum(0, half) + vector(layer, 2)
            branches[layer, 0, own_rows(half)] = branch
            state = xs[layer, own_rows(half)] + vector(layer, 3) * branch
            hidden[own_rows(half)] = state
            norm_start(layer, 1, half, state)

        @pl.when(layer == 0)
        def _():
            relay_pieces(MLP, 0)
            for kind in (HEAD, REST, MLP):
                spread_pieces(kind, 1)

        take_pieces(MLP, layer)
        up_bias = all_biases(layer, 256)

        def feed(pair):
            rows = gather_take(layer, 1, pair)
            pre = dot_nt(rows, up_weights(layer)) + up_bias
            cdf = 0.5 + 0.5 * lax.erf(pre * 0.7071067811865476)
            bell = jnp.exp(-0.5 * pre * pre) * 0.3989422804014327
            value = (pre * cdf).astype(BF16)
            act[layer, half_rows(pair)] = value
            slope[layer, half_rows(pair)] = (cdf + pre * bell).astype(BF16)
            part_start(1, pair, dot_nn(value, down_weights(layer)))

        each_half(feed)

        @pl.when(layer == 0)
        def _():
            relay_pieces(HEAD, 1)
            relay_pieces(REST, 1)

        gather_finish(layer, 1)
        for half in range(HALVES):
            branch = part_sum(1, half) + vector(layer, 6)
            branches[layer, 1, own_rows(half)] = branch
            rounded = (hidden[own_rows(half)] + vector(layer, 7) * branch).astype(BF16)
            outs[0, layer, own_rows(half)] = rounded

            @pl.when(layer == 0)
            def _():
                xs[1, own_rows(half)] = rounded.astype(F32)
                norm_start(1, 0, half, rounded.astype(F32))

    def out_copy(which):
        return remote(outs.at[which, 1 - section], outs_in.at[which],
                      out_send.at[which], out_recv.at[which], to_x(1 - section, high))

    out_copy(0).start()

    grads = (grad_m, grad_a)
    from_core = (core_m, core_a)
    from_dp = (dp_m, dp_a)
    quarters = (part_m, part_a)
    from_x = (recv_m, recv_a)
    fulls = (full_m, full_a)
    lengths = (128, 64)

    def core_copy(kind):
        return remote(grads[kind].at[:, other], from_core[kind],
                      core_send.at[kind], core_recv.at[kind], to_core)

    def dp_rows(kind, index):
        length = lengths[kind]
        return pl.ds(pl.multiple_of(index * length, length), length)

    def dp_copy(kind, layer, step):
        dest = next_of(group, step, DP)
        return remote(grads[kind].at[:, core, dp_rows(kind, dest)],
                      from_dp[kind].at[layer, step - 1],
                      dp_send.at[kind, step], dp_recv.at[kind, layer, step], to_dp(dest))

    def x_copy(kind, layer, source):
        return remote(quarters[kind].at[layer, source], from_x[kind].at[along_x],
                      x_send.at[kind, layer * 2 + source], x_recv.at[kind, along_x],
                      to_x(layer, source))

    def core_done(kind, layer):
        core_copy(kind).wait()
        for source in range(2):
            grads[kind][source, core] = (
                grads[kind][source, core].astype(F32) + from_core[kind][source].astype(F32)
            ).astype(BF16)
        for step in range(1, DP):
            dp_copy(kind, layer, step).start()

    def dp_done(kind, layer):
        total = grads[kind][:, core, dp_rows(kind, group)].astype(F32)
        for step in range(1, DP):
            arrival(from_dp[kind].at[layer, step - 1],
                    dp_recv.at[kind, layer, step]).wait_recv()
            total = total + from_dp[kind][layer, step - 1].astype(F32)
        quarters[kind][layer] = total.astype(BF16)
        for source in range(2):
            @pl.when(jnp.logical_not(is_own(layer, source)))
            def _():
                x_copy(kind, layer, source).start()
        for step in range(1, DP):
            dp_copy(kind, layer, step).wait_send()

    def full_copy(kind, step):
        ref = fulls[kind]
        return remote(ref.at[group], ref.at[group], full_send.at[kind, step],
                      full_recv.at[kind, group], to_dp(next_of(group, step, DP)))

    def x_done(kind):
        total = quarters[kind][section, high].astype(F32)
        for step in range(1, 4):
            source = next_of(along_x, step, 4)
            arrival(from_x[kind].at[source], x_recv.at[kind, source]).wait_recv()
            total = total + from_x[kind][source].astype(F32)
        fulls[kind][group] = total.astype(BF16)
        for step in range(1, DP):
            full_copy(kind, step).start()

    mine = live[group * MICRO + section]
    everyone = live[section]
    for step in range(1, DP):
        everyone = everyone + live[step * MICRO + section]
    weight = jnp.where(mine > 0, 1.0 / jnp.full((1, D), everyone, jnp.int32).astype(F32), 0.0)
    cot[...] = out_grad[section].astype(F32) * weight

    def back_start(layer, half):
        above = cot[own_rows(half)]
        d_branch2 = (above * vector(layer, 7)).astype(BF16)
        gather_start(layer, 2, half, d_branch2)
        vec[layer, 7:8] += sum_rows(above * branches[layer, 1, own_rows(half)])
        vec[layer, 6:7] += sum_rows(d_branch2.astype(F32))

    for half in range(HALVES):
        back_start(1, half)

    @pl.loop(0, 2)
    def _(turn):
        layer = 1 - turn

        def feed_back(pair):
            rows = gather_take(layer, 2, pair)
            d_act = dot_nt(rows, down_weights(layer))
            back = (d_act * slope[layer, half_rows(pair)].astype(F32)).astype(BF16)
            d_pre[half_rows(pair)] = back
            vec[layer, 8:9] += sum_rows(back.astype(F32))
            part_start(2, pair, dot_nn(back, up_weights(layer)))

        each_half(feed_back)
        gather_finish(layer, 2)
        for half in range(HALVES):
            rows = own_rows(half)
            d_normed = part_sum(2, half)
            unit, inv = units[layer, 1, rows], get_inv(layer, 1, half)
            d_hidden = cot[rows] + normalize_back(d_normed, unit, inv, vector(layer, 4))
            hidden[rows] = d_hidden
            d_branch = (d_hidden * vector(layer, 3)).astype(BF16)
            gather_start(layer, 3, half, d_branch)
            vec[layer, 4:5] += sum_rows(d_normed * unit)
            vec[layer, 5:6] += sum_rows(d_normed)
            vec[layer, 3:4] += sum_rows(d_hidden * branches[layer, 0, rows])
            vec[layer, 2:3] += sum_rows(d_branch.astype(F32))

        for member in range(QUAD):
            units_of = slice(member * 256, member * 256 + 256)
            at = (member // 2, member % 2)
            grad_m[at[0], at[1], 0:256] = dot_tn(d_pre[:, units_of], whole(layer, 1)).astype(BF16)
            grad_m[at[0], at[1], 256:512] = dot_tn(
                act[layer, :, units_of], whole(layer, 2)).astype(BF16)
        core_copy(0).start()
        d_outs = []

        def out_back(pair):
            rows = gather_take(layer, 3, pair)
            d_outs.append(dot_nt(rows, out_weights(layer)).astype(BF16))

        each_half(out_back)
        for member in range(QUAD):
            d_att_out[member] = jnp.concatenate(
                [half[:, member * 64:member * 64 + 64] for half in d_outs], axis=-1)
        quad_start(2)
        gather_finish(layer, 3)
        core_done(0, layer)

        @pl.when(turn == 1)
        def _():
            dp_done(1, 1)

        out_grads = dot_tn(attended[layer], whole(layer, 3)).astype(BF16)
        d_keys[...] = jnp.zeros_like(d_keys)
        d_values[...] = jnp.zeros_like(d_values)
        quad_take(2)

        @pl.loop(0, QUAD)
        def _(source):
            d_rows = unpack_halves(d_att_got[source])
            score_grads = []
            for half in range(2):
                rows = token_rows(source, half, 128)
                d_share = dot_nt(d_rows[half * 128:half * 128 + 128], values[layer])
                wide = probs[layer, rows].astype(F32)
                product = wide * d_share
                d_score = (product - wide * jnp.sum(product, axis=-1, keepdims=True)).astype(BF16)
                score_grads.append(d_score)
                d_mix_out[source, half, 0:128, 0:64] = (
                    dot_nn(d_score, keys[layer]) * 0.125).astype(BF16)
            d_keys[...] += dot_tn(jnp.concatenate(score_grads, 0),
                                  queries[layer, token_rows(source)])
            d_values[...] += dot_tn(probs[layer, token_rows(source)], d_rows)

        for source in range(QUAD):
            for half in range(HALVES):
                rows = token_rows(source, half, 128)
                d_mix_out[source, half, 0:128, 64:128] = d_keys[rows].astype(BF16)
                value = d_values[rows].astype(BF16)
                d_mix_out[source, half, 128:192] = jnp.concatenate(
                    [value[0:64], value[64:128]], axis=-1)
        quad_start(3)
        for member in range(QUAD):
            grad_a[member // 2, member % 2, 192:256] = out_grads[member * 64:member * 64 + 64]
        quad_take(3)

        none = jnp.zeros((2 * ROWS, 64), BF16)

        def project_back(pair):
            for member in range(QUAD):
                first = member * 256
                d_mixed[half_rows(pair), first:first + 128] = d_mix_got[member, pair, 0:128]
                d_mixed[half_rows(pair), first + 128:first + 256] = jnp.concatenate(
                    [unpack_values(member, pair), none], axis=-1)
            rows = d_mixed[half_rows(pair)]
            vec[layer, 9:10] += sum_rows(rows.astype(F32))
            part_start(3, pair, dot_nn(rows, attn_weights(layer)))

        each_half(project_back)
        for member in range(QUAD):
            grad_a[member // 2, member % 2, 0:192] = dot_tn(
                d_mixed[:, member * 256:member * 256 + 256], whole(layer, 0))[0:192].astype(BF16)
        core_copy(1).start()
        quad_finish(2)
        quad_finish(3)
        for half in range(HALVES):
            rows = own_rows(half)
            d_normed = part_sum(3, half)
            unit, inv = units[layer, 0, rows], get_inv(layer, 0, half)
            rounded = (hidden[rows] + normalize_back(
                d_normed, unit, inv, vector(layer, 0))).astype(BF16)
            outs[1, layer, rows] = rounded
            cot[rows] = rounded.astype(F32)

            @pl.when(turn == 0)
            def _():
                back_start(0, half)

            vec[layer, 0:1] += sum_rows(d_normed * unit)
            vec[layer, 1:2] += sum_rows(d_normed)

        core_done(1, layer)
        dp_done(0, layer)

    out_copy(1).start()
    x_done(0)

    def lane_copy(dest):
        return remote(vec.at[:, pl.ds(0, 8)], lane_vec.at[lane],
                      lane_send.at[dest], lane_recv.at[lane], to_lane(dest))

    for step in range(1, LANE):
        lane_copy(next_of(lane, step, LANE)).start()
    for step in range(1, LANE):
        source = next_of(lane, step, LANE)
        arrival(lane_vec.at[source], lane_recv.at[source]).wait_recv()
    for step in range(1, LANE):
        lane_copy(next_of(lane, step, LANE)).wait_send()
    for step in range(1, LANE):
        vec[:, 0:8] += lane_vec[next_of(lane, step, LANE)]
    cv_copy = remote(vec, core_vec, cv_send.at[0], cv_recv.at[0], to_core)
    cv_copy.start()
    cv_copy.wait()
    vec[...] += core_vec[...]

    def xv_copy(layer, source):
        return remote(vec.at[layer], x_vec.at[along_x], xv_send.at[layer * 2 + source],
                      xv_recv.at[along_x], to_x(layer, source))

    for layer in range(2):
        for source in range(2):
            @pl.when(jnp.logical_not(is_own(layer, source)))
            def _():
                xv_copy(layer, source).start()

    dp_done(1, 0)

    total = vec[section]
    for step in range(1, 4):
        source = next_of(along_x, step, 4)
        arrival(x_vec.at[source], xv_recv.at[source]).wait_recv()
        total = total + x_vec[source]
    dp_vec[group] = total

    def yv_copy(step):
        return remote(dp_vec.at[group], dp_vec.at[group], yv_send.at[step],
                      yv_recv.at[group], to_dp(next_of(group, step, DP)))

    for step in range(1, DP):
        yv_copy(step).start()
    x_done(1)

    for which, ref in ((0, so_ref), (1, ig_ref)):
        out_copy(which).wait()
        ref[section] = outs[which, section]
        ref[1 - section] = outs_in[which]

    for step in range(1, DP):
        source = next_of(group, step, DP)
        arrival(dp_vec.at[source], yv_recv.at[source]).wait_recv()
        total = total + dp_vec[source]
    for step in range(1, DP):
        yv_copy(step).wait_send()
    g_vec_ref[...] = total[0:8]
    dp_vec[group] = total
    bias_of = dp_vec[group, :, pl.ds(pl.multiple_of(quad * 256, 256), 256)]
    g_bias_ref[...] = bias_of[8:9]
    g_qv_ref[...] = jnp.concatenate([bias_of[9:10, 0:64], bias_of[9:10, 128:192]], axis=0)

    for kind in range(2):
        for step in range(1, DP):
            source = next_of(group, step, DP)
            arrival(fulls[kind].at[source], full_recv.at[kind, source]).wait_recv()
        if kind == 0:
            for part in range(4):
                g_up_ref[part * 256:part * 256 + 256] = full_m[
                    0:2, :, part * 256:part * 256 + 256].reshape(256, 256).astype(F32).T.astype(BF16)
            g_down_ref[...] = full_m[2:4].reshape(256, D)
        else:
            g_in_ref[...] = full_a[0:3].reshape(192, D)
            g_out_ref[...] = full_a[3]

    for layer in range(2):
        @pl.when(section == layer)
        def _():
            for kind in range(4):
                for step in range(1, 4):
                    x_piece(kind, layer, step).wait_send()

        for source in range(2):
            for kind in range(4):
                core_piece(kind, layer, source).wait_send()

            @pl.when(jnp.logical_not(is_own(layer, source)))
            def _():
                for kind in (HEAD, REST, MLP):
                    if by_quarters(kind, layer):
                        for step in range(1, DP):
                            dp_piece(kind, layer, source, step).wait_send()
                for kind in range(2):
                    x_copy(kind, layer, source).wait_send()
                xv_copy(layer, source).wait_send()
    for step in range(1, DP):
        for kind in range(2):
            full_copy(kind, step).wait_send()


def run_layers(*operands):
    vmem = pl.BlockSpec(memory_space=pltpu.VMEM)
    anywhere = pl.BlockSpec(memory_space=pl.ANY)
    dma = pltpu.SemaphoreType.DMA
    every = QUAD * TOKENS
    scratch = [
        pltpu.VMEM((2, QUAD, 16, D), F32),
        pltpu.VMEM((2, QUAD, 256, D), BF16),
        pltpu.VMEM((2, QUAD, 512, D), BF16),
        pltpu.VMEM((2, GATHERS, HALVES, LANE, HALF, D), BF16),
        pltpu.VMEM((2, HALVES, LANE, HALF, D), BF16),
        pltpu.VMEM((2, HALVES, LANE, HALF, D), BF16),
        pltpu.VMEM((2, ROWS, D), F32),
        pltpu.VMEM((2, 2, ROWS, D), F32),
        pltpu.VMEM((2, 2, ROWS, 128), F32),
        pltpu.VMEM((2, 2, ROWS, D), F32),
        pltpu.VMEM((ROWS, D), F32),
        pltpu.VMEM((ROWS, D), F32),
        pltpu.VMEM((QUAD, HALVES, 192, 128), BF16),
        pltpu.VMEM((QUAD, HALVES, 192, 128), BF16),
        pltpu.VMEM((2, every, 64), BF16),
        pltpu.VMEM((2, every, 64), BF16),
        pltpu.VMEM((2, every, 64), BF16),
        pltpu.VMEM((QUAD, 128, 128), BF16),
        pltpu.VMEM((QUAD, 128, 128), BF16),
        pltpu.VMEM((2, TOKENS, 256), BF16),
        pltpu.VMEM((2, every, every), BF16),
        pltpu.VMEM((2, TOKENS, 1024), BF16),
        pltpu.VMEM((2, TOKENS, 1024), BF16),
        pltpu.VMEM((TOKENS, 1024), BF16),
        pltpu.VMEM((TOKENS, 1024), BF16),
        pltpu.VMEM((QUAD, 128, 128), BF16),
        pltpu.VMEM((every, 64), F32),
        pltpu.VMEM((every, 64), F32),
        pltpu.VMEM((2, 2, 512, D), BF16),
        pltpu.VMEM((2, 2, 256, D), BF16),
        pltpu.VMEM((2, 512, D), BF16),
        pltpu.VMEM((2, 256, D), BF16),
        pltpu.VMEM((2, DP - 1, 2, 128, D), BF16),
        pltpu.VMEM((2, DP - 1, 2, 64, D), BF16),
        pltpu.VMEM((2, 2, 128, D), BF16),
        pltpu.VMEM((2, 2, 64, D), BF16),
        pltpu.VMEM((4, 128, D), BF16),
        pltpu.VMEM((4, 64, D), BF16),
        pltpu.VMEM((DP, 128, D), BF16),
        pltpu.VMEM((DP, 64, D), BF16),
        pltpu.VMEM((2, 16, D), F32),
        pltpu.VMEM((LANE, 2, 8, D), F32),
        pltpu.VMEM((2, 16, D), F32),
        pltpu.VMEM((4, 16, D), F32),
        pltpu.VMEM((DP, 16, D), F32),
        pltpu.VMEM((2, 2, ROWS, D), BF16),
        pltpu.VMEM((2, ROWS, D), BF16),
        dma((4,)), dma((4, 4)), dma((4, 4)),
        dma((4, 4, DP)), dma((4, 4, DP)), dma((4, 4)), dma((4, 4)),
        dma((GATHERS, 2 * LANE)), dma((GATHERS, 2 * LANE)),
        dma((2 * LANE,)), dma((GATHERS, 2 * LANE)),
        dma((5, QUAD)), dma((5, QUAD)),
        dma((2,)), dma((2,)),
        dma((2, DP)), dma((2, 2, DP)),
        dma((2, 4)), dma((2, 4)),
        dma((2, DP)), dma((2, DP)),
        dma((2,)), dma((2,)),
        dma((LANE,)), dma((LANE,)),
        dma((1,)), dma((1,)),
        dma((4,)), dma((4,)),
        dma((DP,)), dma((DP,)),
    ]
    return pl.pallas_call(
        kernel,
        out_shape=(
            jax.ShapeDtypeStruct((2, ROWS, D), BF16),
            jax.ShapeDtypeStruct((2, ROWS, D), BF16),
            jax.ShapeDtypeStruct((192, D), BF16),
            jax.ShapeDtypeStruct((64, D), BF16),
            jax.ShapeDtypeStruct((D, 256), BF16),
            jax.ShapeDtypeStruct((256, D), BF16),
            jax.ShapeDtypeStruct((2, 64), F32),
            jax.ShapeDtypeStruct((1, 256), F32),
            jax.ShapeDtypeStruct((8, D), F32),
        ),
        in_specs=[vmem, vmem, pl.BlockSpec(memory_space=pltpu.SMEM)] + [anywhere] * 4 + [vmem] * 3,
        out_specs=(vmem,) * 9,
        scratch_shapes=scratch,
        name="two_layers",
        compiler_params=pltpu.CompilerParams(
            collective_id=0, has_side_effects=True, vmem_limit_bytes=63 * 2**20
        ),
    )(*operands)


def body(
    images, out_grad, live_images, attn_in, qv_bias, attn_out, mlp_in, mlp_bias, mlp_out, vectors
):
    section_out, section_in_grad, g_in, g_out, g_up, g_down, g_qv, g_bias, g_vec = run_layers(
        images, out_grad, live_images, attn_in[0].transpose(1, 2, 0).reshape(192, D),
        attn_out[0], mlp_in[0], mlp_out[0], qv_bias[0], mlp_bias, vectors[0])
    return (
        section_out[None],
        section_in_grad[None],
        g_in.astype(F32).reshape(3, 64, D).transpose(2, 0, 1)[None],
        g_qv[None],
        g_out.astype(F32)[None],
        g_up.astype(F32)[None],
        g_bias,
        g_down.astype(F32)[None],
        g_vec[None],
    )


def solution(mesh):
    placed = (
        P("dp", "tensor", None),
        P("dp", "tensor", None),
        P(),
        P("section", None, None, "tensor"),
        P("section", None, "tensor"),
        P("section", "tensor", None),
        P("section", None, "tensor"),
        P("section", "tensor"),
        P("section", "tensor", None),
        P("section", None, None),
    )
    return jax.shard_map(
        body,
        mesh=mesh,
        in_specs=placed,
        out_specs=(
            P("section", "dp", "tensor", None),
            P("section", "dp", "tensor", None),
            P("section", None, None, "tensor"),
            P("section", None, "tensor"),
            P("section", "tensor", None),
            P("section", None, "tensor"),
            P("section", "tensor"),
            P("section", "tensor", None),
            P("section", None, None),
        ),
        check_vma=False,
    )
```

```python
import jax
import jax.numpy as jnp
from jax import lax
from jax.experimental import pallas as pl
from jax.experimental.pallas import tpu as pltpu
from jax.sharding import PartitionSpec as P

MESH = pl.DeviceIdType.MESH
F32 = jnp.float32
BF16 = jnp.bfloat16
EPSILON = 1e-06
D = 1024
MICRO = 2
LANE = 4
QUAD = 4
ROWS = 64
HALVES = 2
HALF = ROWS // HALVES
TOKENS = LANE * ROWS
DP = 4
BIAS_ROW = 8
XORS = (1, 3, 2, 0)
OWN = 3
GATHERS = 4
SMALL, HEAD, REST, MLP = range(4)


def dot_nn(a, b):
    return lax.dot_general(a, b, (((1,), (0,)), ((), ())), preferred_element_type=F32)


def dot_nt(a, b):
    return lax.dot_general(a, b, (((1,), (1,)), ((), ())), preferred_element_type=F32)


def dot_tn(a, b):
    return lax.dot_general(a, b, (((0,), (0,)), ((), ())), preferred_element_type=F32)


def normalize(rows):
    center = rows - jnp.mean(rows, axis=-1, keepdims=True)
    inv = lax.rsqrt(jnp.mean(center * center, axis=-1, keepdims=True) + EPSILON)
    return center * inv, inv


def normalize_back(grad, unit, inv, gain):
    scaled = grad * gain
    return inv * (
        scaled
        - jnp.mean(scaled, axis=-1, keepdims=True)
        - unit * jnp.mean(scaled * unit, axis=-1, keepdims=True)
    )


def sum_rows(rows):
    return jnp.sum(rows, axis=0, keepdims=True)


def kernel(
    images, out_grad, live, qkv_in, out_in, up_in, down_in, qv_bias, up_bias_in, vectors_in,
    so_ref, ig_ref, g_in_ref, g_out_ref, g_up_ref, g_down_ref, g_qv_ref, g_bias_ref, g_vec_ref,
    small_w, attn_w, mlp_w,
    gathered, parts, landed,
    xs, units, invs, branches, hidden, cot,
    qkv_out, qkv_got, queries, keys, values, att_out, att_got, attended, probs,
    act, slope, d_pre, d_mixed, d_att_got, d_keys, d_values,
    grad_m, grad_a, core_m, core_a, dp_m, dp_a, part_m, part_a, recv_m, recv_a, full_m, full_a,
    vec, lane_vec, core_vec, x_vec, dp_vec, outs, outs_in,
    w_local, w_x_send, w_x_recv, w_dp_send, w_dp_recv, w_core_send, w_core_recv,
    ag_send, ag_recv, rs_send, rs_recv, quad_send, quad_recv,
    core_send, core_recv, dp_send, dp_recv, x_send, x_recv, full_send, full_recv,
    out_send, out_recv, lane_send, lane_recv, cv_send, cv_recv, xv_send, xv_recv,
    yv_send, yv_recv,
):
    section = lax.axis_index("section")
    group = lax.axis_index("dp")
    tensor = lax.axis_index("tensor")
    core = lax.rem(tensor, 2)
    lane = lax.rem(tensor // 2, LANE)
    high = tensor // (2 * LANE)
    other = 1 - core
    quad = high * 2 + core
    along_x = section * 2 + high

    def place(high_at, lane_at, core_at):
        return (high_at * LANE + lane_at) * 2 + core_at

    def to_lane(index):
        return {"tensor": place(high, index, core)}

    def to_quad(index):
        return {"tensor": place(index // 2, lane, lax.rem(index, 2))}

    def to_x(section_at, high_at):
        return {"section": section_at, "tensor": place(high_at, lane, core)}

    def to_dp(index):
        return {"dp": index}

    to_core = {"tensor": place(high, lane, other)}

    def next_of(own, step, count):
        return lax.rem(own + step, count)

    def remote(src, dst, send_sem, recv_sem, device):
        return pltpu.make_async_remote_copy(
            src_ref=src, dst_ref=dst, send_sem=send_sem, recv_sem=recv_sem,
            device_id=device, device_id_type=MESH,
        )

    def arrival(block, recv_sem):
        return remote(block, block, cv_send.at[0], recv_sem, to_core)

    own_attn = attn_w.at[section, quad]
    own_mlp = mlp_w.at[section, quad]
    landing = probs.at[1, :, pl.ds(0, 256)]
    loads = [
        pltpu.make_async_copy(origin, there, w_local.at[at]) for at, (origin, there) in enumerate((
            (qkv_in, own_attn.at[pl.ds(0, 192)]),
            (out_in, own_attn.at[pl.ds(192, 64)]),
            (up_in, landing),
            (down_in, own_mlp.at[pl.ds(256, 256)]),
        ))
    ]
    for load in loads:
        load.start()
    small_w[section, quad, 0:8] = vectors_in[...]
    gap = jnp.zeros((1, 64), F32)
    small_w[section, quad, 8:9] = jnp.concatenate(
        [qv_bias[0:1], gap, qv_bias[1:2], gap, up_bias_in[...], jnp.zeros((1, 512), F32)], axis=1)

    barrier = pltpu.get_barrier_semaphore()
    friends = [to_lane(next_of(lane, step, LANE)) for step in range(1, LANE)]
    friends += [to_quad(next_of(quad, step, QUAD)) for step in range(1, QUAD)]
    friends += [to_x(1 - section, high), to_x(1 - section, 1 - high)]
    friends += [to_dp(next_of(group, step, DP)) for step in range(1, DP)]
    for friend in friends:
        pl.semaphore_signal(barrier, inc=1, device_id=friend, device_id_type=MESH)
    pl.semaphore_wait(barrier, len(friends))

    def is_own(layer, source):
        return jnp.logical_and(layer == section, source == high)

    def piece(kind, layer, member):
        if kind == SMALL:
            return small_w.at[layer, member]
        if kind == MLP:
            return mlp_w.at[layer, member]
        return attn_w.at[layer, member, pl.ds((kind - HEAD) * 128, 128)]

    def by_quarters(kind, layer):
        return kind != SMALL

    def quarter(kind, layer, member, index):
        if kind == MLP:
            return mlp_w.at[layer, member, pl.ds(pl.multiple_of(index * 128, 128), 128)]
        first = pl.multiple_of((kind - HEAD) * 128 + index * 32, 32)
        return attn_w.at[layer, member, pl.ds(first, 32)]

    def x_block(kind, layer, member):
        if by_quarters(kind, layer):
            return quarter(kind, layer, member, group)
        return piece(kind, layer, member)

    def x_piece(kind, layer, step):
        peer = next_of(along_x, step, 4)
        block = x_block(kind, layer, quad)
        return remote(block, block, w_x_send.at[kind, step], w_x_recv.at[kind, along_x],
                      to_x(peer // 2, lax.rem(peer, 2)))

    def dp_piece(kind, layer, source, step):
        block = quarter(kind, layer, source * 2 + core, group)
        return remote(block, block, w_dp_send.at[kind, layer * 2 + source, step],
                      w_dp_recv.at[kind, layer * 2 + source, group],
                      to_dp(next_of(group, step, DP)))

    def core_piece(kind, layer, source):
        block = piece(kind, layer, source * 2 + core)
        return remote(block, block, w_core_send.at[kind, layer * 2 + source],
                      w_core_recv.at[kind, layer * 2 + source], to_core)

    def send_pieces(kind, layer):
        @pl.when(section == layer)
        def _():
            for step in range(1, 4):
                x_piece(kind, layer, step).start()

    def spread_pieces(kind, layer):
        for source in range(2):
            @pl.when(jnp.logical_not(is_own(layer, source)))
            def _():
                arrival(x_block(kind, layer, source * 2 + core),
                        w_x_recv.at[kind, layer * 2 + source]).wait_recv()
                for step in range(1, DP):
                    dp_piece(kind, layer, source, step).start()

    def relay_pieces(kind, layer):
        for source in range(2):
            @pl.when(jnp.logical_not(is_own(layer, source)))
            def _():
                if by_quarters(kind, layer):
                    for step in range(1, DP):
                        sender = next_of(group, step, DP)
                        arrival(quarter(kind, layer, source * 2 + core, sender),
                                w_dp_recv.at[kind, layer * 2 + source, sender]).wait_recv()
                else:
                    arrival(x_block(kind, layer, source * 2 + core),
                            w_x_recv.at[kind, layer * 2 + source]).wait_recv()

            core_piece(kind, layer, source).start()

    def take_pieces(kind, layer):
        for source in range(2):
            arrival(piece(kind, layer, source * 2 + other),
                    w_core_recv.at[kind, layer * 2 + source]).wait_recv()

    def lane_of(slot):
        return jnp.bitwise_xor(lane, XORS[slot])

    def gather_copy(layer, which, half, slot):
        at = half * LANE + slot
        return remote(gathered.at[layer, which, half, OWN], gathered.at[layer, which, half, slot],
                      ag_send.at[which, at], ag_recv.at[which, at], to_lane(lane_of(slot)))

    def gather_start(layer, which, half, rows):
        gathered[layer, which, half, OWN] = rows
        for slot in range(OWN):
            gather_copy(layer, which, half, slot).start()

    def gather_finish(layer, which):
        for half in range(HALVES):
            for slot in range(OWN):
                gather_copy(layer, which, half, slot).wait_send()

    def gather_take(layer, which, half):
        for slot in range(OWN):
            arrival(gathered.at[layer, which, half, slot],
                    ag_recv.at[which, half * LANE + slot]).wait_recv()
        return gathered[layer, which, half].reshape(LANE * HALF, D)

    def whole(layer, which):
        return gathered[layer, which].reshape(TOKENS, D)

    def part_copy(which, half, slot):
        at = half * LANE + slot
        return remote(parts.at[which % 2, half, slot], landed.at[which % 2, half, slot],
                      rs_send.at[at], rs_recv.at[which, at], to_lane(lane_of(slot)))

    def part_start(which, half, rows):
        parts[which % 2, half] = rows.astype(BF16).reshape(LANE, HALF, D)
        for slot in range(OWN):
            part_copy(which, half, slot).start()

    def part_sum(which, half):
        total = parts[which % 2, half, OWN].astype(F32)
        for slot in range(OWN):
            arrival(landed.at[which % 2, half, slot],
                    rs_recv.at[which, half * LANE + slot]).wait_recv()
            total = total + landed[which % 2, half, slot].astype(F32)
        for slot in range(OWN):
            part_copy(which, half, slot).wait_send()
        return total

    def own_rows(half):
        return slice(half * HALF, (half + 1) * HALF)

    def each_half(work):
        for half in range(HALVES):
            work(half)

    def half_rows(half):
        return slice(half * LANE * HALF, (half + 1) * LANE * HALF)

    d_att_out, d_mix_out, d_mix_got = att_out, qkv_out, qkv_got
    exchanges = ((qkv_out, qkv_got), (att_out, att_got), (d_att_out, d_att_got),
                 (d_mix_out, d_mix_got))

    def quad_copy(which, dest):
        origin, there = exchanges[which]
        return remote(origin.at[dest], there.at[quad], quad_send.at[which, dest],
                      quad_recv.at[which, quad], to_quad(dest))

    def pack_rows(member, half, query_key, value):
        qkv_out[member, half, 0:128] = query_key
        qkv_out[member, half, 128:192] = jnp.concatenate([value[0:64], value[64:128]], axis=-1)

    def unpack_values(source, half):
        block = qkv_got[source, half, 128:192]
        return jnp.concatenate([block[:, 0:64], block[:, 64:128]], axis=0)

    def unpack_halves(block):
        return jnp.concatenate([block[:, 0:64], block[:, 64:128]], axis=0)

    def half_copy(half, dest):
        return remote(qkv_out.at[dest, half], qkv_got.at[quad, half],
                      quad_send.at[4 * half, dest], quad_recv.at[4 * half, quad], to_quad(dest))

    def quad_start(which):
        origin, there = exchanges[which]
        for step in (2, 3, 1):
            quad_copy(which, jnp.bitwise_xor(quad, step)).start()
        there[quad] = origin[quad]

    def quad_take(which):
        there = exchanges[which][1]
        for step in (1, 2, 3):
            source = jnp.bitwise_xor(quad, step)
            arrival(there.at[source], quad_recv.at[which, source]).wait_recv()

    def quad_finish(which):
        for step in (1, 2, 3):
            quad_copy(which, jnp.bitwise_xor(quad, step)).wait_send()

    def token_rows(source, half=0, length=TOKENS):
        return pl.ds(pl.multiple_of(source * TOKENS + half * length, length), length)

    def vector(layer, row):
        return small_w[layer, quad, row:row + 1]

    def all_biases(layer, first):
        row = slice(BIAS_ROW, BIAS_ROW + 1)
        return jnp.concatenate(
            [small_w[layer, member, row, first:first + 256] for member in range(QUAD)], axis=-1)

    def keep_inv(layer, which, half, inv):
        invs[layer, which, own_rows(half)] = jnp.broadcast_to(inv, (HALF, 128))

    def get_inv(layer, which, half):
        return invs[layer, which, own_rows(half), 0:1]

    def norm_start(layer, which, half, rows):
        unit, inv = normalize(rows)
        units[layer, which, own_rows(half)] = unit
        keep_inv(layer, which, half, inv)
        gain, offset = vector(layer, which * 4), vector(layer, which * 4 + 1)
        gather_start(layer, which, half, (unit * gain + offset).astype(BF16))

    def attn_weights(layer):
        return attn_w[layer].reshape(QUAD * 256, D)

    def out_weights(layer):
        return attn_w[layer, :, 192:256].reshape(QUAD * 64, D)

    def up_weights(layer):
        return mlp_w[layer, :, 0:256].reshape(QUAD * 256, D)

    def down_weights(layer):
        return mlp_w[layer, :, 256:512].reshape(QUAD * 256, D)

    for layer in range(2):
        send_pieces(SMALL, layer)
    loads[0].wait()
    loads[1].wait()
    send_pieces(HEAD, 0)
    send_pieces(REST, 0)
    loads[2].wait()
    for part in range(4):
        mlp_w[section, quad, 0:256, part * 256:part * 256 + 256] = (
            probs[1, part * 256:part * 256 + 256, 0:256].astype(F32).T.astype(BF16))
    loads[3].wait()
    send_pieces(MLP, 0)
    xs[0] = images[section].astype(F32)
    vec[...] = jnp.zeros_like(vec)
    for layer in range(2):
        relay_pieces(SMALL, layer)

    for half in range(HALVES):
        norm_start(0, 0, half, xs[0, own_rows(half)])

    @pl.loop(0, 2)
    def _(layer):
        @pl.when(layer == 0)
        def _():
            spread_pieces(HEAD, 0)
            spread_pieces(REST, 0)
            relay_pieces(REST, 0)
            relay_pieces(HEAD, 0)
            for either in range(2):
                take_pieces(SMALL, either)

        take_pieces(REST, layer)
        take_pieces(HEAD, layer)
        qkv_bias = all_biases(layer, 0)

        def project(pair):
            rows = gather_take(layer, 0, pair)
            mixed = (dot_nt(rows, attn_weights(layer)) + qkv_bias).astype(BF16)
            for member in range(QUAD):
                first = member * 256
                pack_rows(member, pair, mixed[:, first:first + 128],
                          mixed[:, first + 128:first + 192])
            for step in (2, 3, 1):
                half_copy(pair, jnp.bitwise_xor(quad, step)).start()

        each_half(project)
        qkv_got[quad] = qkv_out[quad]

        @pl.when(layer == 0)
        def _():
            for kind in (HEAD, REST, MLP):
                send_pieces(kind, 1)
            spread_pieces(MLP, 0)

        @pl.when(layer == 1)
        def _():
            relay_pieces(MLP, 1)

        for half in range(HALVES):
            for step in (1, 2, 3):
                source = jnp.bitwise_xor(quad, step)
                arrival(qkv_got.at[source, half],
                        quad_recv.at[4 * half, source]).wait_recv()
        for source in range(QUAD):
            for half in range(HALVES):
                rows = token_rows(source, half, 128)
                block = qkv_got[source, half, 0:128]
                queries[layer, rows] = (block[:, 0:64].astype(F32) * 0.125).astype(BF16)
                keys[layer, rows] = block[:, 64:128]
                values[layer, rows] = unpack_values(source, half)

        @pl.loop(0, QUAD)
        def _(step):
            source = lax.rem(quad + 1 + step, QUAD)
            found = []
            for half in range(2):
                rows = token_rows(source, half, 128)
                scores = dot_nt(queries[layer, rows], keys[layer])
                grown = jnp.exp(scores - jnp.max(scores, axis=-1, keepdims=True))
                share = (grown / jnp.sum(grown, axis=-1, keepdims=True)).astype(BF16)
                probs[layer, rows] = share
                found.append(dot_nn(share, values[layer]).astype(BF16))
            att_out[source] = jnp.concatenate(found, axis=-1)

            @pl.when(source != quad)
            def _():
                quad_copy(1, source).start()

        att_got[quad] = att_out[quad]
        quad_take(1)
        attended[layer] = jnp.concatenate(
            [unpack_halves(att_got[member]) for member in range(QUAD)], axis=-1)

        def project_out(pair):
            part_start(0, pair, dot_nn(attended[layer, half_rows(pair)], out_weights(layer)))

        each_half(project_out)
        for half in range(HALVES):
            for step in (1, 2, 3):
                half_copy(half, jnp.bitwise_xor(quad, step)).wait_send()
        quad_finish(1)
        gather_finish(layer, 0)
        for half in range(HALVES):
            branch = part_sum(0, half) + vector(layer, 2)
            branches[layer, 0, own_rows(half)] = branch
            state = xs[layer, own_rows(half)] + vector(layer, 3) * branch
            hidden[own_rows(half)] = state
            norm_start(layer, 1, half, state)

        @pl.when(layer == 0)
        def _():
            relay_pieces(MLP, 0)
            for kind in (HEAD, REST, MLP):
                spread_pieces(kind, 1)

        take_pieces(MLP, layer)
        up_bias = all_biases(layer, 256)

        def feed(pair):
            rows = gather_take(layer, 1, pair)
            pre = dot_nt(rows, up_weights(layer)) + up_bias
            cdf = 0.5 + 0.5 * lax.erf(pre * 0.7071067811865476)
            bell = jnp.exp(-0.5 * pre * pre) * 0.3989422804014327
            value = (pre * cdf).astype(BF16)
            act[layer, half_rows(pair)] = value
            slope[layer, half_rows(pair)] = (cdf + pre * bell).astype(BF16)
            part_start(1, pair, dot_nn(value, down_weights(layer)))

        each_half(feed)

        @pl.when(layer == 0)
        def _():
            relay_pieces(HEAD, 1)
            relay_pieces(REST, 1)

        gather_finish(layer, 1)
        for half in range(HALVES):
            branch = part_sum(1, half) + vector(layer, 6)
            branches[layer, 1, own_rows(half)] = branch
            rounded = (hidden[own_rows(half)] + vector(layer, 7) * branch).astype(BF16)
            outs[0, layer, own_rows(half)] = rounded

            @pl.when(layer == 0)
            def _():
                xs[1, own_rows(half)] = rounded.astype(F32)
                norm_start(1, 0, half, rounded.astype(F32))

    def out_copy(which):
        return remote(outs.at[which, 1 - section], outs_in.at[which],
                      out_send.at[which], out_recv.at[which], to_x(1 - section, high))

    out_copy(0).start()

    grads = (grad_m, grad_a)
    from_core = (core_m, core_a)
    from_dp = (dp_m, dp_a)
    quarters = (part_m, part_a)
    from_x = (recv_m, recv_a)
    fulls = (full_m, full_a)
    lengths = (128, 64)

    def core_copy(kind):
        return remote(grads[kind].at[:, other], from_core[kind],
                      core_send.at[kind], core_recv.at[kind], to_core)

    def dp_rows(kind, index):
        length = lengths[kind]
        return pl.ds(pl.multiple_of(index * length, length), length)

    def dp_copy(kind, layer, step):
        dest = next_of(group, step, DP)
        return remote(grads[kind].at[:, core, dp_rows(kind, dest)],
                      from_dp[kind].at[layer, step - 1],
                      dp_send.at[kind, step], dp_recv.at[kind, layer, step], to_dp(dest))

    def x_copy(kind, layer, source):
        return remote(quarters[kind].at[layer, source], from_x[kind].at[along_x],
                      x_send.at[kind, layer * 2 + source], x_recv.at[kind, along_x],
                      to_x(layer, source))

    def core_done(kind, layer):
        core_copy(kind).wait()
        for source in range(2):
            grads[kind][source, core] = (
                grads[kind][source, core].astype(F32) + from_core[kind][source].astype(F32)
            ).astype(BF16)
        for step in range(1, DP):
            dp_copy(kind, layer, step).start()

    def dp_done(kind, layer):
        total = grads[kind][:, core, dp_rows(kind, group)].astype(F32)
        for step in range(1, DP):
            arrival(from_dp[kind].at[layer, step - 1],
                    dp_recv.at[kind, layer, step]).wait_recv()
            total = total + from_dp[kind][layer, step - 1].astype(F32)
        quarters[kind][layer] = total.astype(BF16)
        for source in range(2):
            @pl.when(jnp.logical_not(is_own(layer, source)))
            def _():
                x_copy(kind, layer, source).start()
        for step in range(1, DP):
            dp_copy(kind, layer, step).wait_send()

    def full_copy(kind, step):
        ref = fulls[kind]
        return remote(ref.at[group], ref.at[group], full_send.at[kind, step],
                      full_recv.at[kind, group], to_dp(next_of(group, step, DP)))

    def x_done(kind):
        total = quarters[kind][section, high].astype(F32)
        for step in range(1, 4):
            source = next_of(along_x, step, 4)
            arrival(from_x[kind].at[source], x_recv.at[kind, source]).wait_recv()
            total = total + from_x[kind][source].astype(F32)
        fulls[kind][group] = total.astype(BF16)
        for step in range(1, DP):
            full_copy(kind, step).start()

    mine = live[group * MICRO + section]
    everyone = live[section]
    for step in range(1, DP):
        everyone = everyone + live[step * MICRO + section]
    weight = jnp.where(mine > 0, 1.0 / jnp.full((1, D), everyone, jnp.int32).astype(F32), 0.0)
    cot[...] = out_grad[section].astype(F32) * weight

    def back_start(layer, half):
        above = cot[own_rows(half)]
        d_branch2 = (above * vector(layer, 7)).astype(BF16)
        gather_start(layer, 2, half, d_branch2)
        vec[layer, 7:8] += sum_rows(above * branches[layer, 1, own_rows(half)])
        vec[layer, 6:7] += sum_rows(d_branch2.astype(F32))

    for half in range(HALVES):
        back_start(1, half)

    @pl.loop(0, 2)
    def _(turn):
        layer = 1 - turn

        def feed_back(pair):
            rows = gather_take(layer, 2, pair)
            d_act = dot_nt(rows, down_weights(layer))
            back = (d_act * slope[layer, half_rows(pair)].astype(F32)).astype(BF16)
            d_pre[half_rows(pair)] = back
            vec[layer, 8:9] += sum_rows(back.astype(F32))
            part_start(2, pair, dot_nn(back, up_weights(layer)))

        each_half(feed_back)
        gather_finish(layer, 2)
        for member in range(QUAD):
            units_of = slice(member * 256, member * 256 + 256)
            at = (member // 2, member % 2)
            grad_m[at[0], at[1], 0:256] = dot_tn(d_pre[:, units_of], whole(layer, 1)).astype(BF16)
            grad_m[at[0], at[1], 256:512] = dot_tn(
                act[layer, :, units_of], whole(layer, 2)).astype(BF16)
        core_copy(0).start()
        for half in range(HALVES):
            rows = own_rows(half)
            d_normed = part_sum(2, half)
            unit, inv = units[layer, 1, rows], get_inv(layer, 1, half)
            d_hidden = cot[rows] + normalize_back(d_normed, unit, inv, vector(layer, 4))
            hidden[rows] = d_hidden
            d_branch = (d_hidden * vector(layer, 3)).astype(BF16)
            gather_start(layer, 3, half, d_branch)
            vec[layer, 4:5] += sum_rows(d_normed * unit)
            vec[layer, 5:6] += sum_rows(d_normed)
            vec[layer, 3:4] += sum_rows(d_hidden * branches[layer, 0, rows])
            vec[layer, 2:3] += sum_rows(d_branch.astype(F32))

        core_done(0, layer)
        d_outs = []

        def out_back(pair):
            rows = gather_take(layer, 3, pair)
            d_outs.append(dot_nt(rows, out_weights(layer)).astype(BF16))

        each_half(out_back)
        for member in range(QUAD):
            d_att_out[member] = jnp.concatenate(
                [half[:, member * 64:member * 64 + 64] for half in d_outs], axis=-1)
        quad_start(2)
        gather_finish(layer, 3)

        @pl.when(turn == 1)
        def _():
            dp_done(1, 1)

        out_grads = dot_tn(attended[layer], whole(layer, 3)).astype(BF16)
        d_keys[...] = jnp.zeros_like(d_keys)
        d_values[...] = jnp.zeros_like(d_values)
        quad_take(2)

        @pl.loop(0, QUAD)
        def _(source):
            d_rows = unpack_halves(d_att_got[source])
            score_grads = []
            for half in range(2):
                rows = token_rows(source, half, 128)
                d_share = dot_nt(d_rows[half * 128:half * 128 + 128], values[layer])
                wide = probs[layer, rows].astype(F32)
                product = wide * d_share
                d_score = (product - wide * jnp.sum(product, axis=-1, keepdims=True)).astype(BF16)
                score_grads.append(d_score)
                d_mix_out[source, half, 0:128, 0:64] = (
                    dot_nn(d_score, keys[layer]) * 0.125).astype(BF16)
            d_keys[...] += dot_tn(jnp.concatenate(score_grads, 0),
                                  queries[layer, token_rows(source)])
            d_values[...] += dot_tn(probs[layer, token_rows(source)], d_rows)

        for source in range(QUAD):
            for half in range(HALVES):
                rows = token_rows(source, half, 128)
                d_mix_out[source, half, 0:128, 64:128] = d_keys[rows].astype(BF16)
                value = d_values[rows].astype(BF16)
                d_mix_out[source, half, 128:192] = jnp.concatenate(
                    [value[0:64], value[64:128]], axis=-1)
        quad_start(3)
        for member in range(QUAD):
            grad_a[member // 2, member % 2, 192:256] = out_grads[member * 64:member * 64 + 64]
        quad_take(3)

        none = jnp.zeros((2 * ROWS, 64), BF16)

        def project_back(pair):
            for member in range(QUAD):
                first = member * 256
                d_mixed[half_rows(pair), first:first + 128] = d_mix_got[member, pair, 0:128]
                d_mixed[half_rows(pair), first + 128:first + 256] = jnp.concatenate(
                    [unpack_values(member, pair), none], axis=-1)
            rows = d_mixed[half_rows(pair)]
            vec[layer, 9:10] += sum_rows(rows.astype(F32))
            part_start(3, pair, dot_nn(rows, attn_weights(layer)))

        each_half(project_back)
        for member in range(QUAD):
            grad_a[member // 2, member % 2, 0:192] = dot_tn(
                d_mixed[:, member * 256:member * 256 + 256], whole(layer, 0))[0:192].astype(BF16)
        core_copy(1).start()
        quad_finish(2)
        quad_finish(3)

        @pl.when(turn == 1)
        def _():
            core_done(1, 0)

        for half in range(HALVES):
            rows = own_rows(half)
            d_normed = part_sum(3, half)
            unit, inv = units[layer, 0, rows], get_inv(layer, 0, half)
            rounded = (hidden[rows] + normalize_back(
                d_normed, unit, inv, vector(layer, 0))).astype(BF16)
            outs[1, layer, rows] = rounded
            cot[rows] = rounded.astype(F32)

            @pl.when(turn == 0)
            def _():
                back_start(0, half)

            vec[layer, 0:1] += sum_rows(d_normed * unit)
            vec[layer, 1:2] += sum_rows(d_normed)

        @pl.when(turn == 0)
        def _():
            core_done(1, 1)

        dp_done(0, layer)

    out_copy(1).start()
    x_done(0)

    def lane_copy(dest):
        return remote(vec.at[:, pl.ds(0, 8)], lane_vec.at[lane],
                      lane_send.at[dest], lane_recv.at[lane], to_lane(dest))

    for step in range(1, LANE):
        lane_copy(next_of(lane, step, LANE)).start()
    for step in range(1, LANE):
        source = next_of(lane, step, LANE)
        arrival(lane_vec.at[source], lane_recv.at[source]).wait_recv()
    for step in range(1, LANE):
        lane_copy(next_of(lane, step, LANE)).wait_send()
    for step in range(1, LANE):
        vec[:, 0:8] += lane_vec[next_of(lane, step, LANE)]
    cv_copy = remote(vec, core_vec, cv_send.at[0], cv_recv.at[0], to_core)
    cv_copy.start()
    cv_copy.wait()
    vec[...] += core_vec[...]

    def xv_copy(layer, source):
        return remote(vec.at[layer], x_vec.at[along_x], xv_send.at[layer * 2 + source],
                      xv_recv.at[along_x], to_x(layer, source))

    for layer in range(2):
        for source in range(2):
            @pl.when(jnp.logical_not(is_own(layer, source)))
            def _():
                xv_copy(layer, source).start()

    dp_done(1, 0)

    total = vec[section]
    for step in range(1, 4):
        source = next_of(along_x, step, 4)
        arrival(x_vec.at[source], xv_recv.at[source]).wait_recv()
        total = total + x_vec[source]
    dp_vec[group] = total

    def yv_copy(step):
        return remote(dp_vec.at[group], dp_vec.at[group], yv_send.at[step],
                      yv_recv.at[group], to_dp(next_of(group, step, DP)))

    for step in range(1, DP):
        yv_copy(step).start()
    x_done(1)

    for which, ref in ((0, so_ref), (1, ig_ref)):
        out_copy(which).wait()
        ref[section] = outs[which, section]
        ref[1 - section] = outs_in[which]

    for step in range(1, DP):
        source = next_of(group, step, DP)
        arrival(dp_vec.at[source], yv_recv.at[source]).wait_recv()
        total = total + dp_vec[source]
    for step in range(1, DP):
        yv_copy(step).wait_send()
    g_vec_ref[...] = total[0:8]
    dp_vec[group] = total
    bias_of = dp_vec[group, :, pl.ds(pl.multiple_of(quad * 256, 256), 256)]
    g_bias_ref[...] = bias_of[8:9]
    g_qv_ref[...] = jnp.concatenate([bias_of[9:10, 0:64], bias_of[9:10, 128:192]], axis=0)

    for kind in range(2):
        for step in range(1, DP):
            source = next_of(group, step, DP)
            arrival(fulls[kind].at[source], full_recv.at[kind, source]).wait_recv()
        if kind == 0:
            for part in range(4):
                g_up_ref[part * 256:part * 256 + 256] = full_m[
                    0:2, :, part * 256:part * 256 + 256].reshape(256, 256).astype(F32).T.astype(BF16)
            g_down_ref[...] = full_m[2:4].reshape(256, D)
        else:
            g_in_ref[...] = full_a[0:3].reshape(192, D)
            g_out_ref[...] = full_a[3]

    for layer in range(2):
        @pl.when(section == layer)
        def _():
            for kind in range(4):
                for step in range(1, 4):
                    x_piece(kind, layer, step).wait_send()

        for source in range(2):
            for kind in range(4):
                core_piece(kind, layer, source).wait_send()

            @pl.when(jnp.logical_not(is_own(layer, source)))
            def _():
                for kind in (HEAD, REST, MLP):
                    if by_quarters(kind, layer):
                        for step in range(1, DP):
                            dp_piece(kind, layer, source, step).wait_send()
                for kind in range(2):
                    x_copy(kind, layer, source).wait_send()
                xv_copy(layer, source).wait_send()
    for step in range(1, DP):
        for kind in range(2):
            full_copy(kind, step).wait_send()


def run_layers(*operands):
    vmem = pl.BlockSpec(memory_space=pltpu.VMEM)
    anywhere = pl.BlockSpec(memory_space=pl.ANY)
    dma = pltpu.SemaphoreType.DMA
    every = QUAD * TOKENS
    scratch = [
        pltpu.VMEM((2, QUAD, 16, D), F32),
        pltpu.VMEM((2, QUAD, 256, D), BF16),
        pltpu.VMEM((2, QUAD, 512, D), BF16),
        pltpu.VMEM((2, GATHERS, HALVES, LANE, HALF, D), BF16),
        pltpu.VMEM((2, HALVES, LANE, HALF, D), BF16),
        pltpu.VMEM((2, HALVES, LANE, HALF, D), BF16),
        pltpu.VMEM((2, ROWS, D), F32),
        pltpu.VMEM((2, 2, ROWS, D), F32),
        pltpu.VMEM((2, 2, ROWS, 128), F32),
        pltpu.VMEM((2, 2, ROWS, D), F32),
        pltpu.VMEM((ROWS, D), F32),
        pltpu.VMEM((ROWS, D), F32),
        pltpu.VMEM((QUAD, HALVES, 192, 128), BF16),
        pltpu.VMEM((QUAD, HALVES, 192, 128), BF16),
        pltpu.VMEM((2, every, 64), BF16),
        pltpu.VMEM((2, every, 64), BF16),
        pltpu.VMEM((2, every, 64), BF16),
        pltpu.VMEM((QUAD, 128, 128), BF16),
        pltpu.VMEM((QUAD, 128, 128), BF16),
        pltpu.VMEM((2, TOKENS, 256), BF16),
        pltpu.VMEM((2, every, every), BF16),
        pltpu.VMEM((2, TOKENS, 1024), BF16),
        pltpu.VMEM((2, TOKENS, 1024), BF16),
        pltpu.VMEM((TOKENS, 1024), BF16),
        pltpu.VMEM((TOKENS, 1024), BF16),
        pltpu.VMEM((QUAD, 128, 128), BF16),
        pltpu.VMEM((every, 64), F32),
        pltpu.VMEM((every, 64), F32),
        pltpu.VMEM((2, 2, 512, D), BF16),
        pltpu.VMEM((2, 2, 256, D), BF16),
        pltpu.VMEM((2, 512, D), BF16),
        pltpu.VMEM((2, 256, D), BF16),
        pltpu.VMEM((2, DP - 1, 2, 128, D), BF16),
        pltpu.VMEM((2, DP - 1, 2, 64, D), BF16),
        pltpu.VMEM((2, 2, 128, D), BF16),
        pltpu.VMEM((2, 2, 64, D), BF16),
        pltpu.VMEM((4, 128, D), BF16),
        pltpu.VMEM((4, 64, D), BF16),
        pltpu.VMEM((DP, 128, D), BF16),
        pltpu.VMEM((DP, 64, D), BF16),
        pltpu.VMEM((2, 16, D), F32),
        pltpu.VMEM((LANE, 2, 8, D), F32),
        pltpu.VMEM((2, 16, D), F32),
        pltpu.VMEM((4, 16, D), F32),
        pltpu.VMEM((DP, 16, D), F32),
        pltpu.VMEM((2, 2, ROWS, D), BF16),
        pltpu.VMEM((2, ROWS, D), BF16),
        dma((4,)), dma((4, 4)), dma((4, 4)),
        dma((4, 4, DP)), dma((4, 4, DP)), dma((4, 4)), dma((4, 4)),
        dma((GATHERS, 2 * LANE)), dma((GATHERS, 2 * LANE)),
        dma((2 * LANE,)), dma((GATHERS, 2 * LANE)),
        dma((5, QUAD)), dma((5, QUAD)),
        dma((2,)), dma((2,)),
        dma((2, DP)), dma((2, 2, DP)),
        dma((2, 4)), dma((2, 4)),
        dma((2, DP)), dma((2, DP)),
        dma((2,)), dma((2,)),
        dma((LANE,)), dma((LANE,)),
        dma((1,)), dma((1,)),
        dma((4,)), dma((4,)),
        dma((DP,)), dma((DP,)),
    ]
    return pl.pallas_call(
        kernel,
        out_shape=(
            jax.ShapeDtypeStruct((2, ROWS, D), BF16),
            jax.ShapeDtypeStruct((2, ROWS, D), BF16),
            jax.ShapeDtypeStruct((192, D), BF16),
            jax.ShapeDtypeStruct((64, D), BF16),
            jax.ShapeDtypeStruct((D, 256), BF16),
            jax.ShapeDtypeStruct((256, D), BF16),
            jax.ShapeDtypeStruct((2, 64), F32),
            jax.ShapeDtypeStruct((1, 256), F32),
            jax.ShapeDtypeStruct((8, D), F32),
        ),
        in_specs=[vmem, vmem, pl.BlockSpec(memory_space=pltpu.SMEM)] + [anywhere] * 4 + [vmem] * 3,
        out_specs=(vmem,) * 9,
        scratch_shapes=scratch,
        name="two_layers",
        compiler_params=pltpu.CompilerParams(
            collective_id=0, has_side_effects=True, vmem_limit_bytes=63 * 2**20
        ),
    )(*operands)


def body(
    images, out_grad, live_images, attn_in, qv_bias, attn_out, mlp_in, mlp_bias, mlp_out, vectors
):
    section_out, section_in_grad, g_in, g_out, g_up, g_down, g_qv, g_bias, g_vec = run_layers(
        images, out_grad, live_images, attn_in[0].transpose(1, 2, 0).reshape(192, D),
        attn_out[0], mlp_in[0], mlp_out[0], qv_bias[0], mlp_bias, vectors[0])
    return (
        section_out[None],
        section_in_grad[None],
        g_in.astype(F32).reshape(3, 64, D).transpose(2, 0, 1)[None],
        g_qv[None],
        g_out.astype(F32)[None],
        g_up.astype(F32)[None],
        g_bias,
        g_down.astype(F32)[None],
        g_vec[None],
    )


def solution(mesh):
    placed = (
        P("dp", "tensor", None),
        P("dp", "tensor", None),
        P(),
        P("section", None, None, "tensor"),
        P("section", None, "tensor"),
        P("section", "tensor", None),
        P("section", None, "tensor"),
        P("section", "tensor"),
        P("section", "tensor", None),
        P("section", None, None),
    )
    return jax.shard_map(
        body,
        mesh=mesh,
        in_specs=placed,
        out_specs=(
            P("section", "dp", "tensor", None),
            P("section", "dp", "tensor", None),
            P("section", None, None, "tensor"),
            P("section", None, "tensor"),
            P("section", "tensor", None),
            P("section", None, "tensor"),
            P("section", "tensor"),
            P("section", "tensor", None),
            P("section", None, None),
        ),
        check_vma=False,
    )
```

```python
import jax
import jax.numpy as jnp
from jax import lax
from jax.experimental import pallas as pl
from jax.experimental.pallas import tpu as pltpu
from jax.sharding import PartitionSpec as P

MESH = pl.DeviceIdType.MESH
F32 = jnp.float32
BF16 = jnp.bfloat16
EPSILON = 1e-06
D = 1024
MICRO = 2
LANE = 4
QUAD = 4
ROWS = 64
HALVES = 2
HALF = ROWS // HALVES
TOKENS = LANE * ROWS
DP = 4
BIAS_ROW = 8
XORS = (1, 3, 2, 0)
OWN = 3
GATHERS = 4
SMALL, HEAD, REST, MLP = range(4)


def dot_nn(a, b):
    return lax.dot_general(a, b, (((1,), (0,)), ((), ())), preferred_element_type=F32)


def dot_nt(a, b):
    return lax.dot_general(a, b, (((1,), (1,)), ((), ())), preferred_element_type=F32)


def dot_tn(a, b):
    return lax.dot_general(a, b, (((0,), (0,)), ((), ())), preferred_element_type=F32)


def normalize(rows):
    center = rows - jnp.mean(rows, axis=-1, keepdims=True)
    inv = lax.rsqrt(jnp.mean(center * center, axis=-1, keepdims=True) + EPSILON)
    return center * inv, inv


def normalize_back(grad, unit, inv, gain):
    scaled = grad * gain
    return inv * (
        scaled
        - jnp.mean(scaled, axis=-1, keepdims=True)
        - unit * jnp.mean(scaled * unit, axis=-1, keepdims=True)
    )


def sum_rows(rows):
    return jnp.sum(rows, axis=0, keepdims=True)


def kernel(
    images, out_grad, live, qkv_in, out_in, up_in, down_in, qv_bias, up_bias_in, vectors_in,
    so_ref, ig_ref, g_in_ref, g_out_ref, g_up_ref, g_down_ref, g_qv_ref, g_bias_ref, g_vec_ref,
    small_w, attn_w, mlp_w,
    gathered, parts, landed,
    xs, units, invs, branches, hidden, cot,
    qkv_out, qkv_got, queries, keys, values, att_out, att_got, attended, probs,
    act, slope, d_pre, d_mixed, d_att_got, d_keys, d_values,
    grad_m, grad_a, core_m, core_a, dp_m, dp_a, part_m, part_a, recv_m, recv_a, full_m, full_a,
    vec, lane_vec, core_vec, x_vec, dp_vec, outs, outs_in,
    w_local, w_x_send, w_x_recv, w_dp_send, w_dp_recv, w_core_send, w_core_recv,
    ag_send, ag_recv, rs_send, rs_recv, quad_send, quad_recv,
    core_send, core_recv, dp_send, dp_recv, x_send, x_recv, full_send, full_recv,
    out_send, out_recv, lane_send, lane_recv, cv_send, cv_recv, xv_send, xv_recv,
    yv_send, yv_recv,
):
    section = lax.axis_index("section")
    group = lax.axis_index("dp")
    tensor = lax.axis_index("tensor")
    core = lax.rem(tensor, 2)
    lane = lax.rem(tensor // 2, LANE)
    high = tensor // (2 * LANE)
    other = 1 - core
    quad = high * 2 + core
    along_x = section * 2 + high

    def place(high_at, lane_at, core_at):
        return (high_at * LANE + lane_at) * 2 + core_at

    def to_lane(index):
        return {"tensor": place(high, index, core)}

    def to_quad(index):
        return {"tensor": place(index // 2, lane, lax.rem(index, 2))}

    def to_x(section_at, high_at):
        return {"section": section_at, "tensor": place(high_at, lane, core)}

    def to_dp(index):
        return {"dp": index}

    to_core = {"tensor": place(high, lane, other)}

    def next_of(own, step, count):
        return lax.rem(own + step, count)

    def remote(src, dst, send_sem, recv_sem, device):
        return pltpu.make_async_remote_copy(
            src_ref=src, dst_ref=dst, send_sem=send_sem, recv_sem=recv_sem,
            device_id=device, device_id_type=MESH,
        )

    def arrival(block, recv_sem):
        return remote(block, block, cv_send.at[0], recv_sem, to_core)

    own_attn = attn_w.at[section, quad]
    own_mlp = mlp_w.at[section, quad]
    landing = probs.at[1, :, pl.ds(0, 256)]
    loads = [
        pltpu.make_async_copy(origin, there, w_local.at[at]) for at, (origin, there) in enumerate((
            (qkv_in, own_attn.at[pl.ds(0, 192)]),
            (out_in, own_attn.at[pl.ds(192, 64)]),
            (up_in, landing),
            (down_in, own_mlp.at[pl.ds(256, 256)]),
        ))
    ]
    for load in loads:
        load.start()
    small_w[section, quad, 0:8] = vectors_in[...]
    gap = jnp.zeros((1, 64), F32)
    small_w[section, quad, 8:9] = jnp.concatenate(
        [qv_bias[0:1], gap, qv_bias[1:2], gap, up_bias_in[...], jnp.zeros((1, 512), F32)], axis=1)

    barrier = pltpu.get_barrier_semaphore()
    friends = [to_lane(next_of(lane, step, LANE)) for step in range(1, LANE)]
    friends += [to_quad(next_of(quad, step, QUAD)) for step in range(1, QUAD)]
    friends += [to_x(1 - section, high), to_x(1 - section, 1 - high)]
    friends += [to_dp(next_of(group, step, DP)) for step in range(1, DP)]
    for friend in friends:
        pl.semaphore_signal(barrier, inc=1, device_id=friend, device_id_type=MESH)
    pl.semaphore_wait(barrier, len(friends))

    def is_own(layer, source):
        return jnp.logical_and(layer == section, source == high)

    def piece(kind, layer, member):
        if kind == SMALL:
            return small_w.at[layer, member]
        if kind == MLP:
            return mlp_w.at[layer, member]
        return attn_w.at[layer, member, pl.ds((kind - HEAD) * 128, 128)]

    def by_quarters(kind, layer):
        return kind != SMALL

    def quarter(kind, layer, member, index):
        if kind == MLP:
            return mlp_w.at[layer, member, pl.ds(pl.multiple_of(index * 128, 128), 128)]
        first = pl.multiple_of((kind - HEAD) * 128 + index * 32, 32)
        return attn_w.at[layer, member, pl.ds(first, 32)]

    def x_block(kind, layer, member):
        if by_quarters(kind, layer):
            return quarter(kind, layer, member, group)
        return piece(kind, layer, member)

    def x_piece(kind, layer, step):
        peer = next_of(along_x, step, 4)
        block = x_block(kind, layer, quad)
        return remote(block, block, w_x_send.at[kind, step], w_x_recv.at[kind, along_x],
                      to_x(peer // 2, lax.rem(peer, 2)))

    def dp_piece(kind, layer, source, step):
        block = quarter(kind, layer, source * 2 + core, group)
        return remote(block, block, w_dp_send.at[kind, layer * 2 + source, step],
                      w_dp_recv.at[kind, layer * 2 + source, group],
                      to_dp(next_of(group, step, DP)))

    def core_piece(kind, layer, source):
        block = piece(kind, layer, source * 2 + core)
        return remote(block, block, w_core_send.at[kind, layer * 2 + source],
                      w_core_recv.at[kind, layer * 2 + source], to_core)

    def send_pieces(kind, layer):
        @pl.when(section == layer)
        def _():
            for step in range(1, 4):
                x_piece(kind, layer, step).start()

    def spread_pieces(kind, layer):
        for source in range(2):
            @pl.when(jnp.logical_not(is_own(layer, source)))
            def _():
                arrival(x_block(kind, layer, source * 2 + core),
                        w_x_recv.at[kind, layer * 2 + source]).wait_recv()
                for step in range(1, DP):
                    dp_piece(kind, layer, source, step).start()

    def relay_pieces(kind, layer):
        for source in range(2):
            @pl.when(jnp.logical_not(is_own(layer, source)))
            def _():
                if by_quarters(kind, layer):
                    for step in range(1, DP):
                        sender = next_of(group, step, DP)
                        arrival(quarter(kind, layer, source * 2 + core, sender),
                                w_dp_recv.at[kind, layer * 2 + source, sender]).wait_recv()
                else:
                    arrival(x_block(kind, layer, source * 2 + core),
                            w_x_recv.at[kind, layer * 2 + source]).wait_recv()

            core_piece(kind, layer, source).start()

    def take_pieces(kind, layer):
        for source in range(2):
            arrival(piece(kind, layer, source * 2 + other),
                    w_core_recv.at[kind, layer * 2 + source]).wait_recv()

    def lane_of(slot):
        return jnp.bitwise_xor(lane, XORS[slot])

    def gather_copy(layer, which, half, slot):
        at = half * LANE + slot
        return remote(gathered.at[layer, which, half, OWN], gathered.at[layer, which, half, slot],
                      ag_send.at[which, at], ag_recv.at[which, at], to_lane(lane_of(slot)))

    def gather_start(layer, which, half, rows):
        gathered[layer, which, half, OWN] = rows
        for slot in range(OWN):
            gather_copy(layer, which, half, slot).start()

    def gather_finish(layer, which):
        for half in range(HALVES):
            for slot in range(OWN):
                gather_copy(layer, which, half, slot).wait_send()

    def gather_take(layer, which, half):
        for slot in range(OWN):
            arrival(gathered.at[layer, which, half, slot],
                    ag_recv.at[which, half * LANE + slot]).wait_recv()
        return gathered[layer, which, half].reshape(LANE * HALF, D)

    def whole(layer, which):
        return gathered[layer, which].reshape(TOKENS, D)

    def part_copy(which, half, slot):
        at = half * LANE + slot
        return remote(parts.at[which % 2, half, slot], landed.at[which % 2, half, slot],
                      rs_send.at[at], rs_recv.at[which, at], to_lane(lane_of(slot)))

    def part_start(which, half, rows):
        parts[which % 2, half] = rows.astype(BF16).reshape(LANE, HALF, D)
        for slot in range(OWN):
            part_copy(which, half, slot).start()

    def part_sum(which, half):
        total = parts[which % 2, half, OWN].astype(F32)
        for slot in range(OWN):
            arrival(landed.at[which % 2, half, slot],
                    rs_recv.at[which, half * LANE + slot]).wait_recv()
            total = total + landed[which % 2, half, slot].astype(F32)
        for slot in range(OWN):
            part_copy(which, half, slot).wait_send()
        return total

    def own_rows(half):
        return slice(half * HALF, (half + 1) * HALF)

    def each_half(work):
        for half in range(HALVES):
            work(half)

    def half_rows(half):
        return slice(half * LANE * HALF, (half + 1) * LANE * HALF)

    d_att_out, d_mix_out, d_mix_got = att_out, qkv_out, qkv_got
    exchanges = ((qkv_out, qkv_got), (att_out, att_got), (d_att_out, d_att_got),
                 (d_mix_out, d_mix_got))

    def quad_copy(which, dest):
        origin, there = exchanges[which]
        return remote(origin.at[dest], there.at[quad], quad_send.at[which, dest],
                      quad_recv.at[which, quad], to_quad(dest))

    def pack_rows(member, half, query_key, value):
        qkv_out[member, half, 0:128] = query_key
        qkv_out[member, half, 128:192] = jnp.concatenate([value[0:64], value[64:128]], axis=-1)

    def unpack_values(source, half):
        block = qkv_got[source, half, 128:192]
        return jnp.concatenate([block[:, 0:64], block[:, 64:128]], axis=0)

    def unpack_halves(block):
        return jnp.concatenate([block[:, 0:64], block[:, 64:128]], axis=0)

    def half_copy(half, dest):
        return remote(qkv_out.at[dest, half], qkv_got.at[quad, half],
                      quad_send.at[4 * half, dest], quad_recv.at[4 * half, quad], to_quad(dest))

    def quad_start(which):
        origin, there = exchanges[which]
        for step in (2, 3, 1):
            quad_copy(which, jnp.bitwise_xor(quad, step)).start()
        there[quad] = origin[quad]

    def quad_take(which):
        there = exchanges[which][1]
        for step in (1, 2, 3):
            source = jnp.bitwise_xor(quad, step)
            arrival(there.at[source], quad_recv.at[which, source]).wait_recv()

    def quad_finish(which):
        for step in (1, 2, 3):
            quad_copy(which, jnp.bitwise_xor(quad, step)).wait_send()

    def token_rows(source, half=0, length=TOKENS):
        return pl.ds(pl.multiple_of(source * TOKENS + half * length, length), length)

    def vector(layer, row):
        return small_w[layer, quad, row:row + 1]

    def all_biases(layer, first):
        row = slice(BIAS_ROW, BIAS_ROW + 1)
        return jnp.concatenate(
            [small_w[layer, member, row, first:first + 256] for member in range(QUAD)], axis=-1)

    def keep_inv(layer, which, half, inv):
        invs[layer, which, own_rows(half)] = jnp.broadcast_to(inv, (HALF, 128))

    def get_inv(layer, which, half):
        return invs[layer, which, own_rows(half), 0:1]

    def norm_start(layer, which, half, rows):
        unit, inv = normalize(rows)
        units[layer, which, own_rows(half)] = unit
        keep_inv(layer, which, half, inv)
        gain, offset = vector(layer, which * 4), vector(layer, which * 4 + 1)
        gather_start(layer, which, half, (unit * gain + offset).astype(BF16))

    def attn_weights(layer):
        return attn_w[layer].reshape(QUAD * 256, D)

    def out_weights(layer):
        return attn_w[layer, :, 192:256].reshape(QUAD * 64, D)

    def up_weights(layer):
        return mlp_w[layer, :, 0:256].reshape(QUAD * 256, D)

    def down_weights(layer):
        return mlp_w[layer, :, 256:512].reshape(QUAD * 256, D)

    for layer in range(2):
        send_pieces(SMALL, layer)
    loads[0].wait()
    loads[1].wait()
    send_pieces(HEAD, 0)
    send_pieces(REST, 0)
    loads[2].wait()
    for part in range(4):
        mlp_w[section, quad, 0:256, part * 256:part * 256 + 256] = (
            probs[1, part * 256:part * 256 + 256, 0:256].astype(F32).T.astype(BF16))
    loads[3].wait()
    send_pieces(MLP, 0)
    xs[0] = images[section].astype(F32)
    vec[...] = jnp.zeros_like(vec)
    for layer in range(2):
        relay_pieces(SMALL, layer)

    for half in range(HALVES):
        norm_start(0, 0, half, xs[0, own_rows(half)])

    @pl.loop(0, 2)
    def _(layer):
        @pl.when(layer == 0)
        def _():
            spread_pieces(HEAD, 0)
            spread_pieces(REST, 0)
            relay_pieces(REST, 0)
            relay_pieces(HEAD, 0)
            for either in range(2):
                take_pieces(SMALL, either)

        take_pieces(REST, layer)
        take_pieces(HEAD, layer)
        qkv_bias = all_biases(layer, 0)

        def project(pair):
            rows = gather_take(layer, 0, pair)
            mixed = (dot_nt(rows, attn_weights(layer)) + qkv_bias).astype(BF16)
            for member in range(QUAD):
                first = member * 256
                pack_rows(member, pair, mixed[:, first:first + 128],
                          mixed[:, first + 128:first + 192])
            for step in (2, 3, 1):
                half_copy(pair, jnp.bitwise_xor(quad, step)).start()

        each_half(project)
        qkv_got[quad] = qkv_out[quad]

        @pl.when(layer == 0)
        def _():
            for kind in (HEAD, REST, MLP):
                send_pieces(kind, 1)
            spread_pieces(MLP, 0)

        @pl.when(layer == 1)
        def _():
            relay_pieces(MLP, 1)

        for half in range(HALVES):
            for step in (1, 2, 3):
                source = jnp.bitwise_xor(quad, step)
                arrival(qkv_got.at[source, half],
                        quad_recv.at[4 * half, source]).wait_recv()
        for source in range(QUAD):
            for half in range(HALVES):
                rows = token_rows(source, half, 128)
                block = qkv_got[source, half, 0:128]
                queries[layer, rows] = (block[:, 0:64].astype(F32) * 0.125).astype(BF16)
                keys[layer, rows] = block[:, 64:128]
                values[layer, rows] = unpack_values(source, half)

        @pl.loop(0, QUAD)
        def _(step):
            source = jnp.bitwise_xor(quad, 2 + step - step // 2 * (2 * step - 1))
            found = []
            for half in range(2):
                rows = token_rows(source, half, 128)
                scores = dot_nt(queries[layer, rows], keys[layer])
                grown = jnp.exp(scores - jnp.max(scores, axis=-1, keepdims=True))
                share = (grown / jnp.sum(grown, axis=-1, keepdims=True)).astype(BF16)
                probs[layer, rows] = share
                found.append(dot_nn(share, values[layer]).astype(BF16))
            att_out[source] = jnp.concatenate(found, axis=-1)

            @pl.when(source != quad)
            def _():
                quad_copy(1, source).start()

        att_got[quad] = att_out[quad]
        quad_take(1)
        attended[layer] = jnp.concatenate(
            [unpack_halves(att_got[member]) for member in range(QUAD)], axis=-1)

        def project_out(pair):
            part_start(0, pair, dot_nn(attended[layer, half_rows(pair)], out_weights(layer)))

        each_half(project_out)
        for half in range(HALVES):
            for step in (1, 2, 3):
                half_copy(half, jnp.bitwise_xor(quad, step)).wait_send()
        quad_finish(1)
        gather_finish(layer, 0)
        for half in range(HALVES):
            branch = part_sum(0, half) + vector(layer, 2)
            branches[layer, 0, own_rows(half)] = branch
            state = xs[layer, own_rows(half)] + vector(layer, 3) * branch
            hidden[own_rows(half)] = state
            norm_start(layer, 1, half, state)

        @pl.when(layer == 0)
        def _():
            relay_pieces(MLP, 0)
            for kind in (HEAD, REST, MLP):
                spread_pieces(kind, 1)

        take_pieces(MLP, layer)
        up_bias = all_biases(layer, 256)

        def feed(pair):
            rows = gather_take(layer, 1, pair)
            pre = dot_nt(rows, up_weights(layer)) + up_bias
            cdf = 0.5 + 0.5 * lax.erf(pre * 0.7071067811865476)
            bell = jnp.exp(-0.5 * pre * pre) * 0.3989422804014327
            value = (pre * cdf).astype(BF16)
            act[layer, half_rows(pair)] = value
            slope[layer, half_rows(pair)] = (cdf + pre * bell).astype(BF16)
            part_start(1, pair, dot_nn(value, down_weights(layer)))

        each_half(feed)

        @pl.when(layer == 0)
        def _():
            relay_pieces(HEAD, 1)
            relay_pieces(REST, 1)

        gather_finish(layer, 1)
        for half in range(HALVES):
            branch = part_sum(1, half) + vector(layer, 6)
            branches[layer, 1, own_rows(half)] = branch
            rounded = (hidden[own_rows(half)] + vector(layer, 7) * branch).astype(BF16)
            outs[0, layer, own_rows(half)] = rounded

            @pl.when(layer == 0)
            def _():
                xs[1, own_rows(half)] = rounded.astype(F32)
                norm_start(1, 0, half, rounded.astype(F32))

    def out_copy(which):
        return remote(outs.at[which, 1 - section], outs_in.at[which],
                      out_send.at[which], out_recv.at[which], to_x(1 - section, high))

    out_copy(0).start()

    grads = (grad_m, grad_a)
    from_core = (core_m, core_a)
    from_dp = (dp_m, dp_a)
    quarters = (part_m, part_a)
    from_x = (recv_m, recv_a)
    fulls = (full_m, full_a)
    lengths = (128, 64)

    def core_copy(kind):
        return remote(grads[kind].at[:, other], from_core[kind],
                      core_send.at[kind], core_recv.at[kind], to_core)

    def dp_rows(kind, index):
        length = lengths[kind]
        return pl.ds(pl.multiple_of(index * length, length), length)

    def dp_copy(kind, layer, step):
        dest = next_of(group, step, DP)
        return remote(grads[kind].at[:, core, dp_rows(kind, dest)],
                      from_dp[kind].at[layer, step - 1],
                      dp_send.at[kind, step], dp_recv.at[kind, layer, step], to_dp(dest))

    def x_copy(kind, layer, source):
        return remote(quarters[kind].at[layer, source], from_x[kind].at[along_x],
                      x_send.at[kind, layer * 2 + source], x_recv.at[kind, along_x],
                      to_x(layer, source))

    def core_done(kind, layer):
        core_copy(kind).wait()
        for source in range(2):
            grads[kind][source, core] = (
                grads[kind][source, core].astype(F32) + from_core[kind][source].astype(F32)
            ).astype(BF16)
        for step in range(1, DP):
            dp_copy(kind, layer, step).start()

    def dp_done(kind, layer):
        total = grads[kind][:, core, dp_rows(kind, group)].astype(F32)
        for step in range(1, DP):
            arrival(from_dp[kind].at[layer, step - 1],
                    dp_recv.at[kind, layer, step]).wait_recv()
            total = total + from_dp[kind][layer, step - 1].astype(F32)
        quarters[kind][layer] = total.astype(BF16)
        for source in range(2):
            @pl.when(jnp.logical_not(is_own(layer, source)))
            def _():
                x_copy(kind, layer, source).start()
        for step in range(1, DP):
            dp_copy(kind, layer, step).wait_send()

    def full_copy(kind, step):
        ref = fulls[kind]
        return remote(ref.at[group], ref.at[group], full_send.at[kind, step],
                      full_recv.at[kind, group], to_dp(next_of(group, step, DP)))

    def x_done(kind):
        total = quarters[kind][section, high].astype(F32)
        for step in range(1, 4):
            source = next_of(along_x, step, 4)
            arrival(from_x[kind].at[source], x_recv.at[kind, source]).wait_recv()
            total = total + from_x[kind][source].astype(F32)
        fulls[kind][group] = total.astype(BF16)
        for step in range(1, DP):
            full_copy(kind, step).start()

    mine = live[group * MICRO + section]
    everyone = live[section]
    for step in range(1, DP):
        everyone = everyone + live[step * MICRO + section]
    weight = jnp.where(mine > 0, 1.0 / jnp.full((1, D), everyone, jnp.int32).astype(F32), 0.0)
    cot[...] = out_grad[section].astype(F32) * weight

    def back_start(layer, half):
        above = cot[own_rows(half)]
        d_branch2 = (above * vector(layer, 7)).astype(BF16)
        gather_start(layer, 2, half, d_branch2)
        vec[layer, 7:8] += sum_rows(above * branches[layer, 1, own_rows(half)])
        vec[layer, 6:7] += sum_rows(d_branch2.astype(F32))

    for half in range(HALVES):
        back_start(1, half)

    @pl.loop(0, 2)
    def _(turn):
        layer = 1 - turn

        def feed_back(pair):
            rows = gather_take(layer, 2, pair)
            d_act = dot_nt(rows, down_weights(layer))
            back = (d_act * slope[layer, half_rows(pair)].astype(F32)).astype(BF16)
            d_pre[half_rows(pair)] = back
            vec[layer, 8:9] += sum_rows(back.astype(F32))
            part_start(2, pair, dot_nn(back, up_weights(layer)))

        each_half(feed_back)
        gather_finish(layer, 2)
        for member in range(QUAD):
            units_of = slice(member * 256, member * 256 + 256)
            at = (member // 2, member % 2)
            grad_m[at[0], at[1], 0:256] = dot_tn(d_pre[:, units_of], whole(layer, 1)).astype(BF16)
            grad_m[at[0], at[1], 256:512] = dot_tn(
                act[layer, :, units_of], whole(layer, 2)).astype(BF16)
        core_copy(0).start()
        for half in range(HALVES):
            rows = own_rows(half)
            d_normed = part_sum(2, half)
            unit, inv = units[layer, 1, rows], get_inv(layer, 1, half)
            d_hidden = cot[rows] + normalize_back(d_normed, unit, inv, vector(layer, 4))
            hidden[rows] = d_hidden
            d_branch = (d_hidden * vector(layer, 3)).astype(BF16)
            gather_start(layer, 3, half, d_branch)
            vec[layer, 4:5] += sum_rows(d_normed * unit)
            vec[layer, 5:6] += sum_rows(d_normed)
            vec[layer, 3:4] += sum_rows(d_hidden * branches[layer, 0, rows])
            vec[layer, 2:3] += sum_rows(d_branch.astype(F32))

        core_done(0, layer)
        d_outs = []

        def out_back(pair):
            rows = gather_take(layer, 3, pair)
            d_outs.append(dot_nt(rows, out_weights(layer)).astype(BF16))

        each_half(out_back)
        for member in range(QUAD):
            d_att_out[member] = jnp.concatenate(
                [half[:, member * 64:member * 64 + 64] for half in d_outs], axis=-1)
        quad_start(2)
        gather_finish(layer, 3)

        @pl.when(turn == 1)
        def _():
            dp_done(1, 1)

        out_grads = dot_tn(attended[layer], whole(layer, 3)).astype(BF16)
        d_keys[...] = jnp.zeros_like(d_keys)
        d_values[...] = jnp.zeros_like(d_values)
        quad_take(2)

        @pl.loop(0, QUAD)
        def _(source):
            d_rows = unpack_halves(d_att_got[source])
            score_grads = []
            for half in range(2):
                rows = token_rows(source, half, 128)
                d_share = dot_nt(d_rows[half * 128:half * 128 + 128], values[layer])
                wide = probs[layer, rows].astype(F32)
                product = wide * d_share
                d_score = (product - wide * jnp.sum(product, axis=-1, keepdims=True)).astype(BF16)
                score_grads.append(d_score)
                d_mix_out[source, half, 0:128, 0:64] = (
                    dot_nn(d_score, keys[layer]) * 0.125).astype(BF16)
            d_keys[...] += dot_tn(jnp.concatenate(score_grads, 0),
                                  queries[layer, token_rows(source)])
            d_values[...] += dot_tn(probs[layer, token_rows(source)], d_rows)

        for source in range(QUAD):
            for half in range(HALVES):
                rows = token_rows(source, half, 128)
                d_mix_out[source, half, 0:128, 64:128] = d_keys[rows].astype(BF16)
                value = d_values[rows].astype(BF16)
                d_mix_out[source, half, 128:192] = jnp.concatenate(
                    [value[0:64], value[64:128]], axis=-1)
        quad_start(3)
        for member in range(QUAD):
            grad_a[member // 2, member % 2, 192:256] = out_grads[member * 64:member * 64 + 64]
        quad_take(3)

        none = jnp.zeros((2 * ROWS, 64), BF16)

        def project_back(pair):
            for member in range(QUAD):
                first = member * 256
                d_mixed[half_rows(pair), first:first + 128] = d_mix_got[member, pair, 0:128]
                d_mixed[half_rows(pair), first + 128:first + 256] = jnp.concatenate(
                    [unpack_values(member, pair), none], axis=-1)
            rows = d_mixed[half_rows(pair)]
            vec[layer, 9:10] += sum_rows(rows.astype(F32))
            part_start(3, pair, dot_nn(rows, attn_weights(layer)))

        each_half(project_back)
        for member in range(QUAD):
            grad_a[member // 2, member % 2, 0:192] = dot_tn(
                d_mixed[:, member * 256:member * 256 + 256], whole(layer, 0))[0:192].astype(BF16)
        core_copy(1).start()
        quad_finish(2)
        quad_finish(3)

        @pl.when(turn == 1)
        def _():
            core_done(1, 0)

        for half in range(HALVES):
            rows = own_rows(half)
            d_normed = part_sum(3, half)
            unit, inv = units[layer, 0, rows], get_inv(layer, 0, half)
            rounded = (hidden[rows] + normalize_back(
                d_normed, unit, inv, vector(layer, 0))).astype(BF16)
            outs[1, layer, rows] = rounded
            cot[rows] = rounded.astype(F32)

            @pl.when(turn == 0)
            def _():
                back_start(0, half)

            vec[layer, 0:1] += sum_rows(d_normed * unit)
            vec[layer, 1:2] += sum_rows(d_normed)

        @pl.when(turn == 0)
        def _():
            core_done(1, 1)

        dp_done(0, layer)

    out_copy(1).start()
    x_done(0)

    def lane_copy(dest):
        return remote(vec.at[:, pl.ds(0, 8)], lane_vec.at[lane],
                      lane_send.at[dest], lane_recv.at[lane], to_lane(dest))

    for step in range(1, LANE):
        lane_copy(next_of(lane, step, LANE)).start()
    for step in range(1, LANE):
        source = next_of(lane, step, LANE)
        arrival(lane_vec.at[source], lane_recv.at[source]).wait_recv()
    for step in range(1, LANE):
        lane_copy(next_of(lane, step, LANE)).wait_send()
    for step in range(1, LANE):
        vec[:, 0:8] += lane_vec[next_of(lane, step, LANE)]
    cv_copy = remote(vec, core_vec, cv_send.at[0], cv_recv.at[0], to_core)
    cv_copy.start()
    cv_copy.wait()
    vec[...] += core_vec[...]

    def xv_copy(layer, source):
        return remote(vec.at[layer], x_vec.at[along_x], xv_send.at[layer * 2 + source],
                      xv_recv.at[along_x], to_x(layer, source))

    for layer in range(2):
        for source in range(2):
            @pl.when(jnp.logical_not(is_own(layer, source)))
            def _():
                xv_copy(layer, source).start()

    dp_done(1, 0)

    total = vec[section]
    for step in range(1, 4):
        source = next_of(along_x, step, 4)
        arrival(x_vec.at[source], xv_recv.at[source]).wait_recv()
        total = total + x_vec[source]
    dp_vec[group] = total

    def yv_copy(step):
        return remote(dp_vec.at[group], dp_vec.at[group], yv_send.at[step],
                      yv_recv.at[group], to_dp(next_of(group, step, DP)))

    for step in range(1, DP):
        yv_copy(step).start()
    x_done(1)

    for which, ref in ((0, so_ref), (1, ig_ref)):
        out_copy(which).wait()
        ref[section] = outs[which, section]
        ref[1 - section] = outs_in[which]

    for step in range(1, DP):
        source = next_of(group, step, DP)
        arrival(dp_vec.at[source], yv_recv.at[source]).wait_recv()
        total = total + dp_vec[source]
    for step in range(1, DP):
        yv_copy(step).wait_send()
    g_vec_ref[...] = total[0:8]
    dp_vec[group] = total
    bias_of = dp_vec[group, :, pl.ds(pl.multiple_of(quad * 256, 256), 256)]
    g_bias_ref[...] = bias_of[8:9]
    g_qv_ref[...] = jnp.concatenate([bias_of[9:10, 0:64], bias_of[9:10, 128:192]], axis=0)

    for kind in range(2):
        for step in range(1, DP):
            source = next_of(group, step, DP)
            arrival(fulls[kind].at[source], full_recv.at[kind, source]).wait_recv()
        if kind == 0:
            for part in range(4):
                g_up_ref[part * 256:part * 256 + 256] = full_m[
                    0:2, :, part * 256:part * 256 + 256].reshape(256, 256).astype(F32).T.astype(BF16)
            g_down_ref[...] = full_m[2:4].reshape(256, D)
        else:
            g_in_ref[...] = full_a[0:3].reshape(192, D)
            g_out_ref[...] = full_a[3]

    for layer in range(2):
        @pl.when(section == layer)
        def _():
            for kind in range(4):
                for step in range(1, 4):
                    x_piece(kind, layer, step).wait_send()

        for source in range(2):
            for kind in range(4):
                core_piece(kind, layer, source).wait_send()

            @pl.when(jnp.logical_not(is_own(layer, source)))
            def _():
                for kind in (HEAD, REST, MLP):
                    if by_quarters(kind, layer):
                        for step in range(1, DP):
                            dp_piece(kind, layer, source, step).wait_send()
                for kind in range(2):
                    x_copy(kind, layer, source).wait_send()
                xv_copy(layer, source).wait_send()
    for step in range(1, DP):
        for kind in range(2):
            full_copy(kind, step).wait_send()


def run_layers(*operands):
    vmem = pl.BlockSpec(memory_space=pltpu.VMEM)
    anywhere = pl.BlockSpec(memory_space=pl.ANY)
    dma = pltpu.SemaphoreType.DMA
    every = QUAD * TOKENS
    scratch = [
        pltpu.VMEM((2, QUAD, 16, D), F32),
        pltpu.VMEM((2, QUAD, 256, D), BF16),
        pltpu.VMEM((2, QUAD, 512, D), BF16),
        pltpu.VMEM((2, GATHERS, HALVES, LANE, HALF, D), BF16),
        pltpu.VMEM((2, HALVES, LANE, HALF, D), BF16),
        pltpu.VMEM((2, HALVES, LANE, HALF, D), BF16),
        pltpu.VMEM((2, ROWS, D), F32),
        pltpu.VMEM((2, 2, ROWS, D), F32),
        pltpu.VMEM((2, 2, ROWS, 128), F32),
        pltpu.VMEM((2, 2, ROWS, D), F32),
        pltpu.VMEM((ROWS, D), F32),
        pltpu.VMEM((ROWS, D), F32),
        pltpu.VMEM((QUAD, HALVES, 192, 128), BF16),
        pltpu.VMEM((QUAD, HALVES, 192, 128), BF16),
        pltpu.VMEM((2, every, 64), BF16),
        pltpu.VMEM((2, every, 64), BF16),
        pltpu.VMEM((2, every, 64), BF16),
        pltpu.VMEM((QUAD, 128, 128), BF16),
        pltpu.VMEM((QUAD, 128, 128), BF16),
        pltpu.VMEM((2, TOKENS, 256), BF16),
        pltpu.VMEM((2, every, every), BF16),
        pltpu.VMEM((2, TOKENS, 1024), BF16),
        pltpu.VMEM((2, TOKENS, 1024), BF16),
        pltpu.VMEM((TOKENS, 1024), BF16),
        pltpu.VMEM((TOKENS, 1024), BF16),
        pltpu.VMEM((QUAD, 128, 128), BF16),
        pltpu.VMEM((every, 64), F32),
        pltpu.VMEM((every, 64), F32),
        pltpu.VMEM((2, 2, 512, D), BF16),
        pltpu.VMEM((2, 2, 256, D), BF16),
        pltpu.VMEM((2, 512, D), BF16),
        pltpu.VMEM((2, 256, D), BF16),
        pltpu.VMEM((2, DP - 1, 2, 128, D), BF16),
        pltpu.VMEM((2, DP - 1, 2, 64, D), BF16),
        pltpu.VMEM((2, 2, 128, D), BF16),
        pltpu.VMEM((2, 2, 64, D), BF16),
        pltpu.VMEM((4, 128, D), BF16),
        pltpu.VMEM((4, 64, D), BF16),
        pltpu.VMEM((DP, 128, D), BF16),
        pltpu.VMEM((DP, 64, D), BF16),
        pltpu.VMEM((2, 16, D), F32),
        pltpu.VMEM((LANE, 2, 8, D), F32),
        pltpu.VMEM((2, 16, D), F32),
        pltpu.VMEM((4, 16, D), F32),
        pltpu.VMEM((DP, 16, D), F32),
        pltpu.VMEM((2, 2, ROWS, D), BF16),
        pltpu.VMEM((2, ROWS, D), BF16),
        dma((4,)), dma((4, 4)), dma((4, 4)),
        dma((4, 4, DP)), dma((4, 4, DP)), dma((4, 4)), dma((4, 4)),
        dma((GATHERS, 2 * LANE)), dma((GATHERS, 2 * LANE)),
        dma((2 * LANE,)), dma((GATHERS, 2 * LANE)),
        dma((5, QUAD)), dma((5, QUAD)),
        dma((2,)), dma((2,)),
        dma((2, DP)), dma((2, 2, DP)),
        dma((2, 4)), dma((2, 4)),
        dma((2, DP)), dma((2, DP)),
        dma((2,)), dma((2,)),
        dma((LANE,)), dma((LANE,)),
        dma((1,)), dma((1,)),
        dma((4,)), dma((4,)),
        dma((DP,)), dma((DP,)),
    ]
    return pl.pallas_call(
        kernel,
        out_shape=(
            jax.ShapeDtypeStruct((2, ROWS, D), BF16),
            jax.ShapeDtypeStruct((2, ROWS, D), BF16),
            jax.ShapeDtypeStruct((192, D), BF16),
            jax.ShapeDtypeStruct((64, D), BF16),
            jax.ShapeDtypeStruct((D, 256), BF16),
            jax.ShapeDtypeStruct((256, D), BF16),
            jax.ShapeDtypeStruct((2, 64), F32),
            jax.ShapeDtypeStruct((1, 256), F32),
            jax.ShapeDtypeStruct((8, D), F32),
        ),
        in_specs=[vmem, vmem, pl.BlockSpec(memory_space=pltpu.SMEM)] + [anywhere] * 4 + [vmem] * 3,
        out_specs=(vmem,) * 9,
        scratch_shapes=scratch,
        name="two_layers",
        compiler_params=pltpu.CompilerParams(
            collective_id=0, has_side_effects=True, vmem_limit_bytes=63 * 2**20
        ),
    )(*operands)


def body(
    images, out_grad, live_images, attn_in, qv_bias, attn_out, mlp_in, mlp_bias, mlp_out, vectors
):
    section_out, section_in_grad, g_in, g_out, g_up, g_down, g_qv, g_bias, g_vec = run_layers(
        images, out_grad, live_images, attn_in[0].transpose(1, 2, 0).reshape(192, D),
        attn_out[0], mlp_in[0], mlp_out[0], qv_bias[0], mlp_bias, vectors[0])
    return (
        section_out[None],
        section_in_grad[None],
        g_in.astype(F32).reshape(3, 64, D).transpose(2, 0, 1)[None],
        g_qv[None],
        g_out.astype(F32)[None],
        g_up.astype(F32)[None],
        g_bias,
        g_down.astype(F32)[None],
        g_vec[None],
    )


def solution(mesh):
    placed = (
        P("dp", "tensor", None),
        P("dp", "tensor", None),
        P(),
        P("section", None, None, "tensor"),
        P("section", None, "tensor"),
        P("section", "tensor", None),
        P("section", None, "tensor"),
        P("section", "tensor"),
        P("section", "tensor", None),
        P("section", None, None),
    )
    return jax.shard_map(
        body,
        mesh=mesh,
        in_specs=placed,
        out_specs=(
            P("section", "dp", "tensor", None),
            P("section", "dp", "tensor", None),
            P("section", None, None, "tensor"),
            P("section", None, "tensor"),
            P("section", "tensor", None),
            P("section", None, "tensor"),
            P("section", "tensor"),
            P("section", "tensor", None),
            P("section", None, None),
        ),
        check_vma=False,
    )
```
